32 devices in a mesh: grp: 2 (over y), row: 8 (over z, x), key: 2 (over core).
Axes of the slice: x: 2, y: 2, z: 4, core: 2. Of those that a mesh axis runs over, the one named last changes fastest.
Arguments:
- query: bfloat16 [32, 768, 128], P(('grp', 'row'), 'key'), parts along dimension 0, may hold values from -8 to 8
- keys: bfloat16 [32, 768, 128], P(('grp', 'row'), 'key'), parts along dimension 0, may hold values from -8 to 8
- values: bfloat16 [32, 768, 128], P(('grp', 'row'), 'key'), parts along dimension 0, may hold values from -6 to 6
- gate_logits: bfloat16 [32, 768, 128], P(('grp', 'row'), 'key'), parts along dimension 0, may hold values from -8 to 8
- pair_bias: bfloat16 [4, 1536, 768], P(None, ('grp', 'row'), 'key'), parts along dimension 1, may hold values from -6 to 6
- key_mask: int32 [1536], P(('grp', 'key')), parts along dimension 0, may hold values 0 or 1
- grad_out: bfloat16 [32, 768, 128], P(('grp', 'row'), 'key'), parts along dimension 0, may hold values from -6 to 6
Outputs:
- grad_query: bfloat16 [32, 768, 128], P(('grp', 'row'), 'key'), parts along dimension 0
- grad_keys: bfloat16 [32, 768, 128], P(('grp', 'row'), 'key'), parts along dimension 0
- grad_values: bfloat16 [32, 768, 128], P(('grp', 'row'), 'key'), parts along dimension 0
- grad_gate: bfloat16 [32, 768, 128], P(('grp', 'row'), 'key'), parts along dimension 0
- grad_bias: float32 [4, 1536, 768], P(None, ('grp', 'row'), 'key'), parts along dimension 1
The draws below stay inside these ranges and needn't reach their ends.
There are 2 independent parts, one for each index of `grp`. The reference program is written for one: setup_inputs(seed, part) draws one part's arguments, and reference() takes and returns one part's arrays. A program takes and returns all parts, laid end to end along the dimension named above; each array names one. Nothing has to cross between parts.
All inputs are finite; a program needn't handle non-finite values. No bound on the sum of `key_mask` on one device may be relied on, other than what follows from the above.
Results may differ from the reference program's by a relative error of at most 0.024.
Values may be sent and summed in bfloat16 or wider, within the bound.
No kernel may reach another device: no remote copies, remote signals or barrier semaphores. Data moves between devices by JAX's collectives and lax.ppermute only.
A program may use at most 64 MiB of HBM per device.

```python
import math
import jax
import jax.numpy as jnp
from jax import lax

HEADS = 4
HEAD_DIM = 32
C = 128
N = 768
ROWS = 16


def pair_draw(key):
    key_query, key_keys = jax.random.split(jax.random.fold_in(key, 17), 2)
    query = jnp.clip(jax.random.normal(key_query, (ROWS, N, C), jnp.float32), -6.0, 6.0)
    keyset = jnp.clip(jax.random.normal(key_keys, (ROWS, N, C), jnp.float32), -6.0, 6.0)
    return (query, keyset)


def draw_query(key, part):
    return pair_draw(key)[0].astype(jnp.bfloat16)


def draw_keys(key, part):
    return pair_draw(key)[1].astype(jnp.bfloat16)


def with_ends(values, key, least, high):
    longest = values.shape.index(max(values.shape))
    spots = []
    for shift in (0, 1):
        where = [jax.random.randint(jax.random.fold_in(key, axis), (), 0, length) for axis, length in enumerate(values.shape)]
        where[longest] = (where[longest] + shift) % values.shape[longest]
        spots.append(tuple(where))
    return values.at[spots[0]].set(least).at[spots[1]].set(high)


def steps_of(key, dims, cuts, low, top_value):
    factor_of, own = 1.0, jax.random.fold_in(key, 6)
    for axis_at, shards_of in cuts:
        heights = jnp.exp(jax.random.uniform(jax.random.fold_in(own, axis_at), (shards_of,), jnp.float32, low / len(cuts), top_value / len(cuts)))
        factor_of = factor_of * jnp.repeat(heights, dims[axis_at] // shards_of).reshape([-1 if axis == axis_at else 1 for axis in range(len(dims))])
    return factor_of


def gaussian(own_key, dims, deviation, bound, shards=(), dtype=jnp.bfloat16):
    drawn = deviation * jax.random.normal(own_key, dims, jnp.float32)
    if shards:
        drawn = drawn * steps_of(own_key, dims, shards, -0.22, 0.18)
    return jnp.clip(drawn, -bound, bound).astype(dtype)


def setup_inputs(seed: int = 0, part: int = 0) -> dict:
    seeds = jax.random.split(jax.random.key(seed), 8)
    own_keys = jax.random.split(jax.random.fold_in(seeds[7], part), 8)
    return {
        "query": draw_query(jax.random.fold_in(jax.random.fold_in(seeds[7], part), 71), part),
        "keys": draw_keys(jax.random.fold_in(jax.random.fold_in(seeds[7], part), 71), part),
        "values": gaussian(own_keys[2], (ROWS, N, C), 1.0, 6.0, ((0, 8), (1, 2))),
        "gate_logits": gaussian(own_keys[3], (ROWS, N, C), 2.0, 8.0, ((0, 8), (1, 2))),
        "pair_bias": gaussian(own_keys[4], (HEADS, N, N), 1.0, 6.0, ((1, 8), (2, 2))),
        "key_mask": with_ends((jax.random.randint(own_keys[5], (N,), 0, 4) < 3).astype(jnp.int32), jax.random.fold_in(own_keys[5], 1), 0, 1),
        "grad_out": gaussian(own_keys[6], (ROWS, N, C), 1.0, 6.0, ((0, 8), (1, 2))),
    }


def reference(query, keys, values, gate_logits, pair_bias, key_mask, grad_out):
    scaling = 1.0 / math.sqrt(HEAD_DIM)
    bias_full = pair_bias.astype(jnp.float32) + 1000000000.0 * (key_mask.astype(jnp.float32) - 1.0)[None, None, :]

    def one_row(grad_acc, inputs):
        query_row, key_row, value_row, gate_row, cot_row = inputs
        query_heads = query_row.astype(jnp.float32).reshape(N, HEADS, HEAD_DIM)
        key_heads = key_row.astype(jnp.float32).reshape(N, HEADS, HEAD_DIM)
        value_heads = value_row.astype(jnp.float32).reshape(N, HEADS, HEAD_DIM)
        logits = jnp.einsum('jhd,khd->hjk', query_heads, key_heads) * scaling + bias_full
        row_max = lax.optimization_barrier(jnp.max(logits, axis=-1, keepdims=True))
        expo = jnp.exp(logits - row_max)
        softmax_out = expo / lax.optimization_barrier(jnp.sum(expo, axis=-1, keepdims=True))
        softmax_low = softmax_out.astype(jnp.bfloat16)
        attended = jnp.einsum('hjk,khd->jhd', softmax_low.astype(jnp.float32), value_heads).reshape(N, C)
        gate_sig = jax.nn.sigmoid(gate_row.astype(jnp.float32))
        cot_float = cot_row.astype(jnp.float32)
        d_attended = (cot_float * gate_sig).astype(jnp.bfloat16)
        gate_delta = (cot_float * attended * gate_sig * (1.0 - gate_sig)).astype(jnp.bfloat16)
        upstream = d_attended.astype(jnp.float32).reshape(N, HEADS, HEAD_DIM)
        value_delta = jnp.einsum('hjk,jhd->khd', softmax_low.astype(jnp.float32), upstream).reshape(N, C).astype(jnp.bfloat16)
        d_probs = jnp.einsum('jhd,khd->hjk', upstream, value_heads)
        inner = lax.optimization_barrier(jnp.sum(upstream * attended.reshape(N, HEADS, HEAD_DIM), axis=-1)).T
        d_logits = softmax_out * (d_probs - inner[:, :, None])
        d_low = d_logits.astype(jnp.bfloat16).astype(jnp.float32)
        query_delta = (jnp.einsum('hjk,khd->jhd', d_low, key_heads) * scaling).reshape(N, C).astype(jnp.bfloat16)
        key_delta = (jnp.einsum('hjk,jhd->khd', d_low, query_heads) * scaling).reshape(N, C).astype(jnp.bfloat16)
        return (grad_acc + d_logits, (query_delta, key_delta, value_delta, gate_delta))
    empty_grad = jnp.zeros((HEADS, N, N), jnp.float32)
    grad_bias, results = lax.scan(one_row, empty_grad, (query, keys, values, gate_logits, grad_out))
    return (results[0], results[1], results[2], results[3], grad_bias)
```

```python
import functools
import math

import jax
import jax.numpy as jnp
from jax import lax
from jax.experimental import pallas as pl
from jax.experimental.pallas import tpu as pltpu
from jax.sharding import PartitionSpec as P

PAIR = 2
VMEM = pltpu.VMEM
PARAMS = pltpu.CompilerParams(vmem_limit_bytes=40 * 1024 * 1024)


def group_index():
    return lax.rem(lax.axis_index("row"), PAIR) * lax.axis_size("key") + lax.axis_index("key")


def pre_kernel(query, keys, values, gate, cot, bias, mask, *outs):
    packs, slabs, held = outs[:4], outs[4:8], outs[8]
    rows, heads = query.shape[0], bias.shape[0]
    size = query.shape[2] // heads
    me = group_index()
    upstream = [
        (cot[r].astype(jnp.float32) * jax.nn.sigmoid(gate[r].astype(jnp.float32))).astype(jnp.bfloat16)
        for r in range(rows)
    ]
    whole = [[ref[r] for r in range(rows)] for ref in (query, keys, values)] + [upstream]
    for head in range(heads):
        cut = slice(head * size, (head + 1) * size)
        held[me ^ head] = jnp.concatenate([part[:, cut] for array in whole for part in array], axis=1)
    for step in range(heads):
        packs[step][...] = held[step]
        one = bias[me ^ step].astype(jnp.float32)
        slabs[step][...] = jnp.where(mask[...] == 1, one, -1000000000.0).astype(jnp.bfloat16)


def pre(query, keys, values, gate, cot, bias, mask):
    rows, count, channels = query.shape
    heads, own, key_count = bias.shape
    width = 4 * rows * channels // heads
    pack = jax.ShapeDtypeStruct((count, width), jnp.bfloat16)
    slab = jax.ShapeDtypeStruct((own, key_count), jnp.bfloat16)
    return pl.pallas_call(
        pre_kernel,
        out_shape=[pack] * 4 + [slab] * 4,
        scratch_shapes=[VMEM((heads, count, width), jnp.bfloat16)],
        compiler_params=PARAMS,
        name="pack",
    )(query, keys, values, gate, cot, bias, mask.reshape(1, key_count))


NT = (((1,), (1,)), ((), ()))


def dot(a, b, dims=(((1,), (0,)), ((), ()))):
    return lax.dot_general(a, b, dims, preferred_element_type=jnp.float32)


def main_kernel(scaling, size, *refs):
    slabs, bias = refs[:4], refs[4]
    outs, d_bias = refs[5:9], refs[9]
    held, q_all, d_all, k_of, v_of, dk_t, dv_t, att_all, dq_all = refs[10:]
    step = pl.program_id(0)
    half, width = slabs[0].shape
    lanes = q_all.shape[1]
    wide = lanes // 2
    parts = lanes // size
    tile = bias.shape[0]
    me = group_index()

    @pl.when(step == 0)
    def _():
        for s in range(4):
            held[me ^ s] = slabs[s][...]
        lane = lax.broadcasted_iota(jnp.int32, (half, lanes), 1) // size
        for c in range(2):
            rows = slice(c * half, (c + 1) * half)
            pair = [
                jnp.concatenate([held[c][:, j * wide : (j + 1) * wide], held[2 + c][:, j * wide : (j + 1) * wide]], axis=1)
                for j in range(4)
            ]
            q_all[rows], d_all[rows] = pair[0], pair[3]
            for r in range(parts):
                k_of[r, rows] = jnp.where(lane == r, pair[1], 0)
                v_of[r, rows] = jnp.where(lane == r, pair[2], 0)
        dk_t[...] = jnp.zeros_like(dk_t)
        dv_t[...] = jnp.zeros_like(dv_t)

    here = pl.ds(step * tile, tile)
    q, d = q_all[here], d_all[here]
    q_t = q.astype(jnp.float32).T.astype(jnp.bfloat16)
    d_t = d.astype(jnp.float32).T.astype(jnp.bfloat16)
    d_wide = d.astype(jnp.float32)
    bias_wide = bias[...].astype(jnp.float32)
    att_sum, dq_sum, bias_sum = None, None, None
    for r in range(parts):
        k, v = k_of[r], v_of[r]
        logits = dot(q, k, NT) * scaling + bias_wide
        expo = jnp.exp(logits - jnp.max(logits, axis=-1, keepdims=True))
        probs = expo * (1.0 / jnp.sum(expo, axis=-1, keepdims=True))
        low = probs.astype(jnp.bfloat16)
        att = dot(low, v)
        inner = jnp.sum(d_wide * att, axis=-1, keepdims=True)
        d_logits = probs * (dot(d, v, NT) - inner)
        d_low = d_logits.astype(jnp.bfloat16)
        dq = dot(d_low, k)
        cut = slice(r * size, (r + 1) * size)
        dk_t[cut] += dot(q_t[cut], d_low)
        dv_t[cut] += dot(d_t[cut], low)
        att_sum = att if r == 0 else att_sum + att
        dq_sum = dq if r == 0 else dq_sum + dq
        bias_sum = d_logits if r == 0 else bias_sum + d_logits
    att_all[here] = att_sum.astype(jnp.bfloat16)
    dq_all[here] = (dq_sum * scaling).astype(jnp.bfloat16)
    d_bias[...] = bias_sum.astype(jnp.bfloat16)

    @pl.when(step == pl.num_programs(0) - 1)
    def _():
        dk = (dk_t[...] * scaling).T.astype(jnp.bfloat16)
        dv = dv_t[...].T.astype(jnp.bfloat16)
        for c in range(2):
            rows = slice(c * half, (c + 1) * half)
            whole = [att_all[rows], dq_all[rows], dk[rows], dv[rows]]
            for x in range(2):
                held[2 * x + c] = jnp.concatenate([one[:, x * wide : (x + 1) * wide] for one in whole], axis=1)
        for s in range(4):
            outs[s][...] = held[me ^ s]


def main(slabs, bias, scaling, size, tile):
    half, width = slabs[0].shape
    queries, key_count = bias.shape
    lanes = width // 2
    fixed = pl.BlockSpec((half, width), lambda i: (0, 0))
    strip = pl.BlockSpec((tile, key_count), lambda i: (i, 0))
    elements = queries * key_count * (lanes // size)
    return pl.pallas_call(
        functools.partial(main_kernel, scaling, size),
        grid=(queries // tile,),
        in_specs=[fixed] * 4 + [strip],
        out_specs=[fixed] * 4 + [strip],
        out_shape=[jax.ShapeDtypeStruct((half, width), jnp.bfloat16)] * 4
        + [jax.ShapeDtypeStruct((queries, key_count), jnp.bfloat16)],
        scratch_shapes=[
            VMEM((4, half, width), jnp.bfloat16),
            VMEM((queries, lanes), jnp.bfloat16),
            VMEM((queries, lanes), jnp.bfloat16),
            VMEM((lanes // size, key_count, lanes), jnp.bfloat16),
            VMEM((lanes // size, key_count, lanes), jnp.bfloat16),
            VMEM((lanes, key_count), jnp.float32),
            VMEM((lanes, key_count), jnp.float32),
            VMEM((queries, lanes), jnp.bfloat16),
            VMEM((queries, lanes), jnp.bfloat16),
        ],
        compiler_params=PARAMS,
        cost_estimate=pl.CostEstimate(
            flops=12 * elements * size, bytes_accessed=8 * queries * key_count, transcendentals=elements
        ),
        name="attention",
    )(*slabs, bias)


def post_kernel(gate, cot, *refs):
    slabs, (d_query, d_keys, d_values, d_gate), held = refs[:4], refs[4:8], refs[8]
    rows, half, channels = gate.shape
    size = channels // 4
    me = group_index()
    for s in range(4):
        held[me ^ s] = slabs[s][...]
    for r in range(rows):
        full = []
        for j in range(4):
            at = (j * rows + r) * size
            full.append(jnp.concatenate([held[h][:, at : at + size] for h in range(4)], axis=1))
        d_query[r], d_keys[r], d_values[r] = full[1], full[2], full[3]
        sig = jax.nn.sigmoid(gate[r].astype(jnp.float32))
        d_gate[r] = (cot[r].astype(jnp.float32) * full[0].astype(jnp.float32) * sig * (1.0 - sig)).astype(jnp.bfloat16)


def post(gate, cot, slabs):
    one = jax.ShapeDtypeStruct(gate.shape, jnp.bfloat16)
    return pl.pallas_call(
        post_kernel,
        out_shape=[one] * 4,
        scratch_shapes=[VMEM((4,) + slabs[0].shape, jnp.bfloat16)],
        compiler_params=PARAMS,
        name="unpack",
    )(gate, cot, *slabs)


def bias_kernel(*refs):
    me = group_index()
    for s in range(4):
        refs[4][me ^ s] = refs[s][...].astype(jnp.float32)


def bias_out(slabs):
    return pl.pallas_call(
        bias_kernel,
        out_shape=jax.ShapeDtypeStruct((4,) + slabs[0].shape, jnp.float32),
        compiler_params=PARAMS,
        name="bias_grad",
    )(*slabs)


def shards(query, keys, values, gate_logits, pair_bias, key_mask, grad_out):
    rows, half, channels = query.shape
    heads, own, _ = pair_bias.shape
    size = channels // heads
    scaling = 1.0 / math.sqrt(size)
    n_row, n_key = lax.axis_size("row"), lax.axis_size("key")
    assert PAIR * n_key == heads == 4
    count = n_row // PAIR
    place = lax.axis_index("row") // PAIR
    me = group_index()
    column, core = me // n_key, lax.rem(me, n_key)

    def swap(value, step):
        if step == 0:
            return value
        return lax.ppermute(value, ("row", "key"), [(i, i ^ step) for i in range(n_row * n_key)])

    def right(value, senders):
        pairs = [((z * PAIR + x), ((z + 1) * PAIR + x)) for z in senders for x in range(PAIR)]
        return lax.ppermute(value, "row", pairs)

    def left(value, senders):
        pairs = [((z * PAIR + x), ((z - 1) * PAIR + x)) for z in senders for x in range(PAIR)]
        return lax.ppermute(value, "row", pairs)

    out = pre(query, keys, values, gate_logits, grad_out, pair_bias, key_mask)
    packs, slabs = out[:4], out[4:]
    slabs = [swap(slabs[s], s) for s in range(4)]
    packs = [swap(packs[s], s) for s in range(4)]

    by_core = [
        [jnp.where(core == 0, slabs[2 * x], slabs[2 * x + 1]), jnp.where(core == 0, slabs[2 * x + 1], slabs[2 * x])]
        for x in range(2)
    ]
    by_core = [jnp.concatenate(pair, axis=1) for pair in by_core]
    block = jnp.concatenate(
        [jnp.where(column == 0, by_core[0], by_core[1]), jnp.where(column == 0, by_core[1], by_core[0])], axis=0
    )
    from_left, from_right = [], []
    going_right = going_left = block
    for t in range(1, count):
        going_right = right(going_right, range(t - 1, count - 1))
        going_left = left(going_left, range(1, count - t + 1))
        from_left.append(going_right)
        from_right.append(going_left)
    strip = block.shape[0]
    line = jnp.concatenate(from_left[::-1] + [block] + from_right, axis=0)
    bias = lax.dynamic_slice_in_dim(line, (count - 1 - place) * strip, count * strip, axis=0)

    *outs, d_bias = main(packs, bias, scaling, size, 128)
    outs = [swap(outs[s], s) for s in range(4)]
    grads = post(gate_logits, grad_out, outs)

    d_blocks = d_bias.reshape(count, strip, -1)

    def term(index):
        return lax.dynamic_index_in_dim(d_blocks, jnp.clip(index, 0, count - 1), 0, keepdims=False).astype(jnp.float32)

    to_right = to_left = None
    for t in range(1, count):
        first, second = term(place + count - t), term(place - count + t)
        if t > 1:
            first, second = first + to_right.astype(jnp.float32), second + to_left.astype(jnp.float32)
        to_right = right(first.astype(jnp.bfloat16), range(0, t))
        to_left = left(second.astype(jnp.bfloat16), range(count - t, count))
    mine = (term(place) + to_right.astype(jnp.float32) + to_left.astype(jnp.float32)).astype(jnp.bfloat16)
    mine = mine.reshape(PAIR, own, n_key, half)
    pieces = [
        lax.dynamic_slice(mine, (lax.rem(me ^ s, 4) // n_key, 0, lax.rem(me ^ s, n_key), 0), (1, own, 1, half)).reshape(own, half)
        for s in range(4)
    ]
    grad_bias = bias_out([swap(pieces[s], s) for s in range(4)])
    return (grads[0], grads[1], grads[2], grads[3], grad_bias)


def solution(mesh):
    tokens = P(("grp", "row"), "key", None)
    pair = P(None, ("grp", "row"), "key")
    in_specs = (tokens, tokens, tokens, tokens, pair, P(("grp", "key")), tokens)
    out_specs = (tokens, tokens, tokens, tokens, pair)
    return jax.shard_map(shards, mesh=mesh, in_specs=in_specs, out_specs=out_specs, check_vma=False)
```

```python
import functools
import math

import jax
import jax.numpy as jnp
from jax import lax
from jax.experimental import pallas as pl
from jax.experimental.pallas import tpu as pltpu
from jax.sharding import PartitionSpec as P

PAIR = 2
VMEM = pltpu.VMEM
PARAMS = pltpu.CompilerParams(vmem_limit_bytes=40 * 1024 * 1024)
PRE_PARAMS = pltpu.CompilerParams(vmem_limit_bytes=60 * 1024 * 1024)


def pre_kernel(query, keys, values, gate, cot, bias, mask, pack, spread, *held):
    buffers, sems = held[:7], held[7]
    copies = [
        pltpu.make_async_copy(ref, buffer, sems.at[i])
        for i, (ref, buffer) in enumerate(zip((bias, mask, cot, gate, query, keys, values), buffers))
    ]
    for copy in copies:
        copy.start()
    bias, mask, cot, gate, query, keys, values = buffers
    rows, heads = query.shape[0], bias.shape[0]
    size = query.shape[2] // heads
    copies[0].wait()
    copies[1].wait()
    keep = mask[...].reshape(1, mask.shape[0]) == 1
    for head in range(heads):
        slab = jnp.where(keep, bias[head].astype(jnp.float32), -1000000000.0).astype(jnp.bfloat16)
        for z in range(spread.shape[0]):
            spread[z, head] = slab
    for copy in copies[2:]:
        copy.wait()
    upstream = [
        (cot[r].astype(jnp.float32) * jax.nn.sigmoid(gate[r].astype(jnp.float32))).astype(jnp.bfloat16)
        for r in range(rows)
    ]
    whole = [[ref[r] for r in range(rows)] for ref in (query, keys, values)] + [upstream]
    for head in range(heads):
        cut = slice(head * size, (head + 1) * size)
        pack[head] = jnp.concatenate([part[:, cut] for array in whole for part in array], axis=1)


def pre(query, keys, values, gate, cot, bias, mask, places):
    rows, count, channels = query.shape
    heads = bias.shape[0]
    width = 4 * rows * channels // heads
    token = VMEM(query.shape, jnp.bfloat16)
    return pl.pallas_call(
        pre_kernel,
        in_specs=[pl.BlockSpec(memory_space=pl.ANY)] * 7,
        out_shape=[
            jax.ShapeDtypeStruct((heads, count, width), jnp.bfloat16),
            jax.ShapeDtypeStruct((places,) + bias.shape, jnp.bfloat16),
        ],
        scratch_shapes=[VMEM(bias.shape, jnp.bfloat16), VMEM(mask.shape, jnp.int32)]
        + [token] * 5
        + [pltpu.SemaphoreType.DMA((7,))],
        compiler_params=PRE_PARAMS,
        name="pack",
    )(query, keys, values, gate, cot, bias, mask)


NT = (((1,), (1,)), ((), ()))


def dot(a, b, dims=(((1,), (0,)), ((), ()))):
    return lax.dot_general(a, b, dims, preferred_element_type=jnp.float32)


def main_kernel(scaling, size, slabs, bias, outs, d_bias, q_all, d_all, k_of, v_of, dk_t, dv_t, att_all, dq_all, bias_wide):
    step = pl.program_id(0)
    _, half, width = slabs.shape
    lanes = q_all.shape[1]
    wide = lanes // 2
    parts = lanes // size
    blocks, cores, own, _ = bias.shape
    tile = blocks * own

    @pl.when(step == 0)
    def _():
        lane = lax.broadcasted_iota(jnp.int32, (half, lanes), 1) // size
        for c in range(2):
            rows = slice(c * half, (c + 1) * half)
            pair = [
                jnp.concatenate([slabs[c, :, j * wide : (j + 1) * wide], slabs[2 + c, :, j * wide : (j + 1) * wide]], axis=1)
                for j in range(4)
            ]
            q_all[rows], d_all[rows] = pair[0], pair[3]
            for r in range(parts):
                k_of[r, rows] = jnp.where(lane == r, pair[1], 0)
                v_of[r, rows] = jnp.where(lane == r, pair[2], 0)
        dk_t[...] = jnp.zeros_like(dk_t)
        dv_t[...] = jnp.zeros_like(dv_t)

    for i in range(blocks):
        for c in range(cores):
            bias_wide[i * own : (i + 1) * own, c * half : (c + 1) * half] = bias[i, c].astype(jnp.float32)
    here = pl.ds(step * tile, tile)
    q, d = q_all[here], d_all[here]
    q_t = q.astype(jnp.float32).T.astype(jnp.bfloat16)
    d_t = d.astype(jnp.float32).T.astype(jnp.bfloat16)
    d_wide = d.astype(jnp.float32)
    att_sum, dq_sum, bias_sum = None, None, None
    for r in range(parts):
        k, v = k_of[r], v_of[r]
        logits = dot(q, k, NT) * scaling + bias_wide[...]
        expo = jnp.exp(logits - jnp.max(logits, axis=-1, keepdims=True))
        probs = expo * (1.0 / jnp.sum(expo, axis=-1, keepdims=True))
        low = probs.astype(jnp.bfloat16)
        att = dot(low, v)
        inner = jnp.sum(d_wide * att, axis=-1, keepdims=True)
        d_logits = probs * (dot(d, v, NT) - inner)
        d_low = d_logits.astype(jnp.bfloat16)
        dq = dot(d_low, k)
        cut = slice(r * size, (r + 1) * size)
        dk_t[cut] += dot(q_t[cut], d_low)
        dv_t[cut] += dot(d_t[cut], low)
        att_sum = att if r == 0 else att_sum + att
        dq_sum = dq if r == 0 else dq_sum + dq
        bias_sum = d_logits if r == 0 else bias_sum + d_logits
    att_all[here] = att_sum.astype(jnp.bfloat16)
    dq_all[here] = (dq_sum * scaling).astype(jnp.bfloat16)
    for i in range(blocks):
        for c in range(cores):
            part = bias_sum[i * own : (i + 1) * own, c * half : (c + 1) * half]
            d_bias[i, c] = part.astype(jnp.bfloat16)

    @pl.when(step == pl.num_programs(0) - 1)
    def _():
        dk = (dk_t[...] * scaling).T.astype(jnp.bfloat16)
        dv = dv_t[...].T.astype(jnp.bfloat16)
        for c in range(2):
            rows = slice(c * half, (c + 1) * half)
            whole = [att_all[rows], dq_all[rows], dk[rows], dv[rows]]
            for x in range(2):
                outs[2 * x + c] = jnp.concatenate([one[:, x * wide : (x + 1) * wide] for one in whole], axis=1)


def main(slabs, bias, scaling, size, blocks):
    _, half, width = slabs.shape
    strips, cores, own, _ = bias.shape
    queries = key_count = cores * half
    lanes = width // 2
    fixed = pl.BlockSpec(slabs.shape, lambda i: (0, 0, 0))
    strip = pl.BlockSpec((blocks, cores, own, half), lambda i: (i, 0, 0, 0))
    elements = queries * key_count * (lanes // size)
    return pl.pallas_call(
        functools.partial(main_kernel, scaling, size),
        grid=(strips // blocks,),
        in_specs=[fixed, strip],
        out_specs=[fixed, strip],
        out_shape=[jax.ShapeDtypeStruct(slabs.shape, jnp.bfloat16), jax.ShapeDtypeStruct(bias.shape, jnp.bfloat16)],
        scratch_shapes=[
            VMEM((queries, lanes), jnp.bfloat16),
            VMEM((queries, lanes), jnp.bfloat16),
            VMEM((lanes // size, key_count, lanes), jnp.bfloat16),
            VMEM((lanes // size, key_count, lanes), jnp.bfloat16),
            VMEM((lanes, key_count), jnp.float32),
            VMEM((lanes, key_count), jnp.float32),
            VMEM((queries, lanes), jnp.bfloat16),
            VMEM((queries, lanes), jnp.bfloat16),
            VMEM((blocks * own, key_count), jnp.float32),
        ],
        compiler_params=PARAMS,
        cost_estimate=pl.CostEstimate(
            flops=12 * elements * size, bytes_accessed=8 * queries * key_count, transcendentals=elements
        ),
        name="attention",
    )(slabs, bias)


def post_kernel(gate, cot, slabs, d_query, d_keys, d_values, d_gate):
    rows, half, channels = gate.shape
    size = channels // 4
    for r in range(rows):
        full = []
        for j in range(4):
            at = (j * rows + r) * size
            full.append(jnp.concatenate([slabs[h, :, at : at + size] for h in range(4)], axis=1))
        d_query[r], d_keys[r], d_values[r] = full[1], full[2], full[3]
        sig = jax.nn.sigmoid(gate[r].astype(jnp.float32))
        d_gate[r] = (cot[r].astype(jnp.float32) * full[0].astype(jnp.float32) * sig * (1.0 - sig)).astype(jnp.bfloat16)


def post(gate, cot, slabs):
    one = jax.ShapeDtypeStruct(gate.shape, jnp.bfloat16)
    return pl.pallas_call(post_kernel, out_shape=[one] * 4, compiler_params=PARAMS, name="unpack")(gate, cot, slabs)


def shards(query, keys, values, gate_logits, pair_bias, key_mask, grad_out):
    rows, half, channels = query.shape
    heads, own, _ = pair_bias.shape
    size = channels // heads
    scaling = 1.0 / math.sqrt(size)
    places, cores = lax.axis_size("z"), lax.axis_size("key")
    assert PAIR * cores == heads == 4
    strips = places * PAIR

    def everywhere(value):
        return lax.all_to_all(value, ("z", "x", "key"), 0, 0, tiled=True)

    def in_group(value):
        return lax.all_to_all(value, ("x", "key"), 0, 0, tiled=True)

    packs, spread = pre(query, keys, values, gate_logits, grad_out, pair_bias, key_mask, places)
    bias = everywhere(spread.reshape(places * heads, own, half)).reshape(strips, cores, own, half)
    packs = in_group(packs)
    blocks = 2
    aligned = own % 16 == 0
    if not aligned:
        bias = bias.transpose(0, 2, 1, 3).reshape(strips // 16, 16 * own, cores, half).transpose(0, 2, 1, 3)
        blocks = 1
    outs, d_bias = main(packs, bias, scaling, size, blocks)
    if not aligned:
        d_bias = d_bias.transpose(0, 2, 1, 3).reshape(strips, own, cores, half).transpose(0, 2, 1, 3)
    d_bias = everywhere(d_bias.reshape(strips * cores, own, half)).reshape(places, heads, own, half)
    grad_bias = jnp.sum(d_bias.astype(jnp.float32), axis=0)
    grads = post(gate_logits, grad_out, in_group(outs))
    return (grads[0], grads[1], grads[2], grads[3], grad_bias)


def solution(mesh):
    groups, rows, cores = mesh.devices.shape
    mesh = jax.sharding.Mesh(mesh.devices.reshape(groups, rows // PAIR, PAIR, cores), ("grp", "z", "x", "key"))
    tokens = P(("grp", "z", "x"), "key", None)
    pair = P(None, ("grp", "z", "x"), "key")
    in_specs = (tokens, tokens, tokens, tokens, pair, P(("grp", "key")), tokens)
    out_specs = (tokens, tokens, tokens, tokens, pair)
    return jax.shard_map(shards, mesh=mesh, in_specs=in_specs, out_specs=out_specs, check_vma=False)
```

```python
import functools
import math

import jax
import jax.numpy as jnp
from jax import lax
from jax.experimental import pallas as pl
from jax.experimental.pallas import tpu as pltpu
from jax.sharding import PartitionSpec as P

PAIR = 2
VMEM = pltpu.VMEM
PARAMS = pltpu.CompilerParams(vmem_limit_bytes=40 * 1024 * 1024)
PRE_PARAMS = pltpu.CompilerParams(vmem_limit_bytes=60 * 1024 * 1024)


def pre_kernel(query, keys, values, gate, cot, bias, mask, pack, spread, *held):
    buffers, sems = held[:7], held[7]
    copies = [
        pltpu.make_async_copy(ref, buffer, sems.at[i])
        for i, (ref, buffer) in enumerate(zip((bias, mask, cot, gate, query, keys, values), buffers))
    ]
    for copy in copies:
        copy.start()
    bias, mask, cot, gate, query, keys, values = buffers
    rows, heads = query.shape[0], bias.shape[0]
    size = query.shape[2] // heads
    copies[0].wait()
    copies[1].wait()
    keep = mask[...].reshape(1, mask.shape[0]) == 1
    chunks, places, _, part, _ = spread.shape
    for head in range(heads):
        slab = jnp.where(keep, bias[head].astype(jnp.float32), -1000000000.0).astype(jnp.bfloat16)
        for t in range(chunks):
            for z in range(places):
                spread[t, z, head] = slab[t * part : (t + 1) * part]
    for copy in copies[2:]:
        copy.wait()
    upstream = [
        (cot[r].astype(jnp.float32) * jax.nn.sigmoid(gate[r].astype(jnp.float32))).astype(jnp.bfloat16)
        for r in range(rows)
    ]
    whole = [[ref[r] for r in range(rows)] for ref in (query, keys, values)] + [upstream]
    for head in range(heads):
        cut = slice(head * size, (head + 1) * size)
        for r in range(rows):
            pack[head * rows + r] = jnp.concatenate([array[r][:, cut] for array in whole], axis=1)


def pre(query, keys, values, gate, cot, bias, mask, places, chunks):
    rows, count, channels = query.shape
    heads, own, half = bias.shape
    token = VMEM(query.shape, jnp.bfloat16)
    return pl.pallas_call(
        pre_kernel,
        in_specs=[pl.BlockSpec(memory_space=pl.ANY)] * 7,
        out_shape=[
            jax.ShapeDtypeStruct((heads * rows, count, 4 * channels // heads), jnp.bfloat16),
            jax.ShapeDtypeStruct((chunks, places, heads, own // chunks, half), jnp.bfloat16),
        ],
        scratch_shapes=[VMEM(bias.shape, jnp.bfloat16), VMEM(mask.shape, jnp.int32)]
        + [token] * 5
        + [pltpu.SemaphoreType.DMA((7,))],
        compiler_params=PRE_PARAMS,
        name="pack",
    )(query, keys, values, gate, cot, bias, mask)


NT = (((1,), (1,)), ((), ()))


def dot(a, b, dims=(((1,), (0,)), ((), ()))):
    return lax.dot_general(a, b, dims, preferred_element_type=jnp.float32)


def main_kernel(scaling, size, chunk, chunks, *refs):
    slabs, mine, other = refs[:3]
    earlier, refs = refs[3 : 3 + (4 if chunk else 0)], refs[3 + (4 if chunk else 0) :]
    last = chunk == chunks - 1
    (d_mine, d_other), refs = refs[:2], refs[2:]
    results, refs = refs[: 1 if last else 4], refs[1 if last else 4 :]
    q_all, d_all, k_of, v_of, dk_t, dv_t, att_all, dq_all, bias_wide, back = refs
    step = pl.program_id(0)
    core = lax.axis_index("key")
    _, half, lanes = slabs.shape
    parts = lanes // size
    blocks, part, _ = mine.shape
    tile = blocks * part
    own = part * chunks
    strips = half // own

    def lanes_of(index, j):
        return jnp.concatenate([slabs[2 * p + index, :, j * size : (j + 1) * size] for p in range(parts)], axis=1)

    @pl.when(step == 0)
    def _():
        lane = lax.broadcasted_iota(jnp.int32, (half, lanes), 1) // size
        for c in range(2):
            q, d = lanes_of(c, 0), lanes_of(c, 3)
            for i in range(strips):
                to = slice((c * strips + i) * part, (c * strips + i + 1) * part)
                at = slice(i * own + chunk * part, i * own + (chunk + 1) * part)
                q_all[to], d_all[to] = q[at], d[at]
            k, v = lanes_of(core ^ c, 1), lanes_of(core ^ c, 2)
            rows = slice(c * half, (c + 1) * half)
            for r in range(parts):
                k_of[r, rows] = jnp.where(lane == r, k, 0)
                v_of[r, rows] = jnp.where(lane == r, v, 0)
        dk_t[...] = earlier[2][...] if chunk else jnp.zeros_like(dk_t)
        dv_t[...] = earlier[3][...] if chunk else jnp.zeros_like(dv_t)

    for i in range(blocks):
        rows = slice(i * part, (i + 1) * part)
        bias_wide[rows, :half] = mine[i].astype(jnp.float32)
        bias_wide[rows, half:] = other[i].astype(jnp.float32)
    here = pl.ds(step * tile, tile)
    q, d = q_all[here], d_all[here]
    q_t = q.astype(jnp.float32).T.astype(jnp.bfloat16)
    d_t = d.astype(jnp.float32).T.astype(jnp.bfloat16)
    d_wide = d.astype(jnp.float32)
    att_sum, dq_sum, bias_sum = None, None, None
    for r in range(parts):
        k, v = k_of[r], v_of[r]
        logits = dot(q, k, NT) * scaling + bias_wide[...]
        expo = jnp.exp(logits - jnp.max(logits, axis=-1, keepdims=True))
        probs = expo * (1.0 / jnp.sum(expo, axis=-1, keepdims=True))
        low = probs.astype(jnp.bfloat16)
        att = dot(low, v)
        inner = jnp.sum(d_wide * att, axis=-1, keepdims=True)
        d_logits = probs * (dot(d, v, NT) - inner)
        d_low = d_logits.astype(jnp.bfloat16)
        dq = dot(d_low, k)
        cut = slice(r * size, (r + 1) * size)
        dk_t[cut] += dot(q_t[cut], d_low)
        dv_t[cut] += dot(d_t[cut], low)
        att_sum = att if r == 0 else att_sum + att
        dq_sum = dq if r == 0 else dq_sum + dq
        bias_sum = d_logits if r == 0 else bias_sum + d_logits
    att_all[here] = att_sum.astype(jnp.bfloat16)
    dq_all[here] = (dq_sum * scaling).astype(jnp.bfloat16)
    for i in range(blocks):
        rows = slice(i * part, (i + 1) * part)
        d_mine[i] = bias_sum[rows, :half].astype(jnp.bfloat16)
        d_other[i] = bias_sum[rows, half:].astype(jnp.bfloat16)

    @pl.when(step == pl.num_programs(0) - 1)
    def _():
        if not last:
            for ref, value in zip(results, (att_all, dq_all, dk_t, dv_t)):
                ref[...] = value[...]
            return
        dk = (dk_t[...] * scaling).T.astype(jnp.bfloat16)
        dv = dv_t[...].T.astype(jnp.bfloat16)
        for c in range(2):
            back[0, c], back[1, c] = dk[c * half : (c + 1) * half], dv[c * half : (c + 1) * half]
        done = [(earlier[0], earlier[1])] if chunk else []
        done.append((att_all, dq_all))
        for c in range(2):
            whole = []
            for j in range(2):
                pieces = [
                    pair[j][(c * strips + i) * part : (c * strips + i + 1) * part] for i in range(strips) for pair in done
                ]
                whole.append(jnp.concatenate(pieces, axis=0))
            whole += [back[0, core ^ c], back[1, core ^ c]]
            for p in range(parts):
                cut = slice(p * size, (p + 1) * size)
                results[0][2 * p + c] = jnp.concatenate([one[:, cut] for one in whole], axis=1)


def main(slabs, mine, other, earlier, scaling, size, blocks, chunk, chunks):
    _, half, lanes = slabs.shape
    strips, part, _ = mine.shape
    queries, key_count = strips * part, 2 * half
    rows = jax.ShapeDtypeStruct((queries, lanes), jnp.bfloat16)
    turned = jax.ShapeDtypeStruct((lanes, key_count), jnp.float32)
    strip = pl.BlockSpec((blocks, part, half), lambda i: (i, 0, 0))

    def fixed(value):
        return pl.BlockSpec(value.shape, lambda i: (0,) * len(value.shape))

    results = [slabs] if chunk == chunks - 1 else [rows, rows, turned, turned]
    elements = queries * key_count * (lanes // size)
    return pl.pallas_call(
        functools.partial(main_kernel, scaling, size, chunk, chunks),
        grid=(strips // blocks,),
        in_specs=[fixed(slabs), strip, strip] + [fixed(one) for one in earlier],
        out_specs=[strip, strip] + [fixed(one) for one in results],
        out_shape=[jax.ShapeDtypeStruct(one.shape, one.dtype) for one in [mine, other] + results],
        scratch_shapes=[
            VMEM(rows.shape, jnp.bfloat16),
            VMEM(rows.shape, jnp.bfloat16),
            VMEM((lanes // size, key_count, lanes), jnp.bfloat16),
            VMEM((lanes // size, key_count, lanes), jnp.bfloat16),
            VMEM(turned.shape, jnp.float32),
            VMEM(turned.shape, jnp.float32),
            VMEM(rows.shape, jnp.bfloat16),
            VMEM(rows.shape, jnp.bfloat16),
            VMEM((blocks * part, key_count), jnp.float32),
            VMEM((2, 2, half, lanes), jnp.bfloat16),
        ],
        compiler_params=PARAMS,
        cost_estimate=pl.CostEstimate(
            flops=12 * elements * size, bytes_accessed=8 * queries * key_count, transcendentals=elements
        ),
        name="attention",
    )(slabs, mine, other, *earlier)


def post_kernel(gate, cot, slabs, d_query, d_keys, d_values, d_gate):
    rows, half, channels = gate.shape
    size = channels // 4
    for r in range(rows):
        full = []
        for j in range(4):
            full.append(jnp.concatenate([slabs[rows * h + r, :, j * size : (j + 1) * size] for h in range(4)], axis=1))
        d_query[r], d_keys[r], d_values[r] = full[1], full[2], full[3]
        sig = jax.nn.sigmoid(gate[r].astype(jnp.float32))
        d_gate[r] = (cot[r].astype(jnp.float32) * full[0].astype(jnp.float32) * sig * (1.0 - sig)).astype(jnp.bfloat16)


def post(gate, cot, slabs):
    one = jax.ShapeDtypeStruct(gate.shape, jnp.bfloat16)
    return pl.pallas_call(post_kernel, out_shape=[one] * 4, compiler_params=PARAMS, name="unpack")(gate, cot, slabs)


def shards(query, keys, values, gate_logits, pair_bias, key_mask, grad_out):
    rows, half, channels = query.shape
    heads, own, _ = pair_bias.shape
    size = channels // heads
    scaling = 1.0 / math.sqrt(size)
    places, cores = lax.axis_size("far"), lax.axis_size("key")
    assert PAIR * PAIR == heads == 4 and rows == cores == 2
    chunks = 2 if own % 32 == 0 else 1
    part = own // chunks

    def everywhere(value):
        return lax.all_to_all(value, ("far", "near", "side"), 0, 0, tiled=True)

    def in_group(value):
        return lax.all_to_all(value, ("near", "side", "key"), 0, 0, tiled=True)

    def other_core(value):
        return lax.ppermute(value, "key", [(0, 1), (1, 0)])

    packs, spread = pre(query, keys, values, gate_logits, grad_out, pair_bias, key_mask, places, chunks)
    packs = in_group(packs)
    arrived = [everywhere(spread[t].reshape(places * heads, part, half)) for t in range(chunks)]
    earlier, to_sum = [], []
    for t in range(chunks):
        mine = arrived[t]
        other = other_core(mine)
        if chunks == 1:
            mine, other = mine.reshape(8, -1, half), other.reshape(8, -1, half)
        d_mine, d_other, *earlier = main(packs, mine, other, earlier, scaling, size, 4, t, chunks)
        d_sum = (d_mine.astype(jnp.float32) + other_core(d_other).astype(jnp.float32)).astype(jnp.bfloat16)
        d_sum = everywhere(d_sum.reshape(places * heads, part, half)).reshape(places, heads, part, half)
        to_sum.append(jnp.sum(d_sum.astype(jnp.float32), axis=0))
    grads = post(gate_logits, grad_out, in_group(earlier[0]))
    return (grads[0], grads[1], grads[2], grads[3], jnp.concatenate(to_sum, axis=1))


def solution(mesh):
    groups, rows, cores = mesh.devices.shape
    devices = mesh.devices.reshape(groups, rows // PAIR**2, PAIR, PAIR, cores)
    mesh = jax.sharding.Mesh(devices, ("grp", "far", "near", "side", "key"))
    split = ("grp", "far", "near", "side")
    tokens = P(split, "key", None)
    pair = P(None, split, "key")
    in_specs = (tokens, tokens, tokens, tokens, pair, P(("grp", "key")), tokens)
    out_specs = (tokens, tokens, tokens, tokens, pair)
    return jax.shard_map(shards, mesh=mesh, in_specs=in_specs, out_specs=out_specs, check_vma=False)
```

```python
import functools
import math

import jax
import jax.numpy as jnp
from jax import lax
from jax.experimental import pallas as pl
from jax.experimental.pallas import tpu as pltpu
from jax.sharding import PartitionSpec as P

PAIR = 2
VMEM = pltpu.VMEM
PARAMS = pltpu.CompilerParams(vmem_limit_bytes=40 * 1024 * 1024)
PRE_PARAMS = pltpu.CompilerParams(vmem_limit_bytes=60 * 1024 * 1024)


def places():
    near = lax.axis_index("near") * PAIR + lax.axis_index("side")
    return lax.axis_index("far") * PAIR * PAIR + near, near, lax.axis_index("key")


def pre_kernel(query, keys, values, gate, cot, bias, mask, *refs):
    packs, slabs, buffers, sems, held = refs[:8], refs[8:12], refs[12:19], refs[19], refs[20]
    copies = [
        pltpu.make_async_copy(ref, buffer, sems.at[i])
        for i, (ref, buffer) in enumerate(zip((bias, mask, cot, gate, query, keys, values), buffers))
    ]
    for copy in copies:
        copy.start()
    bias, mask, cot, gate, query, keys, values = buffers
    rows, heads = query.shape[0], bias.shape[0]
    size = query.shape[2] // heads
    _, near, core = places()
    copies[0].wait()
    copies[1].wait()
    keep = mask[...].reshape(1, mask.shape[0]) == 1
    for s in range(heads):
        one = bias[near ^ s].astype(jnp.float32)
        slabs[s][...] = jnp.where(keep, one, -1000000000.0).astype(jnp.bfloat16)
    for copy in copies[2:]:
        copy.wait()
    upstream = [
        (cot[r].astype(jnp.float32) * jax.nn.sigmoid(gate[r].astype(jnp.float32))).astype(jnp.bfloat16)
        for r in range(rows)
    ]
    whole = [[ref[r] for r in range(rows)] for ref in (query, keys, values)] + [upstream]
    for head in range(heads):
        cut = slice(head * size, (head + 1) * size)
        for r in range(rows):
            held[head * rows + r] = jnp.concatenate([array[r][:, cut] for array in whole], axis=1)
    for s in range(8):
        packs[s][...] = held[(near * 2 + core) ^ s]


def pre(query, keys, values, gate, cot, bias, mask):
    rows, count, channels = query.shape
    heads, own, half = bias.shape
    token = VMEM(query.shape, jnp.bfloat16)
    width = 4 * channels // heads
    return pl.pallas_call(
        pre_kernel,
        in_specs=[pl.BlockSpec(memory_space=pl.ANY)] * 7,
        out_shape=[jax.ShapeDtypeStruct((count, width), jnp.bfloat16)] * 8
        + [jax.ShapeDtypeStruct((own, half), jnp.bfloat16)] * 4,
        scratch_shapes=[VMEM(bias.shape, jnp.bfloat16), VMEM(mask.shape, jnp.int32)]
        + [token] * 5
        + [pltpu.SemaphoreType.DMA((7,)), VMEM((8, count, width), jnp.bfloat16)],
        compiler_params=PRE_PARAMS,
        name="pack",
    )(query, keys, values, gate, cot, bias, mask)


NT = (((1,), (1,)), ((), ()))


def dot(a, b, dims=(((1,), (0,)), ((), ()))):
    return lax.dot_general(a, b, dims, preferred_element_type=jnp.float32)


def main_kernel(scaling, size, first, final, start, relative, *refs):
    packs, (mine, other), refs = refs[:8], refs[8:10], refs[10:]
    earlier, refs = refs[: 0 if first else 4], refs[0 if first else 4 :]
    (d_mine, d_other), refs = refs[:2], refs[2:]
    results, refs = refs[: 8 if final else 4], refs[8 if final else 4 :]
    held, q_all, d_all, k_of, v_of, dk_t, dv_t, att_all, dq_all, bias_wide, q_now, d_now, back = refs
    step = pl.program_id(0)
    chip, near, core = places()
    _, half, lanes = held.shape
    parts = lanes // size
    blocks, own, _ = mine.shape

    def lanes_of(index, j):
        return jnp.concatenate([held[2 * p + index, :, j * size : (j + 1) * size] for p in range(parts)], axis=1)

    @pl.when(step == 0)
    def _():
        for s in range(8):
            held[(near * 2 + core) ^ s] = packs[s][...]
        lane = lax.broadcasted_iota(jnp.int32, (half, lanes), 1) // size
        for c in range(2):
            rows = slice(c * half, (c + 1) * half)
            q_all[rows], d_all[rows] = lanes_of(c, 0), lanes_of(c, 3)
            k, v = lanes_of(core ^ c, 1), lanes_of(core ^ c, 2)
            for r in range(parts):
                k_of[r, rows] = jnp.where(lane == r, k, 0)
                v_of[r, rows] = jnp.where(lane == r, v, 0)
        for ref, value in zip((att_all, dq_all, dk_t, dv_t), earlier):
            ref[...] = value[...]
        if first:
            for ref in (att_all, dq_all, dk_t, dv_t):
                ref[...] = jnp.zeros_like(ref)

    def strip(i):
        at = start + step * blocks + i
        at = chip ^ at if relative else at
        return pl.ds(pl.multiple_of(at * own, own), own)

    for i in range(blocks):
        rows = slice(i * own, (i + 1) * own)
        bias_wide[rows, :half] = mine[i].astype(jnp.float32)
        bias_wide[rows, half:] = other[i].astype(jnp.float32)
        q_now[rows], d_now[rows] = q_all[strip(i)], d_all[strip(i)]
    q, d = q_now[...], d_now[...]
    q_t = q.astype(jnp.float32).T.astype(jnp.bfloat16)
    d_t = d.astype(jnp.float32).T.astype(jnp.bfloat16)
    d_wide = d.astype(jnp.float32)
    att_sum, dq_sum, bias_sum = None, None, None
    for r in range(parts):
        k, v = k_of[r], v_of[r]
        logits = dot(q, k, NT) * scaling + bias_wide[...]
        expo = jnp.exp(logits - jnp.max(logits, axis=-1, keepdims=True))
        probs = expo * (1.0 / jnp.sum(expo, axis=-1, keepdims=True))
        low = probs.astype(jnp.bfloat16)
        att = dot(low, v)
        inner = jnp.sum(d_wide * att, axis=-1, keepdims=True)
        d_logits = probs * (dot(d, v, NT) - inner)
        d_low = d_logits.astype(jnp.bfloat16)
        dq = dot(d_low, k)
        cut = slice(r * size, (r + 1) * size)
        dk_t[cut] += dot(q_t[cut], d_low)
        dv_t[cut] += dot(d_t[cut], low)
        att_sum = att if r == 0 else att_sum + att
        dq_sum = dq if r == 0 else dq_sum + dq
        bias_sum = d_logits if r == 0 else bias_sum + d_logits
    att_low, dq_low = att_sum.astype(jnp.bfloat16), (dq_sum * scaling).astype(jnp.bfloat16)
    for i in range(blocks):
        rows = slice(i * own, (i + 1) * own)
        att_all[strip(i)], dq_all[strip(i)] = att_low[rows], dq_low[rows]
        d_mine[i] = bias_sum[rows, :half].astype(jnp.bfloat16)
        d_other[i] = bias_sum[rows, half:].astype(jnp.bfloat16)

    @pl.when(step == pl.num_programs(0) - 1)
    def _():
        if not final:
            for ref, value in zip(results, (att_all, dq_all, dk_t, dv_t)):
                ref[...] = value[...]
            return
        dk = (dk_t[...] * scaling).T.astype(jnp.bfloat16)
        dv = dv_t[...].T.astype(jnp.bfloat16)
        for c in range(2):
            back[0, c], back[1, c] = dk[c * half : (c + 1) * half], dv[c * half : (c + 1) * half]
        for c in range(2):
            rows = slice(c * half, (c + 1) * half)
            whole = [att_all[rows], dq_all[rows], back[0, core ^ c], back[1, core ^ c]]
            for p in range(parts):
                cut = slice(p * size, (p + 1) * size)
                held[2 * p + c] = jnp.concatenate([one[:, cut] for one in whole], axis=1)
        for s in range(8):
            results[s][...] = held[(near * 2 + core) ^ s]


def main(packs, mine, other, earlier, scaling, size, blocks, final, start, relative):
    half, lanes = packs[0].shape
    strips, own, _ = mine.shape
    key_count = queries = 2 * half
    rows = jax.ShapeDtypeStruct((queries, lanes), jnp.bfloat16)
    turned = jax.ShapeDtypeStruct((lanes, key_count), jnp.float32)
    strip = pl.BlockSpec((blocks, own, half), lambda i: (i, 0, 0))
    now = VMEM((blocks * own, lanes), jnp.bfloat16)

    def fixed(value):
        return pl.BlockSpec(value.shape, lambda i: (0,) * len(value.shape))

    results = list(packs) if final else [rows, rows, turned, turned]
    elements = strips * own * key_count * (lanes // size)
    return pl.pallas_call(
        functools.partial(main_kernel, scaling, size, not earlier, final, start, relative),
        grid=(strips // blocks,),
        in_specs=[fixed(one) for one in packs] + [strip, strip] + [fixed(one) for one in earlier],
        out_specs=[strip, strip] + [fixed(one) for one in results],
        out_shape=[jax.ShapeDtypeStruct(one.shape, one.dtype) for one in [mine, other] + results],
        scratch_shapes=[
            VMEM((8, half, lanes), jnp.bfloat16),
            VMEM(rows.shape, jnp.bfloat16),
            VMEM(rows.shape, jnp.bfloat16),
            VMEM((lanes // size, key_count, lanes), jnp.bfloat16),
            VMEM((lanes // size, key_count, lanes), jnp.bfloat16),
            VMEM(turned.shape, jnp.float32),
            VMEM(turned.shape, jnp.float32),
            VMEM(rows.shape, jnp.bfloat16),
            VMEM(rows.shape, jnp.bfloat16),
            VMEM((blocks * own, key_count), jnp.float32),
            now,
            now,
            VMEM((2, 2, half, lanes), jnp.bfloat16),
        ],
        compiler_params=PARAMS,
        cost_estimate=pl.CostEstimate(
            flops=12 * elements * size * 8, bytes_accessed=8 * strips * own * key_count, transcendentals=elements
        ),
        name="attention",
    )(*packs, mine, other, *earlier)


def post_kernel(gate, cot, *refs):
    packs, refs = refs[:8], refs[8:]
    pieces, (d_query, d_keys, d_values, d_gate, d_bias, held) = refs[:-6], refs[-6:]
    rows, half, channels = gate.shape
    size = channels // 4
    _, near, core = places()
    for s in range(8):
        held[(near * 2 + core) ^ s] = packs[s][...]
    for s in range(4):
        total = pieces[s][...].astype(jnp.float32)
        for piece in pieces[s + 4 :: 4]:
            total = total + piece[...].astype(jnp.float32)
        d_bias[near ^ s] = total
    for r in range(rows):
        full = []
        for j in range(4):
            full.append(jnp.concatenate([held[rows * h + r, :, j * size : (j + 1) * size] for h in range(4)], axis=1))
        d_query[r], d_keys[r], d_values[r] = full[1], full[2], full[3]
        sig = jax.nn.sigmoid(gate[r].astype(jnp.float32))
        d_gate[r] = (cot[r].astype(jnp.float32) * full[0].astype(jnp.float32) * sig * (1.0 - sig)).astype(jnp.bfloat16)


def post(gate, cot, packs, pieces):
    one = jax.ShapeDtypeStruct(gate.shape, jnp.bfloat16)
    return pl.pallas_call(
        post_kernel,
        out_shape=[one] * 4 + [jax.ShapeDtypeStruct((4,) + pieces[0].shape, jnp.float32)],
        scratch_shapes=[VMEM((8,) + packs[0].shape, jnp.bfloat16)],
        compiler_params=PARAMS,
        name="unpack",
    )(gate, cot, *packs, *pieces)


def shards(query, keys, values, gate_logits, pair_bias, key_mask, grad_out):
    rows, half, channels = query.shape
    heads, own, _ = pair_bias.shape
    size = channels // heads
    scaling = 1.0 / math.sqrt(size)
    chips, cores = lax.axis_size("far") * PAIR * PAIR, lax.axis_size("key")
    assert PAIR * PAIR == heads == 4 and rows == cores == 2
    relative = own % 16 == 0
    chip = places()[0]

    def chip_swap(value, s):
        return lax.ppermute(value, ("far", "near", "side"), [(i, i ^ s) for i in range(chips)]) if s else value

    def pack_swap(value, s):
        return lax.ppermute(value, ("near", "side", "key"), [(i, i ^ s) for i in range(8)]) if s else value

    def other_core(value):
        return lax.ppermute(value, "key", [(0, 1), (1, 0)])

    out = pre(query, keys, values, gate_logits, grad_out, pair_bias, key_mask)
    packs, slabs = out[:8], out[8:]
    order = list(range(4, chips)) + list(range(4))
    arrived = {s: chip_swap(slabs[s % 4], s) for s in order}
    packs = [pack_swap(packs[s], s) for s in range(8)]
    calls = [order[:-4], order[-4:]] if relative else [order]
    earlier, pieces = [], {}
    for call in calls:
        mine = jnp.stack([arrived[s] for s in call])
        if not relative:
            there = [call.index(s) for s in range(chips)]
            mine = mine[jnp.array(there)][chip ^ jnp.arange(chips)].reshape(8, -1, half)
        other = other_core(mine)
        d_mine, d_other, *earlier = main(
            packs, mine, other, earlier, scaling, size, 4, call is calls[-1], call[0] if relative else 0, relative
        )
        d_sum = (d_mine.astype(jnp.float32) + other_core(d_other).astype(jnp.float32)).astype(jnp.bfloat16)
        if not relative:
            d_sum = d_sum.reshape(chips, own, half)[chip ^ jnp.array(call)]
        for i, s in enumerate(call):
            pieces[s] = chip_swap(d_sum[i], s)
    packs = [pack_swap(earlier[s], s) for s in range(8)]
    return tuple(post(gate_logits, grad_out, packs, [pieces[s] for s in range(chips)]))


def solution(mesh):
    groups, rows, cores = mesh.devices.shape
    devices = mesh.devices.reshape(groups, rows // PAIR**2, PAIR, PAIR, cores)
    mesh = jax.sharding.Mesh(devices, ("grp", "far", "near", "side", "key"))
    split = ("grp", "far", "near", "side")
    tokens = P(split, "key", None)
    pair = P(None, split, "key")
    in_specs = (tokens, tokens, tokens, tokens, pair, P(("grp", "key")), tokens)
    out_specs = (tokens, tokens, tokens, tokens, pair)
    return jax.shard_map(shards, mesh=mesh, in_specs=in_specs, out_specs=out_specs, check_vma=False)
```

```python
import functools
import math

import jax
import jax.numpy as jnp
from jax import lax
from jax.experimental import pallas as pl
from jax.experimental.pallas import tpu as pltpu
from jax.sharding import PartitionSpec as P

PAIR = 2
VMEM = pltpu.VMEM
PARAMS = pltpu.CompilerParams(vmem_limit_bytes=32 * 1024 * 1024)
PRE_PARAMS = pltpu.CompilerParams(vmem_limit_bytes=60 * 1024 * 1024)


def places():
    near = lax.axis_index("near") * PAIR + lax.axis_index("side")
    return lax.axis_index("far") * PAIR * PAIR + near, near, lax.axis_index("key")


def fetch(pairs, sems):
    copies = [pltpu.make_async_copy(ref, buffer, sems.at[i]) for i, (ref, buffer) in enumerate(pairs)]
    for copy in copies:
        copy.start()
    for copy in copies:
        copy.wait()


def slab_kernel(bias_ref, mask_ref, *refs):
    slabs, (bias, mask, sems) = refs[:4], refs[4:]
    fetch([(bias_ref, bias), (mask_ref, mask)], sems)
    near = places()[1]
    keep = mask[...].reshape(1, mask.shape[0]) == 1
    for s in range(4):
        one = bias[near ^ s].astype(jnp.float32)
        slabs[s][...] = jnp.where(keep, one, -1000000000.0).astype(jnp.bfloat16)


def make_slabs(bias, mask):
    return pl.pallas_call(
        slab_kernel,
        in_specs=[pl.BlockSpec(memory_space=pl.ANY)] * 2,
        out_shape=[jax.ShapeDtypeStruct(bias.shape[1:], jnp.bfloat16)] * 4,
        scratch_shapes=[VMEM(bias.shape, jnp.bfloat16), VMEM(mask.shape, jnp.int32), pltpu.SemaphoreType.DMA((2,))],
        compiler_params=PRE_PARAMS,
        name="mask_bias",
    )(bias, mask)


def pack_kernel(*refs):
    inputs, packs, buffers, (sems, held) = refs[:5], refs[5:9], refs[9:14], refs[14:]
    fetch(list(zip(inputs, buffers)), sems)
    query, keys, values, gate, cot = buffers
    rows = query.shape[0]
    size = query.shape[2] // 4
    _, near, core = places()
    for r in range(rows):
        upstream = (cot[r].astype(jnp.float32) * jax.nn.sigmoid(gate[r].astype(jnp.float32))).astype(jnp.bfloat16)
        whole = [query[r], keys[r], values[r], upstream]
        for head in range(4):
            held[head, r] = jnp.concatenate([one[:, head * size : (head + 1) * size] for one in whole], axis=1)
    for s in range(4):
        for i in range(2):
            packs[s][i] = held[near ^ s, core ^ i]


def make_packs(*inputs):
    one = inputs[0]
    return pl.pallas_call(
        pack_kernel,
        in_specs=[pl.BlockSpec(memory_space=pl.ANY)] * 5,
        out_shape=[jax.ShapeDtypeStruct(one.shape, jnp.bfloat16)] * 4,
        scratch_shapes=[VMEM(one.shape, jnp.bfloat16)] * 5
        + [pltpu.SemaphoreType.DMA((5,)), VMEM((4,) + one.shape, jnp.bfloat16)],
        compiler_params=PRE_PARAMS,
        name="pack",
    )(*inputs)


NT = (((1,), (1,)), ((), ()))


def dot(a, b, dims=(((1,), (0,)), ((), ()))):
    return lax.dot_general(a, b, dims, preferred_element_type=jnp.float32)


def main_kernel(scaling, size, first, final, start, relative, *refs):
    packs, swapped, (mine, other), refs = refs[:4], refs[4], refs[5:7], refs[7:]
    earlier, refs = refs[: 0 if first else 4], refs[0 if first else 4 :]
    (d_mine, d_other), refs = refs[:2], refs[2:]
    results, refs = refs[: 5 if final else 4], refs[5 if final else 4 :]
    held, q_all, d_all, k_of, v_of, dk_t, dv_t, att_all, dq_all, bias_wide, q_now, d_now, back = refs
    step = pl.program_id(0)
    chip, near, core = places()
    _, half, lanes = held.shape
    parts = lanes // size
    blocks, own, _ = mine.shape

    def lanes_of(index, j):
        return jnp.concatenate([held[2 * p + index, :, j * size : (j + 1) * size] for p in range(parts)], axis=1)

    @pl.when(step == 0)
    def _():
        for s in range(4):
            held[(near ^ s) * 2 + core] = packs[s][0]
            held[(near ^ s) * 2 + 1 - core] = swapped[s]
        lane = lax.broadcasted_iota(jnp.int32, (half, lanes), 1) // size
        for c in range(2):
            rows = slice(c * half, (c + 1) * half)
            q_all[rows], d_all[rows] = lanes_of(c, 0), lanes_of(c, 3)
            k, v = lanes_of(core ^ c, 1), lanes_of(core ^ c, 2)
            for r in range(parts):
                k_of[r, rows] = jnp.where(lane == r, k, 0)
                v_of[r, rows] = jnp.where(lane == r, v, 0)
        for ref, value in zip((att_all, dq_all, dk_t, dv_t), earlier):
            ref[...] = value[...]
        if first:
            for ref in (att_all, dq_all, dk_t, dv_t):
                ref[...] = jnp.zeros_like(ref)

    def strip(i):
        at = start + step * blocks + i
        at = chip ^ at if relative else at
        return pl.ds(pl.multiple_of(at * own, own), own)

    for i in range(blocks):
        rows = slice(i * own, (i + 1) * own)
        bias_wide[rows, :half] = mine[i].astype(jnp.float32)
        bias_wide[rows, half:] = other[i].astype(jnp.float32)
        q_now[rows], d_now[rows] = q_all[strip(i)], d_all[strip(i)]
    q, d = q_now[...], d_now[...]
    q_t = q.astype(jnp.float32).T.astype(jnp.bfloat16)
    d_t = d.astype(jnp.float32).T.astype(jnp.bfloat16)
    d_wide = d.astype(jnp.float32)
    att_sum, dq_sum, bias_sum = None, None, None
    for r in range(parts):
        k, v = k_of[r], v_of[r]
        logits = dot(q, k, NT) * scaling + bias_wide[...]
        expo = jnp.exp(logits - jnp.max(logits, axis=-1, keepdims=True))
        probs = expo * (1.0 / jnp.sum(expo, axis=-1, keepdims=True))
        low = probs.astype(jnp.bfloat16)
        att = dot(low, v)
        inner = jnp.sum(d_wide * att, axis=-1, keepdims=True)
        d_logits = probs * (dot(d, v, NT) - inner)
        d_low = d_logits.astype(jnp.bfloat16)
        dq = dot(d_low, k)
        cut = slice(r * size, (r + 1) * size)
        dk_t[cut] += dot(q_t[cut], d_low)
        dv_t[cut] += dot(d_t[cut], low)
        att_sum = att if r == 0 else att_sum + att
        dq_sum = dq if r == 0 else dq_sum + dq
        bias_sum = d_logits if r == 0 else bias_sum + d_logits
    att_low, dq_low = att_sum.astype(jnp.bfloat16), (dq_sum * scaling).astype(jnp.bfloat16)
    for i in range(blocks):
        rows = slice(i * own, (i + 1) * own)
        att_all[strip(i)], dq_all[strip(i)] = att_low[rows], dq_low[rows]
        d_mine[i] = bias_sum[rows, :half].astype(jnp.bfloat16)
        d_other[i] = bias_sum[rows, half:].astype(jnp.bfloat16)

    @pl.when(step == pl.num_programs(0) - 1)
    def _():
        if not final:
            for ref, value in zip(results, (att_all, dq_all, dk_t, dv_t)):
                ref[...] = value[...]
            return
        dk = (dk_t[...] * scaling).T.astype(jnp.bfloat16)
        dv = dv_t[...].T.astype(jnp.bfloat16)
        for c in range(2):
            back[0, c], back[1, c] = dk[c * half : (c + 1) * half], dv[c * half : (c + 1) * half]
        for c in range(2):
            rows = slice(c * half, (c + 1) * half)
            whole = [att_all[rows], dq_all[rows], back[0, core ^ c], back[1, core ^ c]]
            for p in range(parts):
                cut = slice(p * size, (p + 1) * size)
                held[2 * p + c] = jnp.concatenate([one[:, cut] for one in whole], axis=1)
        for s in range(4):
            results[s][...] = held[(near ^ s) * 2 + core]
            results[4][s] = held[(near ^ s) * 2 + 1 - core]


def main(packs, swapped, mine, other, earlier, scaling, size, blocks, final, start, relative):
    _, half, lanes = packs[0].shape
    strips, own, _ = mine.shape
    key_count = queries = 2 * half
    rows = jax.ShapeDtypeStruct((queries, lanes), jnp.bfloat16)
    turned = jax.ShapeDtypeStruct((lanes, key_count), jnp.float32)
    strip = pl.BlockSpec((blocks, own, half), lambda i: (i, 0, 0))
    now = VMEM((blocks * own, lanes), jnp.bfloat16)

    def fixed(value):
        return pl.BlockSpec(value.shape, lambda i: (0,) * len(value.shape))

    ours = jax.ShapeDtypeStruct((half, lanes), jnp.bfloat16)
    own_row = pl.BlockSpec((1, half, lanes), lambda i: (0, 0, 0))
    results = [ours] * 4 + [swapped] if final else [rows, rows, turned, turned]
    elements = strips * own * key_count * (lanes // size)
    return pl.pallas_call(
        functools.partial(main_kernel, scaling, size, not earlier, final, start, relative),
        grid=(strips // blocks,),
        in_specs=[own_row] * 4 + [fixed(swapped), strip, strip] + [fixed(one) for one in earlier],
        out_specs=[strip, strip] + [fixed(one) for one in results],
        out_shape=[jax.ShapeDtypeStruct(one.shape, one.dtype) for one in [mine, other] + results],
        scratch_shapes=[
            VMEM((8, half, lanes), jnp.bfloat16),
            VMEM(rows.shape, jnp.bfloat16),
            VMEM(rows.shape, jnp.bfloat16),
            VMEM((lanes // size, key_count, lanes), jnp.bfloat16),
            VMEM((lanes // size, key_count, lanes), jnp.bfloat16),
            VMEM(turned.shape, jnp.float32),
            VMEM(turned.shape, jnp.float32),
            VMEM(rows.shape, jnp.bfloat16),
            VMEM(rows.shape, jnp.bfloat16),
            VMEM((blocks * own, key_count), jnp.float32),
            now,
            now,
            VMEM((2, 2, half, lanes), jnp.bfloat16),
        ],
        compiler_params=PARAMS,
        cost_estimate=pl.CostEstimate(
            flops=1, bytes_accessed=1, transcendentals=0
        ),
        name="attention",
    )(*packs, swapped, mine, other, *earlier)


def post_kernel(gate, cot, *refs):
    packs, pieces, (d_query, d_keys, d_values, d_gate, d_bias, held) = refs[:4], refs[4:8], refs[8:]
    rows, half, channels = gate.shape
    size = channels // 4
    _, near, core = places()
    for s in range(4):
        for i in range(2):
            held[near ^ s, core ^ i] = packs[s][i]
        d_bias[near ^ s] = pieces[s][...].astype(jnp.float32)
    for r in range(rows):
        full = []
        for j in range(4):
            full.append(jnp.concatenate([held[h, r, :, j * size : (j + 1) * size] for h in range(4)], axis=1))
        d_query[r], d_keys[r], d_values[r] = full[1], full[2], full[3]
        sig = jax.nn.sigmoid(gate[r].astype(jnp.float32))
        d_gate[r] = (cot[r].astype(jnp.float32) * full[0].astype(jnp.float32) * sig * (1.0 - sig)).astype(jnp.bfloat16)


def post(gate, cot, packs, pieces):
    one = jax.ShapeDtypeStruct(gate.shape, jnp.bfloat16)
    return pl.pallas_call(
        post_kernel,
        out_shape=[one] * 4 + [jax.ShapeDtypeStruct((4,) + pieces[0].shape, jnp.float32)],
        scratch_shapes=[VMEM((4,) + packs[0].shape, jnp.bfloat16)],
        compiler_params=PARAMS,
        name="unpack",
    )(gate, cot, *packs, *pieces)


def shards(query, keys, values, gate_logits, pair_bias, key_mask, grad_out):
    rows, half, channels = query.shape
    heads, own, _ = pair_bias.shape
    size = channels // heads
    scaling = 1.0 / math.sqrt(size)
    far, cores = lax.axis_size("far"), lax.axis_size("key")
    chips = far * PAIR * PAIR
    assert PAIR * PAIR == heads == 4 and rows == cores == 2
    relative = own % 16 == 0
    chip = places()[0]

    def swap(value, axes, s, count):
        return lax.ppermute(value, axes, [(i, i ^ s) for i in range(count)]) if s else value

    def near_swap(value, s):
        return swap(value, ("near", "side"), s, 4)

    def far_swap(value, s):
        return swap(value, "far", s, far)

    def other_core(value):
        return swap(value, "key", 1, 2)

    def wide(value):
        return value.astype(jnp.float32)

    slabs = make_slabs(pair_bias, key_mask)
    arrived = [near_swap(slabs[s], s) for s in range(4)]
    query, *slabs = lax.optimization_barrier((query, *slabs))
    packs = make_packs(query, keys, values, gate_logits, grad_out)
    packs = [near_swap(packs[s], s) for s in range(4)]
    swapped = other_core(jnp.stack([pack[1] for pack in packs]))
    strips = jnp.stack(arrived)
    groups = [far_swap(strips, f) for f in range(far)]
    calls = [(f * 4, groups[f]) for f in range(1, far)] + [(0, groups[0])]
    if not relative:
        strips = jnp.concatenate(groups)[chip ^ jnp.arange(chips)]
        calls = [(0, strips.reshape(8, -1, half))]
    earlier, sums, d_sum = [], {}, None
    for start, mine in calls:
        other = other_core(mine)
        if d_sum is not None:
            mine, d_sum = lax.optimization_barrier((mine, d_sum))
            sums[last] = d_sum
        final = start == calls[-1][0]
        d_mine, d_other, *earlier = main(
            packs, swapped, mine, other, earlier, scaling, size, 4, final, start, relative
        )
        if final and relative:
            d_mine = wide(d_mine)
            for f in range(1, far):
                d_mine = d_mine + wide(far_swap(sums[f * 4], f))
            d_mine = lax.optimization_barrier(d_mine)
        d_sum = (wide(d_mine) + wide(other_core(d_other))).astype(jnp.bfloat16)
        sums[start], last = d_sum, start
    if not relative:
        d_sum = sums[0].reshape(chips, own, half)[chip ^ jnp.arange(chips)]
        sums = {f * 4: d_sum[f * 4 : f * 4 + 4] for f in range(far)}
        total = wide(sums[0])
        for f in range(1, far):
            total = total + wide(far_swap(sums[f * 4], f))
        d_sum = total.astype(jnp.bfloat16)
    pieces = [near_swap(d_sum[s], s) for s in range(4)]
    swapped = other_core(earlier[4])
    packs = [near_swap(jnp.stack([earlier[s], swapped[s]]), s) for s in range(4)]
    return tuple(post(gate_logits, grad_out, packs, pieces))


def solution(mesh):
    groups, rows, cores = mesh.devices.shape
    devices = mesh.devices.reshape(groups, rows // PAIR**2, PAIR, PAIR, cores)
    mesh = jax.sharding.Mesh(devices, ("grp", "far", "near", "side", "key"))
    split = ("grp", "far", "near", "side")
    tokens = P(split, "key", None)
    pair = P(None, split, "key")
    in_specs = (tokens, tokens, tokens, tokens, pair, P(("grp", "key")), tokens)
    out_specs = (tokens, tokens, tokens, tokens, pair)
    return jax.shard_map(shards, mesh=mesh, in_specs=in_specs, out_specs=out_specs, check_vma=False)
```

```python
import functools
import math

import jax
import jax.numpy as jnp
from jax import lax
from jax.experimental import pallas as pl
from jax.experimental.pallas import tpu as pltpu
from jax.sharding import PartitionSpec as P

PAIR = 2
VMEM = pltpu.VMEM
PARAMS = pltpu.CompilerParams(vmem_limit_bytes=32 * 1024 * 1024)
PRE_PARAMS = pltpu.CompilerParams(vmem_limit_bytes=60 * 1024 * 1024)


def places():
    near = lax.axis_index("near") * PAIR + lax.axis_index("side")
    return lax.axis_index("far") * PAIR * PAIR + near, near, lax.axis_index("key")


def fetch(pairs, sems):
    copies = [pltpu.make_async_copy(ref, buffer, sems.at[i]) for i, (ref, buffer) in enumerate(pairs)]
    for copy in copies:
        copy.start()
    for copy in copies:
        copy.wait()


def masked(bias, keep):
    return jnp.where(keep, bias.astype(jnp.float32), -1000000000.0).astype(jnp.bfloat16)


def slab_kernel(bias, mask, *slabs):
    near = places()[1]
    keep = mask[...].reshape(1, mask.shape[0]) == 1
    for s in range(4):
        slabs[s][...] = masked(bias[near ^ s], keep)


def make_slabs(bias, mask):
    return pl.pallas_call(
        slab_kernel,
        out_shape=[jax.ShapeDtypeStruct(bias.shape[1:], jnp.bfloat16)] * 4,
        compiler_params=PARAMS,
        name="mask_bias",
    )(bias, mask)


def padded(own):
    return -(-own // 16) * 16


def pack_kernel(*refs):
    inputs, packs, buffers, (sems, held) = refs[:7], refs[7:11], refs[11:18], refs[18:]
    fetch(list(zip(inputs, buffers)), sems)
    query, keys, values, gate, cot, bias, mask = buffers
    rows, half, channels = query.shape
    size = channels // 4
    own = bias.shape[1]
    _, near, core = places()
    for r in range(rows):
        upstream = (cot[r].astype(jnp.float32) * jax.nn.sigmoid(gate[r].astype(jnp.float32))).astype(jnp.bfloat16)
        whole = [query[r], keys[r], values[r], upstream]
        for head in range(4):
            held[head, r] = jnp.concatenate([one[:, head * size : (head + 1) * size] for one in whole], axis=1)
    keep = mask[...].reshape(1, mask.shape[0]) == 1
    for s in range(4):
        for i in range(2):
            packs[s][i * half : (i + 1) * half] = held[near ^ s, core ^ i]
        slab = masked(bias[near ^ s], keep)
        for i in range(half // channels):
            at = 2 * half + i * padded(own)
            packs[s][at : at + own] = slab[:, i * channels : (i + 1) * channels]


def make_packs(*inputs):
    one, bias = inputs[0], inputs[5]
    rows, half, channels = one.shape
    length = rows * half + half // channels * padded(bias.shape[1])
    return pl.pallas_call(
        pack_kernel,
        in_specs=[pl.BlockSpec(memory_space=pl.ANY)] * 7,
        out_shape=[jax.ShapeDtypeStruct((length, channels), jnp.bfloat16)] * 4,
        scratch_shapes=[VMEM(value.shape, value.dtype) for value in inputs]
        + [pltpu.SemaphoreType.DMA((7,)), VMEM((4,) + one.shape, jnp.bfloat16)],
        compiler_params=PRE_PARAMS,
        name="pack",
    )(*inputs)


NT = (((1,), (1,)), ((), ()))


def dot(a, b, dims=(((1,), (0,)), ((), ()))):
    return lax.dot_general(a, b, dims, preferred_element_type=jnp.float32)


def main_kernel(scaling, size, first, final, start, relative, *refs):
    packs, swapped, (mine, other), refs = refs[:4], refs[4], refs[5:7], refs[7:]
    earlier, refs = refs[: 0 if first else 4], refs[0 if first else 4 :]
    (d_mine, d_other), refs = refs[:2], refs[2:]
    results, refs = refs[:4], refs[4:]
    held, q_all, d_all, k_of, v_of, dk_t, dv_t, att_all, dq_all, bias_wide, q_now, d_now, back = refs
    step = pl.program_id(0)
    chip, near, core = places()
    _, half, lanes = held.shape
    parts = lanes // size
    blocks, own, _ = mine.shape

    def lanes_of(index, j):
        return jnp.concatenate([held[2 * p + index, :, j * size : (j + 1) * size] for p in range(parts)], axis=1)

    @pl.when(step == 0)
    def _():
        for s in range(4):
            held[(near ^ s) * 2 + core] = packs[s][...]
            held[(near ^ s) * 2 + 1 - core] = swapped[s]
        lane = lax.broadcasted_iota(jnp.int32, (half, lanes), 1) // size
        for c in range(2):
            rows = slice(c * half, (c + 1) * half)
            q_all[rows], d_all[rows] = lanes_of(c, 0), lanes_of(c, 3)
            k, v = lanes_of(core ^ c, 1), lanes_of(core ^ c, 2)
            for r in range(parts):
                k_of[r, rows] = jnp.where(lane == r, k, 0)
                v_of[r, rows] = jnp.where(lane == r, v, 0)
        for ref, value in zip((att_all, dq_all, dk_t, dv_t), earlier):
            ref[...] = value[...]
        if first:
            for ref in (att_all, dq_all, dk_t, dv_t):
                ref[...] = jnp.zeros_like(ref)

    def strip(i):
        at = start + step * blocks + i
        at = chip ^ at if relative else at
        return pl.ds(pl.multiple_of(at * own, own), own)

    for i in range(blocks):
        rows = slice(i * own, (i + 1) * own)
        bias_wide[rows, :half] = mine[i].astype(jnp.float32)
        bias_wide[rows, half:] = other[i].astype(jnp.float32)
        q_now[rows], d_now[rows] = q_all[strip(i)], d_all[strip(i)]
    q, d = q_now[...], d_now[...]
    q_t = q.astype(jnp.float32).T.astype(jnp.bfloat16)
    d_t = d.astype(jnp.float32).T.astype(jnp.bfloat16)
    d_wide = d.astype(jnp.float32)
    att_sum, dq_sum, bias_sum = None, None, None
    for r in range(parts):
        k, v = k_of[r], v_of[r]
        logits = dot(q, k, NT) * scaling + bias_wide[...]
        expo = jnp.exp(logits - jnp.max(logits, axis=-1, keepdims=True))
        probs = expo * (1.0 / jnp.sum(expo, axis=-1, keepdims=True))
        low = probs.astype(jnp.bfloat16)
        att = dot(low, v)
        inner = jnp.sum(d_wide * att, axis=-1, keepdims=True)
        d_logits = probs * (dot(d, v, NT) - inner)
        d_low = d_logits.astype(jnp.bfloat16)
        dq = dot(d_low, k)
        cut = slice(r * size, (r + 1) * size)
        dk_t[cut] += dot(q_t[cut], d_low)
        dv_t[cut] += dot(d_t[cut], low)
        att_sum = att if r == 0 else att_sum + att
        dq_sum = dq if r == 0 else dq_sum + dq
        bias_sum = d_logits if r == 0 else bias_sum + d_logits
    att_low, dq_low = att_sum.astype(jnp.bfloat16), (dq_sum * scaling).astype(jnp.bfloat16)
    for i in range(blocks):
        rows = slice(i * own, (i + 1) * own)
        att_all[strip(i)], dq_all[strip(i)] = att_low[rows], dq_low[rows]
        d_mine[i] = bias_sum[rows, :half].astype(jnp.bfloat16)
        d_other[i] = bias_sum[rows, half:].astype(jnp.bfloat16)

    @pl.when(step == pl.num_programs(0) - 1)
    def _():
        if not final:
            for ref, value in zip(results, (att_all, dq_all, dk_t, dv_t)):
                ref[...] = value[...]
            return
        dk = (dk_t[...] * scaling).T.astype(jnp.bfloat16)
        dv = dv_t[...].T.astype(jnp.bfloat16)
        for c in range(2):
            back[0, c], back[1, c] = dk[c * half : (c + 1) * half], dv[c * half : (c + 1) * half]
        for c in range(2):
            rows = slice(c * half, (c + 1) * half)
            whole = [att_all[rows], dq_all[rows], back[0, core ^ c], back[1, core ^ c]]
            for p in range(parts):
                cut = slice(p * size, (p + 1) * size)
                held[2 * p + c] = jnp.concatenate([one[:, cut] for one in whole], axis=1)
        for s in range(4):
            for i in range(2):
                results[s][i] = held[(near ^ s) * 2 + (core ^ i)]


def fixed(value):
    return pl.BlockSpec(value.shape, lambda i: (0,) * len(value.shape))


def main(packs, swapped, mine, other, earlier, scaling, size, blocks, final, start, relative):
    _, half, lanes = swapped.shape
    strips, own, _ = mine.shape
    key_count = queries = 2 * half
    rows = jax.ShapeDtypeStruct((queries, lanes), jnp.bfloat16)
    turned = jax.ShapeDtypeStruct((lanes, key_count), jnp.float32)
    strip = pl.BlockSpec((blocks, own, half), lambda i: (i, 0, 0))
    now = VMEM((blocks * own, lanes), jnp.bfloat16)

    own_row = pl.BlockSpec((half, lanes), lambda i: (0, 0))
    results = [jax.ShapeDtypeStruct((2, half, lanes), jnp.bfloat16)] * 4 if final else [rows, rows, turned, turned]
    elements = strips * own * key_count * (lanes // size)
    return pl.pallas_call(
        functools.partial(main_kernel, scaling, size, not earlier, final, start, relative),
        grid=(strips // blocks,),
        in_specs=[own_row] * 4 + [fixed(swapped), strip, strip] + [fixed(one) for one in earlier],
        out_specs=[strip, strip] + [fixed(one) for one in results],
        out_shape=[jax.ShapeDtypeStruct(one.shape, one.dtype) for one in [mine, other] + results],
        scratch_shapes=[
            VMEM((8, half, lanes), jnp.bfloat16),
            VMEM(rows.shape, jnp.bfloat16),
            VMEM(rows.shape, jnp.bfloat16),
            VMEM((lanes // size, key_count, lanes), jnp.bfloat16),
            VMEM((lanes // size, key_count, lanes), jnp.bfloat16),
            VMEM(turned.shape, jnp.float32),
            VMEM(turned.shape, jnp.float32),
            VMEM(rows.shape, jnp.bfloat16),
            VMEM(rows.shape, jnp.bfloat16),
            VMEM((blocks * own, key_count), jnp.float32),
            now,
            now,
            VMEM((2, 2, half, lanes), jnp.bfloat16),
        ],
        compiler_params=PARAMS,
        cost_estimate=pl.CostEstimate(
            flops=1, bytes_accessed=1, transcendentals=0
        ),
        name="attention",
    )(*packs, swapped, mine, other, *earlier)


def post_kernel(gate, cot, *refs):
    packs, swapped, pieces, (d_query, d_keys, d_values, d_gate, d_bias, held) = refs[:4], refs[4], refs[5:9], refs[9:]
    rows, half, channels = gate.shape
    size = channels // 4
    _, near, core = places()
    for s in range(4):
        held[near ^ s, core] = packs[s][0]
        held[near ^ s, 1 - core] = swapped[s]
        d_bias[near ^ s] = pieces[s][...].astype(jnp.float32)
    for r in range(rows):
        full = []
        for j in range(4):
            full.append(jnp.concatenate([held[h, r, :, j * size : (j + 1) * size] for h in range(4)], axis=1))
        d_query[r], d_keys[r], d_values[r] = full[1], full[2], full[3]
        sig = jax.nn.sigmoid(gate[r].astype(jnp.float32))
        d_gate[r] = (cot[r].astype(jnp.float32) * full[0].astype(jnp.float32) * sig * (1.0 - sig)).astype(jnp.bfloat16)


def post(gate, cot, packs, swapped, pieces):
    one = jax.ShapeDtypeStruct(gate.shape, jnp.bfloat16)
    bias = jax.ShapeDtypeStruct((4,) + pieces[0].shape, jnp.float32)

    first = pl.BlockSpec((1,) + gate.shape[1:], lambda i: (0, 0, 0))
    return pl.pallas_call(
        post_kernel,
        grid=(1,),
        in_specs=[fixed(one)] * 2 + [first] * 4 + [fixed(swapped)] + [fixed(piece) for piece in pieces],
        out_specs=[fixed(one)] * 4 + [fixed(bias)],
        out_shape=[one] * 4 + [bias],
        scratch_shapes=[VMEM((4,) + gate.shape, jnp.bfloat16)],
        compiler_params=PARAMS,
        name="unpack",
    )(gate, cot, *packs, swapped, *pieces)


def shards(query, keys, values, gate_logits, pair_bias, key_mask, grad_out):
    rows, half, channels = query.shape
    heads, own, _ = pair_bias.shape
    size = channels // heads
    scaling = 1.0 / math.sqrt(size)
    far, cores = lax.axis_size("far"), lax.axis_size("key")
    chips = far * PAIR * PAIR
    assert PAIR * PAIR == heads == 4 and rows == cores == 2
    relative = own % 16 == 0
    chip = places()[0]

    def swap(value, axes, s, count):
        return lax.ppermute(value, axes, [(i, i ^ s) for i in range(count)]) if s else value

    def near_swap(value, s):
        return swap(value, ("near", "side"), s, 4)

    def far_swap(value, s):
        return swap(value, "far", s, far)

    def other_core(value):
        return swap(value, "key", 1, 2)

    def wide(value):
        return value.astype(jnp.float32)

    distant = [far_swap(pair_bias, f) for f in range(1, far)]
    packs = make_packs(query, keys, values, gate_logits, grad_out, pair_bias, key_mask)
    packs = [near_swap(packs[s], s) for s in range(4)]
    groups = [None]
    for bias in distant:
        slabs = make_slabs(bias, key_mask)
        slabs = [near_swap(slabs[s], s) for s in range(4)]
        groups.append(jnp.stack(slabs))
        packs = lax.optimization_barrier((*packs, *slabs))[:4]
    groups[0] = jnp.stack([
        jnp.concatenate(
            [pack[at : at + own] for at in range(2 * half, pack.shape[0], padded(own))], axis=1
        )
        for pack in packs
    ])
    swapped = other_core(jnp.stack([pack[half : 2 * half] for pack in packs]))
    calls = [(f * 4, groups[f]) for f in range(1, far)] + [(0, groups[0])]
    if not relative:
        strips = jnp.concatenate(groups)[chip ^ jnp.arange(chips)]
        calls = [(0, strips.reshape(8, -1, half))]
    earlier, sums, d_sum = [], {}, None
    for start, mine in calls:
        other = other_core(mine)
        if d_sum is not None:
            mine, d_sum = lax.optimization_barrier((mine, d_sum))
            sums[last] = d_sum
        final = start == calls[-1][0]
        d_mine, d_other, *earlier = main(
            packs, swapped, mine, other, earlier, scaling, size, 4, final, start, relative
        )
        if final and relative:
            d_mine = wide(d_mine)
            for f in range(1, far):
                d_mine = d_mine + wide(far_swap(sums[f * 4], f))
            d_mine = lax.optimization_barrier(d_mine)
        d_sum = (wide(d_mine) + wide(other_core(d_other))).astype(jnp.bfloat16)
        sums[start], last = d_sum, start
    if not relative:
        d_sum = sums[0].reshape(chips, own, half)[chip ^ jnp.arange(chips)]
        sums = {f * 4: d_sum[f * 4 : f * 4 + 4] for f in range(far)}
        total = wide(sums[0])
        for f in range(1, far):
            total = total + wide(far_swap(sums[f * 4], f))
        d_sum = total.astype(jnp.bfloat16)
    pieces = [near_swap(d_sum[s], s) for s in range(4)]
    packs = [near_swap(earlier[s], s) for s in range(4)]
    packs = lax.optimization_barrier((*packs, *pieces))[:4]
    swapped = other_core(jnp.stack([pack[1] for pack in packs]))
    return tuple(post(gate_logits, grad_out, packs, swapped, pieces))


def solution(mesh):
    groups, rows, cores = mesh.devices.shape
    devices = mesh.devices.reshape(groups, rows // PAIR**2, PAIR, PAIR, cores)
    mesh = jax.sharding.Mesh(devices, ("grp", "far", "near", "side", "key"))
    split = ("grp", "far", "near", "side")
    tokens = P(split, "key", None)
    pair = P(None, split, "key")
    in_specs = (tokens, tokens, tokens, tokens, pair, P(("grp", "key")), tokens)
    out_specs = (tokens, tokens, tokens, tokens, pair)
    return jax.shard_map(shards, mesh=mesh, in_specs=in_specs, out_specs=out_specs, check_vma=False)
```

```python
import functools
import math

import jax
import jax.numpy as jnp
from jax import lax
from jax.experimental import pallas as pl
from jax.experimental.pallas import tpu as pltpu
from jax.sharding import PartitionSpec as P

PAIR = 2
VMEM = pltpu.VMEM
PARAMS = pltpu.CompilerParams(vmem_limit_bytes=32 * 1024 * 1024)
PRE_PARAMS = pltpu.CompilerParams(vmem_limit_bytes=60 * 1024 * 1024)


def places():
    near = lax.axis_index("near") * PAIR + lax.axis_index("side")
    return lax.axis_index("far") * PAIR * PAIR + near, near, lax.axis_index("key")


def fetch(pairs, sems):
    copies = [pltpu.make_async_copy(ref, buffer, sems.at[i]) for i, (ref, buffer) in enumerate(pairs)]
    for copy in copies:
        copy.start()
    for copy in copies:
        copy.wait()


def masked(bias, keep):
    return jnp.where(keep, bias.astype(jnp.float32), -1000000000.0).astype(jnp.bfloat16)


def slab_kernel(bias, mask, *slabs):
    near = places()[1]
    keep = mask[...].reshape(1, mask.shape[0]) == 1
    for s in range(4):
        slabs[s][...] = masked(bias[near ^ s], keep)


def make_slabs(bias, mask):
    return pl.pallas_call(
        slab_kernel,
        out_shape=[jax.ShapeDtypeStruct(bias.shape[1:], jnp.bfloat16)] * 4,
        compiler_params=PARAMS,
        name="mask_bias",
    )(bias, mask)


def pack_kernel(*refs):
    inputs, packs, buffers, (sems, held) = refs[:5], refs[5:9], refs[9:14], refs[14:]
    fetch(list(zip(inputs, buffers)), sems)
    query, keys, values, gate, cot = buffers
    rows = query.shape[0]
    size = query.shape[2] // 4
    _, near, core = places()
    for r in range(rows):
        upstream = (cot[r].astype(jnp.float32) * jax.nn.sigmoid(gate[r].astype(jnp.float32))).astype(jnp.bfloat16)
        whole = [query[r], keys[r], values[r], upstream]
        for head in range(4):
            held[head, r] = jnp.concatenate([one[:, head * size : (head + 1) * size] for one in whole], axis=1)
    for s in range(4):
        for i in range(2):
            packs[s][i] = held[near ^ s, core ^ i]


def make_packs(*inputs):
    one = inputs[0]
    return pl.pallas_call(
        pack_kernel,
        in_specs=[pl.BlockSpec(memory_space=pl.ANY)] * 5,
        out_shape=[jax.ShapeDtypeStruct(one.shape, jnp.bfloat16)] * 4,
        scratch_shapes=[VMEM(one.shape, jnp.bfloat16)] * 5
        + [pltpu.SemaphoreType.DMA((5,)), VMEM((4,) + one.shape, jnp.bfloat16)],
        compiler_params=PRE_PARAMS,
        name="pack",
    )(*inputs)


NT = (((1,), (1,)), ((), ()))


def dot(a, b, dims=(((1,), (0,)), ((), ()))):
    return lax.dot_general(a, b, dims, preferred_element_type=jnp.float32)


def main_kernel(scaling, size, start, relative, begun, ended, opened, closed, *refs):
    packs, swapped, (mine, other), refs = refs[:2], refs[2], refs[3:5], refs[5:]
    earlier, refs = refs[: 4 if begun else 0], refs[4 if begun else 0 :]
    before, refs = refs[: 1 if opened else 0], refs[1 if opened else 0 :]
    d_bias, refs = refs[: 2 if closed else 1], refs[2 if closed else 1 :]
    results, refs = refs[: 2 if ended else 4], refs[2 if ended else 4 :]
    q_all, d_all, k_of, v_of, dk_t, dv_t, att_all, dq_all, bias_wide, q_now, d_now = refs
    step = pl.program_id(0)
    chip, _, core = places()
    parts, half, _ = swapped.shape
    blocks, own, _ = mine.shape
    lanes = parts * size

    def side(i):
        return pl.ds(pl.multiple_of((core ^ i) * half, half), half)

    @pl.when(step == 0)
    def _():
        lane = lax.broadcasted_iota(jnp.int32, (half, lanes), 1) // size
        for i in range(2):
            here = [swapped[p] if i else packs[p][...] for p in range(parts)]
            q, k, v, d = [
                jnp.concatenate([one[:, j * size : (j + 1) * size] for one in here], axis=1) for j in range(4)
            ]
            q_all[side(i)], d_all[side(i)] = q, d
            rows = slice(i * half, (i + 1) * half)
            for r in range(parts):
                k_of[r, rows] = jnp.where(lane == r, k, 0)
                v_of[r, rows] = jnp.where(lane == r, v, 0)
        for i, ref in enumerate((att_all, dq_all, dk_t, dv_t)):
            ref[...] = earlier[i][...] if begun else jnp.zeros_like(ref)

    def strip(i):
        at = start + step * blocks + i
        at = chip ^ at if relative else at
        return pl.ds(pl.multiple_of(at * own, own), own)

    for i in range(blocks):
        rows = slice(i * own, (i + 1) * own)
        bias_wide[rows, :half] = mine[i].astype(jnp.float32)
        bias_wide[rows, half:] = other[i].astype(jnp.float32)
        q_now[rows], d_now[rows] = q_all[strip(i)], d_all[strip(i)]
    q, d = q_now[...], d_now[...]
    q_t = q.astype(jnp.float32).T.astype(jnp.bfloat16)
    d_t = d.astype(jnp.float32).T.astype(jnp.bfloat16)
    d_wide = d.astype(jnp.float32)
    att_sum, dq_sum, bias_sum = None, None, before[0][...] if opened else None
    for r in range(parts):
        k, v = k_of[r], v_of[r]
        logits = dot(q, k, NT) * scaling + bias_wide[...]
        expo = jnp.exp(logits - jnp.max(logits, axis=-1, keepdims=True))
        probs = expo * (1.0 / jnp.sum(expo, axis=-1, keepdims=True))
        low = probs.astype(jnp.bfloat16)
        att = dot(low, v)
        inner = jnp.sum(d_wide * att, axis=-1, keepdims=True)
        d_logits = probs * (dot(d, v, NT) - inner)
        d_low = d_logits.astype(jnp.bfloat16)
        dq = dot(d_low, k)
        cut = slice(r * size, (r + 1) * size)
        dk_t[cut] += dot(q_t[cut], d_low)
        dv_t[cut] += dot(d_t[cut], low)
        att_sum = att if r == 0 else att_sum + att
        dq_sum = dq if r == 0 else dq_sum + dq
        bias_sum = d_logits if bias_sum is None else bias_sum + d_logits
    att_low, dq_low = att_sum.astype(jnp.bfloat16), (dq_sum * scaling).astype(jnp.bfloat16)
    for i in range(blocks):
        rows = slice(i * own, (i + 1) * own)
        att_all[strip(i)], dq_all[strip(i)] = att_low[rows], dq_low[rows]
        if closed:
            d_bias[0][i] = bias_sum[rows, :half].astype(jnp.bfloat16)
            d_bias[1][i] = bias_sum[rows, half:].astype(jnp.bfloat16)
    if not closed:
        d_bias[0][...] = bias_sum

    @pl.when(step == pl.num_programs(0) - 1)
    def _():
        if not ended:
            for ref, value in zip(results, (att_all, dq_all, dk_t, dv_t)):
                ref[...] = value[...]
            return
        dk = (dk_t[...] * scaling).T.astype(jnp.bfloat16)
        dv = dv_t[...].T.astype(jnp.bfloat16)
        for i in range(2):
            rows = slice(i * half, (i + 1) * half)
            whole = [att_all[side(i)], dq_all[side(i)], dk[rows], dv[rows]]
            for p in range(parts):
                results[p][i] = jnp.concatenate([one[:, p * size : (p + 1) * size] for one in whole], axis=1)


def fixed(value):
    return pl.BlockSpec(value.shape, lambda i: (0,) * len(value.shape))


def main(packs, swapped, mine, other, earlier, before, scaling, size, start, relative, ended, closed):
    parts, half, width = swapped.shape
    strips, own, _ = mine.shape
    blocks, lanes = 4, parts * size
    key_count = queries = 2 * half
    rows = jax.ShapeDtypeStruct((queries, lanes), jnp.bfloat16)
    turned = jax.ShapeDtypeStruct((lanes, key_count), jnp.float32)
    wide = jax.ShapeDtypeStruct((strips * own, key_count), jnp.float32)
    strip = pl.BlockSpec((blocks, own, half), lambda i: (i, 0, 0))
    wide_strip = pl.BlockSpec((blocks * own, key_count), lambda i: (i, 0))
    now = VMEM((blocks * own, lanes), jnp.bfloat16)
    own_row = pl.BlockSpec((None, half, width), lambda i: (0, 0, 0))
    results = [jax.ShapeDtypeStruct((2, half, width), jnp.bfloat16)] * parts if ended else [rows, rows, turned, turned]
    d_bias = [mine, other] if closed else [wide]
    return pl.pallas_call(
        functools.partial(main_kernel, scaling, size, start, relative, bool(earlier), ended, bool(before), closed),
        grid=(strips // blocks,),
        in_specs=[own_row] * parts
        + [fixed(swapped), strip, strip]
        + [fixed(one) for one in earlier]
        + [wide_strip] * len(before),
        out_specs=([strip] * 2 if closed else [wide_strip]) + [fixed(one) for one in results],
        out_shape=[jax.ShapeDtypeStruct(one.shape, one.dtype) for one in d_bias + results],
        scratch_shapes=[
            VMEM(rows.shape, jnp.bfloat16),
            VMEM(rows.shape, jnp.bfloat16),
            VMEM((parts, key_count, lanes), jnp.bfloat16),
            VMEM((parts, key_count, lanes), jnp.bfloat16),
            VMEM(turned.shape, jnp.float32),
            VMEM(turned.shape, jnp.float32),
            VMEM(rows.shape, jnp.bfloat16),
            VMEM(rows.shape, jnp.bfloat16),
            VMEM((blocks * own, key_count), jnp.float32),
            now,
            now,
        ],
        compiler_params=PARAMS,
        cost_estimate=pl.CostEstimate(flops=1, bytes_accessed=1, transcendentals=0),
        name="attention",
    )(*packs, swapped, mine, other, *earlier, *before)


def post_kernel(gate, cot, *refs):
    packs, swapped, pieces, (d_query, d_keys, d_values, d_gate, d_bias, held) = refs[:4], refs[4], refs[5:9], refs[9:]
    rows, half, channels = gate.shape
    size = channels // 4
    _, near, core = places()
    for s in range(4):
        held[near ^ s, core] = packs[s][0]
        held[near ^ s, 1 - core] = swapped[s]
        d_bias[near ^ s] = pieces[s][...].astype(jnp.float32)
    for r in range(rows):
        full = []
        for j in range(4):
            full.append(jnp.concatenate([held[h, r, :, j * size : (j + 1) * size] for h in range(4)], axis=1))
        d_query[r], d_keys[r], d_values[r] = full[1], full[2], full[3]
        sig = jax.nn.sigmoid(gate[r].astype(jnp.float32))
        d_gate[r] = (cot[r].astype(jnp.float32) * full[0].astype(jnp.float32) * sig * (1.0 - sig)).astype(jnp.bfloat16)


def post(gate, cot, packs, swapped, pieces):
    one = jax.ShapeDtypeStruct(gate.shape, jnp.bfloat16)
    bias = jax.ShapeDtypeStruct((4,) + pieces[0].shape, jnp.float32)

    first = pl.BlockSpec((1,) + gate.shape[1:], lambda i: (0, 0, 0))
    return pl.pallas_call(
        post_kernel,
        grid=(1,),
        in_specs=[fixed(one)] * 2 + [first] * 4 + [fixed(swapped)] + [fixed(piece) for piece in pieces],
        out_specs=[fixed(one)] * 4 + [fixed(bias)],
        out_shape=[one] * 4 + [bias],
        scratch_shapes=[VMEM((4,) + gate.shape, jnp.bfloat16)],
        compiler_params=PARAMS,
        name="unpack",
    )(gate, cot, *packs, swapped, *pieces)


def shards(query, keys, values, gate_logits, pair_bias, key_mask, grad_out):
    rows, half, channels = query.shape
    heads, own, _ = pair_bias.shape
    size = channels // heads
    scaling = 1.0 / math.sqrt(size)
    far, cores = lax.axis_size("far"), lax.axis_size("key")
    chips = far * PAIR * PAIR
    assert PAIR * PAIR == heads == 4 and rows == cores == 2
    relative = own % 16 == 0
    chip = places()[0]

    def swap(value, axes, s, count):
        return lax.ppermute(value, axes, [(i, i ^ s) for i in range(count)]) if s else value

    def near_swap(value, s):
        return swap(value, ("near", "side"), s, 4)

    def far_swap(value, s):
        return swap(value, "far", s, far)

    def other_core(value):
        return swap(value, "key", 1, 2)

    def wide(value):
        return value.astype(jnp.float32)

    slabs = make_slabs(pair_bias, key_mask)
    strips = jnp.stack([near_swap(slabs[s], s) for s in range(4)])
    groups = [far_swap(strips, f) for f in range(far)]
    packs = make_packs(query, keys, values, gate_logits, grad_out)
    packs = lax.optimization_barrier((*packs, strips))[:4]
    packs = [near_swap(packs[s], s) for s in range(4)]
    sets = [packs[:2], packs[2:]]
    if relative:
        starts = [f * 4 for f in range(far)]
    else:
        starts = [0]
        groups = [jnp.concatenate(groups)[chip ^ jnp.arange(chips)].reshape(8, -1, half)]
    others = [None] * len(starts)
    orders = [list(range(len(starts))), list(range(len(starts)))[::-1]]
    before, sums, returned = [[]] * len(starts), [None] * len(starts), []
    for a, order in enumerate(orders):
        if a:
            sets[a] = lax.optimization_barrier((*sets[a], before[0][0]))[:2]
        swapped = other_core(jnp.stack([pack[1] for pack in sets[a]]))
        earlier = []
        for g in order:
            if others[g] is None:
                if g != order[0]:
                    groups[g] = lax.optimization_barrier((groups[g], out[0]))[0]
                others[g] = other_core(groups[g])
            mine, closed, ended = groups[g], a == len(orders) - 1, g == order[-1]
            if closed and g != order[0]:
                mine, last = lax.optimization_barrier((mine, sums[order[order.index(g) - 1]]))
                sums[order[order.index(g) - 1]] = last
            out = main(
                sets[a], swapped, mine, others[g], earlier, before[g], scaling, size, starts[g], relative, ended, closed
            )
            if not closed:
                before[g], earlier = out[:1], out[1:]
                continue
            d_mine, d_other, *earlier = out
            d_mine = wide(d_mine)
            if ended and relative:
                for f in range(1, far):
                    d_mine = d_mine + wide(far_swap(sums[f], f))
                d_mine = lax.optimization_barrier(d_mine)
            sums[g] = (d_mine + wide(other_core(d_other))).astype(jnp.bfloat16)
        returned += [near_swap(earlier[i], 2 * a + i) for i in range(2)]
    d_sum = sums[0]
    if not relative:
        d_sum = d_sum.reshape(chips, own, half)[chip ^ jnp.arange(chips)]
        total = wide(d_sum[:4])
        for f in range(1, far):
            total = total + wide(far_swap(d_sum[f * 4 : f * 4 + 4], f))
        d_sum = total.astype(jnp.bfloat16)
    pieces = [near_swap(d_sum[s], s) for s in range(4)]
    returned = lax.optimization_barrier((*returned, *pieces))[:4]
    swapped = other_core(jnp.stack([pack[1] for pack in returned]))
    return tuple(post(gate_logits, grad_out, returned, swapped, pieces))


def solution(mesh):
    groups, rows, cores = mesh.devices.shape
    devices = mesh.devices.reshape(groups, rows // PAIR**2, PAIR, PAIR, cores)
    mesh = jax.sharding.Mesh(devices, ("grp", "far", "near", "side", "key"))
    split = ("grp", "far", "near", "side")
    tokens = P(split, "key", None)
    pair = P(None, split, "key")
    in_specs = (tokens, tokens, tokens, tokens, pair, P(("grp", "key")), tokens)
    out_specs = (tokens, tokens, tokens, tokens, pair)
    return jax.shard_map(shards, mesh=mesh, in_specs=in_specs, out_specs=out_specs, check_vma=False)
```

```python
import functools
import math

import jax
import jax.numpy as jnp
from jax import lax
from jax.experimental import pallas as pl
from jax.experimental.pallas import tpu as pltpu
from jax.sharding import PartitionSpec as P

PAIR = 2
VMEM = pltpu.VMEM
PARAMS = pltpu.CompilerParams(vmem_limit_bytes=32 * 1024 * 1024)
PRE_PARAMS = pltpu.CompilerParams(vmem_limit_bytes=60 * 1024 * 1024)


def places():
    near = lax.axis_index("near") * PAIR + lax.axis_index("side")
    return lax.axis_index("far") * PAIR * PAIR + near, near, lax.axis_index("key")


def fetch(pairs, sems):
    copies = [pltpu.make_async_copy(ref, buffer, sems.at[i]) for i, (ref, buffer) in enumerate(pairs)]
    for copy in copies:
        copy.start()
    for copy in copies:
        copy.wait()


def masked(bias, keep):
    return jnp.where(keep, bias.astype(jnp.float32), -1000000000.0).astype(jnp.bfloat16)


def slab_kernel(bias, mask, *slabs):
    near = places()[1]
    keep = mask[...].reshape(1, mask.shape[0]) == 1
    for s in range(4):
        slabs[s][...] = masked(bias[near ^ s], keep)


def make_slabs(bias, mask):
    return pl.pallas_call(
        slab_kernel,
        out_shape=[jax.ShapeDtypeStruct(bias.shape[1:], jnp.bfloat16)] * 4,
        compiler_params=PARAMS,
        name="mask_bias",
    )(bias, mask)


def pack_kernel(*refs):
    inputs, packs, buffers, (sems, held) = refs[:5], refs[5:9], refs[9:14], refs[14:]
    fetch(list(zip(inputs, buffers)), sems)
    query, keys, values, gate, cot = buffers
    rows = query.shape[0]
    size = query.shape[2] // 4
    _, near, core = places()
    for r in range(rows):
        upstream = (cot[r].astype(jnp.float32) * jax.nn.sigmoid(gate[r].astype(jnp.float32))).astype(jnp.bfloat16)
        whole = [query[r], keys[r], values[r], upstream]
        for head in range(4):
            held[head, r] = jnp.concatenate([one[:, head * size : (head + 1) * size] for one in whole], axis=1)
    for s in range(4):
        for i in range(2):
            packs[s][i] = held[near ^ s, core ^ i]


def make_packs(*inputs):
    one = inputs[0]
    return pl.pallas_call(
        pack_kernel,
        in_specs=[pl.BlockSpec(memory_space=pl.ANY)] * 5,
        out_shape=[jax.ShapeDtypeStruct(one.shape, jnp.bfloat16)] * 4,
        scratch_shapes=[VMEM(one.shape, jnp.bfloat16)] * 5
        + [pltpu.SemaphoreType.DMA((5,)), VMEM((4,) + one.shape, jnp.bfloat16)],
        compiler_params=PRE_PARAMS,
        name="pack",
    )(*inputs)


NT = (((1,), (1,)), ((), ()))


def dot(a, b, dims=(((1,), (0,)), ((), ()))):
    return lax.dot_general(a, b, dims, preferred_element_type=jnp.float32)


def main_kernel(scaling, size, first, final, start, relative, *refs):
    packs, swapped, (mine, other), refs = refs[:4], refs[4], refs[5:7], refs[7:]
    earlier, refs = refs[: 0 if first else 4], refs[0 if first else 4 :]
    (d_mine, d_other), refs = refs[:2], refs[2:]
    results, refs = refs[:4], refs[4:]
    held, q_all, d_all, k_of, v_of, dk_t, dv_t, att_all, dq_all, bias_wide, q_now, d_now, back = refs
    step = pl.program_id(0)
    chip, near, core = places()
    _, half, lanes = held.shape
    parts = lanes // size
    blocks, own, _ = mine.shape

    def lanes_of(index, j):
        return jnp.concatenate([held[2 * p + index, :, j * size : (j + 1) * size] for p in range(parts)], axis=1)

    @pl.when(step == 0)
    def _():
        for s in range(4):
            held[(near ^ s) * 2 + core] = packs[s][...]
            held[(near ^ s) * 2 + 1 - core] = swapped[s]
        lane = lax.broadcasted_iota(jnp.int32, (half, lanes), 1) // size
        for c in range(2):
            rows = slice(c * half, (c + 1) * half)
            q_all[rows], d_all[rows] = lanes_of(c, 0), lanes_of(c, 3)
            k, v = lanes_of(core ^ c, 1), lanes_of(core ^ c, 2)
            for r in range(parts):
                k_of[r, rows] = jnp.where(lane == r, k, 0)
                v_of[r, rows] = jnp.where(lane == r, v, 0)
        for ref, value in zip((att_all, dq_all, dk_t, dv_t), earlier):
            ref[...] = value[...]
        if first:
            for ref in (att_all, dq_all, dk_t, dv_t):
                ref[...] = jnp.zeros_like(ref)

    def strip(i):
        at = start + step * blocks + i
        at = chip ^ at if relative else at
        return pl.ds(pl.multiple_of(at * own, own), own)

    for i in range(blocks):
        rows = slice(i * own, (i + 1) * own)
        bias_wide[rows, :half] = mine[i].astype(jnp.float32)
        bias_wide[rows, half:] = other[i].astype(jnp.float32)
        q_now[rows], d_now[rows] = q_all[strip(i)], d_all[strip(i)]
    q, d = q_now[...], d_now[...]
    q_t = q.astype(jnp.float32).T.astype(jnp.bfloat16)
    d_t = d.astype(jnp.float32).T.astype(jnp.bfloat16)
    d_wide = d.astype(jnp.float32)
    att_sum, dq_sum, bias_sum = None, None, None
    for r in range(parts):
        k, v = k_of[r], v_of[r]
        logits = dot(q, k, NT) * scaling + bias_wide[...]
        expo = jnp.exp(logits - jnp.max(logits, axis=-1, keepdims=True))
        probs = expo * (1.0 / jnp.sum(expo, axis=-1, keepdims=True))
        low = probs.astype(jnp.bfloat16)
        att = dot(low, v)
        inner = jnp.sum(d_wide * att, axis=-1, keepdims=True)
        d_logits = probs * (dot(d, v, NT) - inner)
        d_low = d_logits.astype(jnp.bfloat16)
        dq = dot(d_low, k)
        cut = slice(r * size, (r + 1) * size)
        dk_t[cut] += dot(q_t[cut], d_low)
        dv_t[cut] += dot(d_t[cut], low)
        att_sum = att if r == 0 else att_sum + att
        dq_sum = dq if r == 0 else dq_sum + dq
        bias_sum = d_logits if r == 0 else bias_sum + d_logits
    att_low, dq_low = att_sum.astype(jnp.bfloat16), (dq_sum * scaling).astype(jnp.bfloat16)
    for i in range(blocks):
        rows = slice(i * own, (i + 1) * own)
        att_all[strip(i)], dq_all[strip(i)] = att_low[rows], dq_low[rows]
        d_mine[i] = bias_sum[rows, :half].astype(jnp.bfloat16)
        d_other[i] = bias_sum[rows, half:].astype(jnp.bfloat16)

    @pl.when(step == pl.num_programs(0) - 1)
    def _():
        if not final:
            for ref, value in zip(results, (att_all, dq_all, dk_t, dv_t)):
                ref[...] = value[...]
            return
        dk = (dk_t[...] * scaling).T.astype(jnp.bfloat16)
        dv = dv_t[...].T.astype(jnp.bfloat16)
        for c in range(2):
            back[0, c], back[1, c] = dk[c * half : (c + 1) * half], dv[c * half : (c + 1) * half]
        for c in range(2):
            rows = slice(c * half, (c + 1) * half)
            whole = [att_all[rows], dq_all[rows], back[0, core ^ c], back[1, core ^ c]]
            for p in range(parts):
                cut = slice(p * size, (p + 1) * size)
                held[2 * p + c] = jnp.concatenate([one[:, cut] for one in whole], axis=1)
        for s in range(4):
            for i in range(2):
                results[s][i] = held[(near ^ s) * 2 + (core ^ i)]


def fixed(value):
    return pl.BlockSpec(value.shape, lambda i: (0,) * len(value.shape))


def main(packs, swapped, mine, other, earlier, scaling, size, blocks, final, start, relative):
    _, half, lanes = swapped.shape
    strips, own, _ = mine.shape
    key_count = queries = 2 * half
    rows = jax.ShapeDtypeStruct((queries, lanes), jnp.bfloat16)
    turned = jax.ShapeDtypeStruct((lanes, key_count), jnp.float32)
    strip = pl.BlockSpec((blocks, own, half), lambda i: (i, 0, 0))
    now = VMEM((blocks * own, lanes), jnp.bfloat16)

    own_row = pl.BlockSpec((None, half, lanes), lambda i: (0, 0, 0))
    results = [jax.ShapeDtypeStruct((2, half, lanes), jnp.bfloat16)] * 4 if final else [rows, rows, turned, turned]
    elements = strips * own * key_count * (lanes // size)
    return pl.pallas_call(
        functools.partial(main_kernel, scaling, size, not earlier, final, start, relative),
        grid=(strips // blocks,),
        in_specs=[own_row] * 4 + [fixed(swapped), strip, strip] + [fixed(one) for one in earlier],
        out_specs=[strip, strip] + [fixed(one) for one in results],
        out_shape=[jax.ShapeDtypeStruct(one.shape, one.dtype) for one in [mine, other] + results],
        scratch_shapes=[
            VMEM((8, half, lanes), jnp.bfloat16),
            VMEM(rows.shape, jnp.bfloat16),
            VMEM(rows.shape, jnp.bfloat16),
            VMEM((lanes // size, key_count, lanes), jnp.bfloat16),
            VMEM((lanes // size, key_count, lanes), jnp.bfloat16),
            VMEM(turned.shape, jnp.float32),
            VMEM(turned.shape, jnp.float32),
            VMEM(rows.shape, jnp.bfloat16),
            VMEM(rows.shape, jnp.bfloat16),
            VMEM((blocks * own, key_count), jnp.float32),
            now,
            now,
            VMEM((2, 2, half, lanes), jnp.bfloat16),
        ],
        compiler_params=PARAMS,
        cost_estimate=pl.CostEstimate(
            flops=1, bytes_accessed=1, transcendentals=0
        ),
        name="attention",
    )(*packs, swapped, mine, other, *earlier)


def post_kernel(gate, cot, *refs):
    packs, swapped, pieces, (d_query, d_keys, d_values, d_gate, d_bias, held) = refs[:4], refs[4], refs[5:9], refs[9:]
    rows, half, channels = gate.shape
    size = channels // 4
    _, near, core = places()
    for s in range(4):
        held[near ^ s, core] = packs[s][0]
        held[near ^ s, 1 - core] = swapped[s]
        d_bias[near ^ s] = pieces[s][...].astype(jnp.float32)
    for r in range(rows):
        full = []
        for j in range(4):
            full.append(jnp.concatenate([held[h, r, :, j * size : (j + 1) * size] for h in range(4)], axis=1))
        d_query[r], d_keys[r], d_values[r] = full[1], full[2], full[3]
        sig = jax.nn.sigmoid(gate[r].astype(jnp.float32))
        d_gate[r] = (cot[r].astype(jnp.float32) * full[0].astype(jnp.float32) * sig * (1.0 - sig)).astype(jnp.bfloat16)


def post(gate, cot, packs, swapped, pieces):
    one = jax.ShapeDtypeStruct(gate.shape, jnp.bfloat16)
    bias = jax.ShapeDtypeStruct((4,) + pieces[0].shape, jnp.float32)

    first = pl.BlockSpec((1,) + gate.shape[1:], lambda i: (0, 0, 0))
    return pl.pallas_call(
        post_kernel,
        grid=(1,),
        in_specs=[fixed(one)] * 2 + [first] * 4 + [fixed(swapped)] + [fixed(piece) for piece in pieces],
        out_specs=[fixed(one)] * 4 + [fixed(bias)],
        out_shape=[one] * 4 + [bias],
        scratch_shapes=[VMEM((4,) + gate.shape, jnp.bfloat16)],
        compiler_params=PARAMS,
        name="unpack",
    )(gate, cot, *packs, swapped, *pieces)


def shards(query, keys, values, gate_logits, pair_bias, key_mask, grad_out):
    rows, half, channels = query.shape
    heads, own, _ = pair_bias.shape
    size = channels // heads
    scaling = 1.0 / math.sqrt(size)
    far, cores = lax.axis_size("far"), lax.axis_size("key")
    chips = far * PAIR * PAIR
    assert PAIR * PAIR == heads == 4 and rows == cores == 2
    relative = own % 16 == 0
    chip = places()[0]

    def swap(value, axes, s, count):
        return lax.ppermute(value, axes, [(i, i ^ s) for i in range(count)]) if s else value

    def near_swap(value, s):
        return swap(value, ("near", "side"), s, 4)

    def far_swap(value, s):
        return swap(value, "far", s, far)

    def other_core(value):
        return swap(value, "key", 1, 2)

    def wide(value):
        return value.astype(jnp.float32)

    slabs = make_slabs(pair_bias, key_mask)
    strips = jnp.stack([near_swap(slabs[s], s) for s in range(4)])
    groups = [far_swap(strips, f) for f in range(far)]
    packs = make_packs(query, keys, values, gate_logits, grad_out)
    packs = [near_swap(packs[s], s) for s in range(4)]
    packs = lax.optimization_barrier((*packs, *groups[1:]))[:4]
    swapped = other_core(jnp.stack([pack[1] for pack in packs]))
    calls = [(f * 4, groups[f]) for f in range(1, far)] + [(0, groups[0])]
    if not relative:
        strips = jnp.concatenate(groups)[chip ^ jnp.arange(chips)]
        calls = [(0, strips.reshape(8, -1, half))]
    earlier, sums, d_sum = [], {}, None
    for start, mine in calls:
        other = other_core(mine)
        if d_sum is not None:
            mine, d_sum = lax.optimization_barrier((mine, d_sum))
            sums[last] = d_sum
        final = start == calls[-1][0]
        d_mine, d_other, *earlier = main(
            packs, swapped, mine, other, earlier, scaling, size, 4, final, start, relative
        )
        if final and relative:
            d_mine = wide(d_mine)
            for f in range(1, far):
                d_mine = d_mine + wide(far_swap(sums[f * 4], f))
            d_mine = lax.optimization_barrier(d_mine)
        d_sum = (wide(d_mine) + wide(other_core(d_other))).astype(jnp.bfloat16)
        sums[start], last = d_sum, start
    if not relative:
        d_sum = sums[0].reshape(chips, own, half)[chip ^ jnp.arange(chips)]
        sums = {f * 4: d_sum[f * 4 : f * 4 + 4] for f in range(far)}
        total = wide(sums[0])
        for f in range(1, far):
            total = total + wide(far_swap(sums[f * 4], f))
        d_sum = total.astype(jnp.bfloat16)
    pieces = [near_swap(d_sum[s], s) for s in range(4)]
    packs = [near_swap(earlier[s], s) for s in range(4)]
    packs = lax.optimization_barrier((*packs, *pieces))[:4]
    swapped = other_core(jnp.stack([pack[1] for pack in packs]))
    return tuple(post(gate_logits, grad_out, packs, swapped, pieces))


def solution(mesh):
    groups, rows, cores = mesh.devices.shape
    devices = mesh.devices.reshape(groups, rows // PAIR**2, PAIR, PAIR, cores)
    mesh = jax.sharding.Mesh(devices, ("grp", "far", "near", "side", "key"))
    split = ("grp", "far", "near", "side")
    tokens = P(split, "key", None)
    pair = P(None, split, "key")
    in_specs = (tokens, tokens, tokens, tokens, pair, P(("grp", "key")), tokens)
    out_specs = (tokens, tokens, tokens, tokens, pair)
    return jax.shard_map(shards, mesh=mesh, in_specs=in_specs, out_specs=out_specs, check_vma=False)
```

```python
import functools
import math

import jax
import jax.numpy as jnp
from jax import lax
from jax.experimental import pallas as pl
from jax.experimental.pallas import tpu as pltpu
from jax.sharding import PartitionSpec as P

PAIR = 2
ROWS_AT_ONCE = 16
VMEM = pltpu.VMEM
PARAMS = pltpu.CompilerParams(vmem_limit_bytes=32 * 1024 * 1024)
PRE_PARAMS = pltpu.CompilerParams(vmem_limit_bytes=60 * 1024 * 1024)


def places():
    near = lax.axis_index("near") * PAIR + lax.axis_index("side")
    return lax.axis_index("far") * PAIR * PAIR + near, near, lax.axis_index("key")


def fetch(pairs, sems):
    copies = [pltpu.make_async_copy(ref, buffer, sems.at[i]) for i, (ref, buffer) in enumerate(pairs)]
    for copy in copies:
        copy.start()
    for copy in copies:
        copy.wait()


def masked(bias, keep):
    return jnp.where(keep, bias.astype(jnp.float32), -1000000000.0).astype(jnp.bfloat16)


def slab_kernel(bias, mask, *slabs):
    near = places()[1]
    keep = mask[...].reshape(1, mask.shape[0]) == 1
    for s in range(4):
        slabs[s][...] = masked(bias[near ^ s], keep)


def make_slabs(bias, mask):
    return pl.pallas_call(
        slab_kernel,
        out_shape=[jax.ShapeDtypeStruct(bias.shape[1:], jnp.bfloat16)] * 4,
        compiler_params=PARAMS,
        name="mask_bias",
    )(bias, mask)


def pack_kernel(*refs):
    inputs, packs, spare, buffers, (sems, held) = refs[:5], refs[5:9], refs[9], refs[10:15], refs[15:]
    fetch(list(zip(inputs, buffers)), sems)
    query, keys, values, gate, cot = buffers
    rows = query.shape[0]
    size = query.shape[2] // 4
    _, near, core = places()
    for r in range(rows):
        upstream = (cot[r].astype(jnp.float32) * jax.nn.sigmoid(gate[r].astype(jnp.float32))).astype(jnp.bfloat16)
        whole = [query[r], keys[r], values[r], upstream]
        for head in range(4):
            held[head, r] = jnp.concatenate([one[:, head * size : (head + 1) * size] for one in whole], axis=1)
    for s in range(4):
        for i in range(2):
            packs[s][i] = held[near ^ s, core ^ i]
    spare[...] = held[near, 1 - core]


def make_packs(*inputs):
    one = inputs[0]
    return pl.pallas_call(
        pack_kernel,
        in_specs=[pl.BlockSpec(memory_space=pl.ANY)] * 5,
        out_shape=[jax.ShapeDtypeStruct(one.shape, jnp.bfloat16)] * 4
        + [jax.ShapeDtypeStruct(one.shape[1:], jnp.bfloat16)],
        scratch_shapes=[VMEM(one.shape, jnp.bfloat16)] * 5
        + [pltpu.SemaphoreType.DMA((5,)), VMEM((4,) + one.shape, jnp.bfloat16)],
        compiler_params=PRE_PARAMS,
        name="pack",
    )(*inputs)


NT = (((1,), (1,)), ((), ()))


def dot(a, b, dims=(((1,), (0,)), ((), ()))):
    return lax.dot_general(a, b, dims, preferred_element_type=jnp.float32)


def main_kernel(scaling, size, first, final, start, relative, *refs):
    packs, swapped, (mine, other), refs = refs[:4], refs[4], refs[5:7], refs[7:]
    earlier, refs = refs[: 0 if first else 4], refs[0 if first else 4 :]
    (d_mine, d_other), refs = refs[:2], refs[2:]
    results, refs = refs[:4], refs[4:]
    held, q_all, d_all, k_of, v_of, dk_t, dv_t, att_all, dq_all, bias_wide, q_now, d_now, back, s_now, p_now, low_now, d_low_now, bias_sum = refs
    step = pl.program_id(0)
    chip, near, core = places()
    _, half, lanes = held.shape
    parts = lanes // size
    blocks, own, _ = mine.shape

    def lanes_of(index, j):
        return jnp.concatenate([held[2 * p + index, :, j * size : (j + 1) * size] for p in range(parts)], axis=1)

    @pl.when(step == 0)
    def _():
        for s in range(4):
            held[(near ^ s) * 2 + core] = packs[s][...]
            held[(near ^ s) * 2 + 1 - core] = swapped[s]
        lane = lax.broadcasted_iota(jnp.int32, (half, lanes), 1) // size
        for c in range(2):
            rows = slice(c * half, (c + 1) * half)
            q_all[rows], d_all[rows] = lanes_of(c, 0), lanes_of(c, 3)
            k, v = lanes_of(core ^ c, 1), lanes_of(core ^ c, 2)
            for r in range(parts):
                k_of[r, rows] = jnp.where(lane == r, k, 0)
                v_of[r, rows] = jnp.where(lane == r, v, 0)
        for ref, value in zip((att_all, dq_all, dk_t, dv_t), earlier):
            ref[...] = value[...]
        if first:
            for ref in (att_all, dq_all, dk_t, dv_t):
                ref[...] = jnp.zeros_like(ref)

    def strip(i):
        at = start + step * blocks + i
        at = chip ^ at if relative else at
        return pl.ds(pl.multiple_of(at * own, own), own)

    for i in range(blocks):
        rows = slice(i * own, (i + 1) * own)
        bias_wide[rows, :half] = mine[i].astype(jnp.float32)
        bias_wide[rows, half:] = other[i].astype(jnp.float32)
        q_now[rows], d_now[rows] = q_all[strip(i)], d_all[strip(i)]
    q, d = q_now[...], d_now[...]
    q_t = q.astype(jnp.float32).T.astype(jnp.bfloat16)
    d_t = d.astype(jnp.float32).T.astype(jnp.bfloat16)

    def scores(r):
        s_now[r % 2] = dot(q, k_of[r], NT)
        p_now[r % 2] = dot(d, v_of[r], NT)

    att_sum, dq_sum = None, None
    scores(0)
    for r in range(parts):
        if r + 1 < parts:
            scores(r + 1)
        for at in range(0, blocks * own, ROWS_AT_ONCE):
            rows = slice(at, at + ROWS_AT_ONCE)
            logits = s_now[r % 2, rows] * scaling + bias_wide[rows]
            expo = jnp.exp(logits - jnp.max(logits, axis=-1, keepdims=True))
            probs = expo * (1.0 / jnp.sum(expo, axis=-1, keepdims=True))
            d_probs = p_now[r % 2, rows]
            inner = jnp.sum(probs * d_probs, axis=-1, keepdims=True)
            d_logits = probs * (d_probs - inner)
            low_now[r % 2, rows] = probs.astype(jnp.bfloat16)
            d_low_now[r % 2, rows] = d_logits.astype(jnp.bfloat16)
            bias_sum[rows] = d_logits if r == 0 else bias_sum[rows] + d_logits
        low, d_low = low_now[r % 2], d_low_now[r % 2]
        att, dq = dot(low, v_of[r]), dot(d_low, k_of[r])
        cut = slice(r * size, (r + 1) * size)
        dk_t[cut] += dot(q_t[cut], d_low)
        dv_t[cut] += dot(d_t[cut], low)
        att_sum = att if r == 0 else att_sum + att
        dq_sum = dq if r == 0 else dq_sum + dq
    att_low, dq_low = att_sum.astype(jnp.bfloat16), (dq_sum * scaling).astype(jnp.bfloat16)
    for i in range(blocks):
        rows = slice(i * own, (i + 1) * own)
        att_all[strip(i)], dq_all[strip(i)] = att_low[rows], dq_low[rows]
        d_mine[i] = bias_sum[rows, :half].astype(jnp.bfloat16)
        d_other[i] = bias_sum[rows, half:].astype(jnp.bfloat16)

    @pl.when(step == pl.num_programs(0) - 1)
    def _():
        if not final:
            for ref, value in zip(results, (att_all, dq_all, dk_t, dv_t)):
                ref[...] = value[...]
            return
        dk = (dk_t[...] * scaling).T.astype(jnp.bfloat16)
        dv = dv_t[...].T.astype(jnp.bfloat16)
        for c in range(2):
            back[0, c], back[1, c] = dk[c * half : (c + 1) * half], dv[c * half : (c + 1) * half]
        for c in range(2):
            rows = slice(c * half, (c + 1) * half)
            whole = [att_all[rows], dq_all[rows], back[0, core ^ c], back[1, core ^ c]]
            for p in range(parts):
                cut = slice(p * size, (p + 1) * size)
                held[2 * p + c] = jnp.concatenate([one[:, cut] for one in whole], axis=1)
        for s in range(4):
            for i in range(2):
                results[s][i] = held[(near ^ s) * 2 + (core ^ i)]


def fixed(value):
    return pl.BlockSpec(value.shape, lambda i: (0,) * len(value.shape))


def main(packs, swapped, mine, other, earlier, scaling, size, blocks, final, start, relative):
    _, half, lanes = swapped.shape
    strips, own, _ = mine.shape
    key_count = queries = 2 * half
    rows = jax.ShapeDtypeStruct((queries, lanes), jnp.bfloat16)
    turned = jax.ShapeDtypeStruct((lanes, key_count), jnp.float32)
    strip = pl.BlockSpec((blocks, own, half), lambda i: (i, 0, 0))
    now = VMEM((blocks * own, lanes), jnp.bfloat16)

    own_row = pl.BlockSpec((None, half, lanes), lambda i: (0, 0, 0))
    results = [jax.ShapeDtypeStruct((2, half, lanes), jnp.bfloat16)] * 4 if final else [rows, rows, turned, turned]
    elements = strips * own * key_count * (lanes // size)
    return pl.pallas_call(
        functools.partial(main_kernel, scaling, size, not earlier, final, start, relative),
        grid=(strips // blocks,),
        in_specs=[own_row] * 4 + [fixed(swapped), strip, strip] + [fixed(one) for one in earlier],
        out_specs=[strip, strip] + [fixed(one) for one in results],
        out_shape=[jax.ShapeDtypeStruct(one.shape, one.dtype) for one in [mine, other] + results],
        scratch_shapes=[
            VMEM((8, half, lanes), jnp.bfloat16),
            VMEM(rows.shape, jnp.bfloat16),
            VMEM(rows.shape, jnp.bfloat16),
            VMEM((lanes // size, key_count, lanes), jnp.bfloat16),
            VMEM((lanes // size, key_count, lanes), jnp.bfloat16),
            VMEM(turned.shape, jnp.float32),
            VMEM(turned.shape, jnp.float32),
            VMEM(rows.shape, jnp.bfloat16),
            VMEM(rows.shape, jnp.bfloat16),
            VMEM((blocks * own, key_count), jnp.float32),
            now,
            now,
            VMEM((2, 2, half, lanes), jnp.bfloat16),
            VMEM((2, blocks * own, key_count), jnp.float32),
            VMEM((2, blocks * own, key_count), jnp.float32),
            VMEM((2, blocks * own, key_count), jnp.bfloat16),
            VMEM((2, blocks * own, key_count), jnp.bfloat16),
            VMEM((blocks * own, key_count), jnp.float32),
        ],
        compiler_params=PARAMS,
        cost_estimate=pl.CostEstimate(
            flops=1, bytes_accessed=1, transcendentals=0
        ),
        name="attention",
    )(*packs, swapped, mine, other, *earlier)


def post_kernel(gate, cot, *refs):
    packs, swapped, pieces, (d_query, d_keys, d_values, d_gate, d_bias, held) = refs[:4], refs[4], refs[5:9], refs[9:]
    rows, half, channels = gate.shape
    size = channels // 4
    _, near, core = places()
    for s in range(4):
        held[near ^ s, core] = packs[s][0]
        held[near ^ s, 1 - core] = swapped[s]
        d_bias[near ^ s] = pieces[s][...].astype(jnp.float32)
    for r in range(rows):
        full = []
        for j in range(4):
            full.append(jnp.concatenate([held[h, r, :, j * size : (j + 1) * size] for h in range(4)], axis=1))
        d_query[r], d_keys[r], d_values[r] = full[1], full[2], full[3]
        sig = jax.nn.sigmoid(gate[r].astype(jnp.float32))
        d_gate[r] = (cot[r].astype(jnp.float32) * full[0].astype(jnp.float32) * sig * (1.0 - sig)).astype(jnp.bfloat16)


def post(gate, cot, packs, swapped, pieces):
    one = jax.ShapeDtypeStruct(gate.shape, jnp.bfloat16)
    bias = jax.ShapeDtypeStruct((4,) + pieces[0].shape, jnp.float32)

    first = pl.BlockSpec((1,) + gate.shape[1:], lambda i: (0, 0, 0))
    return pl.pallas_call(
        post_kernel,
        grid=(1,),
        in_specs=[fixed(one)] * 2 + [first] * 4 + [fixed(swapped)] + [fixed(piece) for piece in pieces],
        out_specs=[fixed(one)] * 4 + [fixed(bias)],
        out_shape=[one] * 4 + [bias],
        scratch_shapes=[VMEM((4,) + gate.shape, jnp.bfloat16)],
        compiler_params=PARAMS,
        name="unpack",
    )(gate, cot, *packs, swapped, *pieces)


def shards(query, keys, values, gate_logits, pair_bias, key_mask, grad_out):
    rows, half, channels = query.shape
    heads, own, _ = pair_bias.shape
    size = channels // heads
    scaling = 1.0 / math.sqrt(size)
    far, cores = lax.axis_size("far"), lax.axis_size("key")
    chips = far * PAIR * PAIR
    assert PAIR * PAIR == heads == 4 and rows == cores == 2
    relative = own % 16 == 0
    chip = places()[0]

    def swap(value, axes, s, count):
        return lax.ppermute(value, axes, [(i, i ^ s) for i in range(count)]) if s else value

    def near_swap(value, s):
        return swap(value, ("near", "side"), s, 4)

    def far_swap(value, s):
        return swap(value, "far", s, far)

    def other_core(value):
        return swap(value, "key", 1, 2)

    def wide(value):
        return value.astype(jnp.float32)

    slabs = make_slabs(pair_bias, key_mask)
    strips = jnp.stack([near_swap(slabs[s], s) for s in range(4)])
    groups = [far_swap(strips, f) for f in range(far)]
    *packs, spare = make_packs(query, keys, values, gate_logits, grad_out)
    packs = [near_swap(packs[s], s) for s in range(4)]
    swapped = other_core(jnp.stack([spare] + [pack[1] for pack in packs[1:]]))
    calls = [(f * 4, groups[f]) for f in range(1, far)] + [(0, groups[0])]
    if not relative:
        strips = jnp.concatenate(groups)[chip ^ jnp.arange(chips)]
        calls = [(0, strips.reshape(8, -1, half))]
    earlier, sums, d_sum = [], {}, None
    for start, mine in calls:
        other = other_core(mine)
        if d_sum is not None:
            mine, d_sum = lax.optimization_barrier((mine, d_sum))
            sums[last] = d_sum
        final = start == calls[-1][0]
        d_mine, d_other, *earlier = main(
            packs, swapped, mine, other, earlier, scaling, size, 4, final, start, relative
        )
        if final and relative:
            d_mine = wide(d_mine)
            for f in range(1, far):
                d_mine = d_mine + wide(far_swap(sums[f * 4], f))
            d_mine = lax.optimization_barrier(d_mine)
        d_sum = (wide(d_mine) + wide(other_core(d_other))).astype(jnp.bfloat16)
        sums[start], last = d_sum, start
    if not relative:
        d_sum = sums[0].reshape(chips, own, half)[chip ^ jnp.arange(chips)]
        sums = {f * 4: d_sum[f * 4 : f * 4 + 4] for f in range(far)}
        total = wide(sums[0])
        for f in range(1, far):
            total = total + wide(far_swap(sums[f * 4], f))
        d_sum = total.astype(jnp.bfloat16)
    pieces = [near_swap(d_sum[s], s) for s in range(4)]
    packs = [near_swap(earlier[s], s) for s in range(4)]
    packs = lax.optimization_barrier((*packs, *pieces))[:4]
    swapped = other_core(jnp.stack([pack[1] for pack in packs]))
    return tuple(post(gate_logits, grad_out, packs, swapped, pieces))


def solution(mesh):
    groups, rows, cores = mesh.devices.shape
    devices = mesh.devices.reshape(groups, rows // PAIR**2, PAIR, PAIR, cores)
    mesh = jax.sharding.Mesh(devices, ("grp", "far", "near", "side", "key"))
    split = ("grp", "far", "near", "side")
    tokens = P(split, "key", None)
    pair = P(None, split, "key")
    in_specs = (tokens, tokens, tokens, tokens, pair, P(("grp", "key")), tokens)
    out_specs = (tokens, tokens, tokens, tokens, pair)
    return jax.shard_map(shards, mesh=mesh, in_specs=in_specs, out_specs=out_specs, check_vma=False)
```

```python
import functools
import math

import jax
import jax.numpy as jnp
from jax import lax
from jax.experimental import pallas as pl
from jax.experimental.pallas import tpu as pltpu
from jax.sharding import PartitionSpec as P

PAIR = 2
OTHER_PARTS, PACK_PARTS = (2, 4), 1
ROWS_AT_ONCE = 16
VMEM = pltpu.VMEM
PARAMS = pltpu.CompilerParams(vmem_limit_bytes=32 * 1024 * 1024)
PRE_PARAMS = pltpu.CompilerParams(vmem_limit_bytes=60 * 1024 * 1024)


def places():
    near = lax.axis_index("near") * PAIR + lax.axis_index("side")
    return lax.axis_index("far") * PAIR * PAIR + near, near, lax.axis_index("key")


def fetch(pairs, sems):
    copies = [pltpu.make_async_copy(ref, buffer, sems.at[i]) for i, (ref, buffer) in enumerate(pairs)]
    for copy in copies:
        copy.start()
    for copy in copies:
        copy.wait()


def masked(bias, keep):
    return jnp.where(keep, bias.astype(jnp.float32), -1000000000.0).astype(jnp.bfloat16)


def slab_kernel(bias, mask, *outs):
    near = places()[1]
    keep = mask[...].reshape(1, mask.shape[0]) == 1
    for s in range(4):
        slab = masked(bias[near ^ s], keep)
        outs[s][...] = slab
        outs[4 + s // 2][s % 2] = slab


def make_slabs(bias, mask):
    _, own, half = bias.shape
    return pl.pallas_call(
        slab_kernel,
        out_shape=[jax.ShapeDtypeStruct((own, half), jnp.bfloat16)] * 4
        + [jax.ShapeDtypeStruct((2, own, half), jnp.bfloat16)] * 2,
        compiler_params=PARAMS,
        name="mask_bias",
    )(bias, mask)


def pack_kernel(*refs):
    inputs, packs, spare, buffers, (sems, held) = refs[:5], refs[5:9], refs[9], refs[10:15], refs[15:]
    fetch(list(zip(inputs, buffers)), sems)
    query, keys, values, gate, cot = buffers
    rows = query.shape[0]
    size = query.shape[2] // 4
    _, near, core = places()
    for r in range(rows):
        upstream = (cot[r].astype(jnp.float32) * jax.nn.sigmoid(gate[r].astype(jnp.float32))).astype(jnp.bfloat16)
        whole = [query[r], keys[r], values[r], upstream]
        for head in range(4):
            held[head, r] = jnp.concatenate([one[:, head * size : (head + 1) * size] for one in whole], axis=1)
    for s in range(4):
        for i in range(2):
            packs[s][i] = held[near ^ s, core ^ i]
    spare[...] = held[near, 1 - core]


def make_packs(*inputs):
    one = inputs[0]
    return pl.pallas_call(
        pack_kernel,
        in_specs=[pl.BlockSpec(memory_space=pl.ANY)] * 5,
        out_shape=[jax.ShapeDtypeStruct(one.shape, jnp.bfloat16)] * 4
        + [jax.ShapeDtypeStruct(one.shape[1:], jnp.bfloat16)],
        scratch_shapes=[VMEM(one.shape, jnp.bfloat16)] * 5
        + [pltpu.SemaphoreType.DMA((5,)), VMEM((4,) + one.shape, jnp.bfloat16)],
        compiler_params=PRE_PARAMS,
        name="pack",
    )(*inputs)


NT = (((1,), (1,)), ((), ()))


def dot(a, b, dims=(((1,), (0,)), ((), ()))):
    return lax.dot_general(a, b, dims, preferred_element_type=jnp.float32)


def main_kernel(scaling, size, start, relative, begun, ended, opened, closed, *refs):
    packs, swapped, (mine, other), refs = refs[:2], refs[2:4], refs[4:6], refs[6:]
    earlier, refs = refs[: 4 if begun else 0], refs[4 if begun else 0 :]
    before, refs = refs[: 1 if opened else 0], refs[1 if opened else 0 :]
    d_bias, refs = refs[: 2 if closed else 1], refs[2 if closed else 1 :]
    results, refs = refs[: 2 if ended else 4], refs[2 if ended else 4 :]
    q_all, d_all, k_of, v_of, dk_t, dv_t, att_all, dq_all, bias_wide, q_now, d_now, s_now, p_now, low_now, d_low_now, bias_sum = refs
    step = pl.program_id(0)
    chip, _, core = places()
    parts, (half, _) = len(packs), packs[0].shape
    blocks, own, _ = mine.shape
    lanes = parts * size

    def side(i):
        return pl.ds(pl.multiple_of((core ^ i) * half, half), half)

    @pl.when(step == 0)
    def _():
        lane = lax.broadcasted_iota(jnp.int32, (half, lanes), 1) // size
        for i in range(2):
            here = [(swapped if i else packs)[p][...] for p in range(parts)]
            q, k, v, d = [
                jnp.concatenate([one[:, j * size : (j + 1) * size] for one in here], axis=1) for j in range(4)
            ]
            q_all[side(i)], d_all[side(i)] = q, d
            rows = slice(i * half, (i + 1) * half)
            for r in range(parts):
                k_of[r, rows] = jnp.where(lane == r, k, 0)
                v_of[r, rows] = jnp.where(lane == r, v, 0)
        for i, ref in enumerate((att_all, dq_all, dk_t, dv_t)):
            ref[...] = earlier[i][...] if begun else jnp.zeros_like(ref)

    def strip(i):
        at = start + step * blocks + i
        at = chip ^ at if relative else at
        return pl.ds(pl.multiple_of(at * own, own), own)

    for i in range(blocks):
        rows = slice(i * own, (i + 1) * own)
        bias_wide[rows, :half] = mine[i].astype(jnp.float32)
        bias_wide[rows, half:] = other[i].astype(jnp.float32)
        q_now[rows], d_now[rows] = q_all[strip(i)], d_all[strip(i)]
    q, d = q_now[...], d_now[...]
    q_t = q.astype(jnp.float32).T.astype(jnp.bfloat16)
    d_t = d.astype(jnp.float32).T.astype(jnp.bfloat16)

    def scores(r):
        s_now[r % 2] = dot(q, k_of[r], NT)
        p_now[r % 2] = dot(d, v_of[r], NT)

    att_sum, dq_sum = None, None
    scores(0)
    for r in range(parts):
        if r + 1 < parts:
            scores(r + 1)
        for at in range(0, blocks * own, ROWS_AT_ONCE):
            rows = slice(at, at + ROWS_AT_ONCE)
            logits = s_now[r % 2, rows] * scaling + bias_wide[rows]
            expo = jnp.exp(logits - jnp.max(logits, axis=-1, keepdims=True))
            probs = expo * (1.0 / jnp.sum(expo, axis=-1, keepdims=True))
            d_probs = p_now[r % 2, rows]
            inner = jnp.sum(probs * d_probs, axis=-1, keepdims=True)
            d_logits = probs * (d_probs - inner)
            low_now[r % 2, rows] = probs.astype(jnp.bfloat16)
            d_low_now[r % 2, rows] = d_logits.astype(jnp.bfloat16)
            if r:
                d_logits = bias_sum[rows] + d_logits
            elif opened:
                d_logits = before[0][rows] + d_logits
            bias_sum[rows] = d_logits
        low, d_low = low_now[r % 2], d_low_now[r % 2]
        att, dq = dot(low, v_of[r]), dot(d_low, k_of[r])
        cut = slice(r * size, (r + 1) * size)
        dk_t[cut] += dot(q_t[cut], d_low)
        dv_t[cut] += dot(d_t[cut], low)
        att_sum = att if r == 0 else att_sum + att
        dq_sum = dq if r == 0 else dq_sum + dq
    att_low, dq_low = att_sum.astype(jnp.bfloat16), (dq_sum * scaling).astype(jnp.bfloat16)
    for i in range(blocks):
        rows = slice(i * own, (i + 1) * own)
        att_all[strip(i)], dq_all[strip(i)] = att_low[rows], dq_low[rows]
        if closed:
            d_bias[0][i] = bias_sum[rows, :half].astype(jnp.bfloat16)
            d_bias[1][i] = bias_sum[rows, half:].astype(jnp.bfloat16)
    if not closed:
        d_bias[0][...] = bias_sum[...]

    @pl.when(step == pl.num_programs(0) - 1)
    def _():
        if not ended:
            for ref, value in zip(results, (att_all, dq_all, dk_t, dv_t)):
                ref[...] = value[...]
            return
        dk = (dk_t[...] * scaling).T.astype(jnp.bfloat16)
        dv = dv_t[...].T.astype(jnp.bfloat16)
        for i in range(2):
            rows = slice(i * half, (i + 1) * half)
            whole = [att_all[side(i)], dq_all[side(i)], dk[rows], dv[rows]]
            for p in range(parts):
                results[p][i] = jnp.concatenate([one[:, p * size : (p + 1) * size] for one in whole], axis=1)


def fixed(value):
    return pl.BlockSpec(value.shape, lambda i: (0,) * len(value.shape))


def main(packs, swapped, mine, other, earlier, before, scaling, size, start, relative, ended, closed):
    parts, (half, width) = len(packs), swapped[0].shape
    strips, own, _ = mine.shape
    blocks, lanes = 4, parts * size
    key_count = queries = 2 * half
    rows = jax.ShapeDtypeStruct((queries, lanes), jnp.bfloat16)
    turned = jax.ShapeDtypeStruct((lanes, key_count), jnp.float32)
    wide = jax.ShapeDtypeStruct((strips * own, key_count), jnp.float32)
    strip = pl.BlockSpec((blocks, own, half), lambda i: (i, 0, 0))
    wide_strip = pl.BlockSpec((blocks * own, key_count), lambda i: (i, 0))
    now = VMEM((blocks * own, lanes), jnp.bfloat16)
    own_row = pl.BlockSpec((None, half, width), lambda i: (0, 0, 0))
    results = [jax.ShapeDtypeStruct((2, half, width), jnp.bfloat16)] * parts if ended else [rows, rows, turned, turned]
    d_bias = [mine, other] if closed else [wide]
    return pl.pallas_call(
        functools.partial(main_kernel, scaling, size, start, relative, bool(earlier), ended, bool(before), closed),
        grid=(strips // blocks,),
        in_specs=[own_row] * parts
        + [fixed(one) for one in swapped]
        + [strip, strip]
        + [fixed(one) for one in earlier]
        + [wide_strip] * len(before),
        out_specs=([strip] * 2 if closed else [wide_strip]) + [fixed(one) for one in results],
        out_shape=[jax.ShapeDtypeStruct(one.shape, one.dtype) for one in d_bias + results],
        scratch_shapes=[
            VMEM(rows.shape, jnp.bfloat16),
            VMEM(rows.shape, jnp.bfloat16),
            VMEM((parts, key_count, lanes), jnp.bfloat16),
            VMEM((parts, key_count, lanes), jnp.bfloat16),
            VMEM(turned.shape, jnp.float32),
            VMEM(turned.shape, jnp.float32),
            VMEM(rows.shape, jnp.bfloat16),
            VMEM(rows.shape, jnp.bfloat16),
            VMEM((blocks * own, key_count), jnp.float32),
            now,
            now,
            VMEM((2, blocks * own, key_count), jnp.float32),
            VMEM((2, blocks * own, key_count), jnp.float32),
            VMEM((2, blocks * own, key_count), jnp.bfloat16),
            VMEM((2, blocks * own, key_count), jnp.bfloat16),
            VMEM((blocks * own, key_count), jnp.float32),
        ],
        compiler_params=PARAMS,
        cost_estimate=pl.CostEstimate(flops=1, bytes_accessed=1, transcendentals=0),
        name="attention",
    )(*packs, *swapped, mine, other, *earlier, *before)


def post_kernel(gate, cot, *refs):
    packs, swapped, pieces, (d_query, d_keys, d_values, d_gate, d_bias, held) = refs[:4], refs[4], refs[5:9], refs[9:]
    rows, half, channels = gate.shape
    size = channels // 4
    _, near, core = places()
    for s in range(4):
        held[near ^ s, core] = packs[s][0]
        held[near ^ s, 1 - core] = swapped[s]
        d_bias[near ^ s] = pieces[s][...].astype(jnp.float32)
    for r in range(rows):
        full = []
        for j in range(4):
            full.append(jnp.concatenate([held[h, r, :, j * size : (j + 1) * size] for h in range(4)], axis=1))
        d_query[r], d_keys[r], d_values[r] = full[1], full[2], full[3]
        sig = jax.nn.sigmoid(gate[r].astype(jnp.float32))
        d_gate[r] = (cot[r].astype(jnp.float32) * full[0].astype(jnp.float32) * sig * (1.0 - sig)).astype(jnp.bfloat16)


def post(gate, cot, packs, swapped, pieces):
    one = jax.ShapeDtypeStruct(gate.shape, jnp.bfloat16)
    bias = jax.ShapeDtypeStruct((4,) + pieces[0].shape, jnp.float32)

    first = pl.BlockSpec((1,) + gate.shape[1:], lambda i: (0, 0, 0))
    return pl.pallas_call(
        post_kernel,
        grid=(1,),
        in_specs=[fixed(one)] * 2 + [first] * 4 + [fixed(swapped)] + [fixed(piece) for piece in pieces],
        out_specs=[fixed(one)] * 4 + [fixed(bias)],
        out_shape=[one] * 4 + [bias],
        scratch_shapes=[VMEM((4,) + gate.shape, jnp.bfloat16)],
        compiler_params=PARAMS,
        name="unpack",
    )(gate, cot, *packs, swapped, *pieces)


def shards(query, keys, values, gate_logits, pair_bias, key_mask, grad_out):
    rows, half, channels = query.shape
    heads, own, _ = pair_bias.shape
    size = channels // heads
    scaling = 1.0 / math.sqrt(size)
    far, cores = lax.axis_size("far"), lax.axis_size("key")
    chips = far * PAIR * PAIR
    assert PAIR * PAIR == heads == 4 and rows == cores == 2
    relative = own % 16 == 0
    chip = places()[0]

    def swap(value, axes, s, count):
        return lax.ppermute(value, axes, [(i, i ^ s) for i in range(count)]) if s else value

    def near_swap(value, s):
        return swap(value, ("near", "side"), s, 4)

    def other_core(value):
        return swap(value, "key", 1, 2)

    def in_parts(value, count):
        return jnp.concatenate([other_core(part) for part in jnp.split(value, count)])

    def far_swap(pairs, f, after):
        got = [swap(pairs[a], ("far", "near"), 2 * f + a, 2 * far) for a in range(2)]
        got = lax.optimization_barrier((*got, *after))[:2]
        beside = swap(jnp.stack([got[0][1], got[1][1]]), "side", 1, 2)
        return [got[0][0], beside[0], got[1][0], beside[1]]

    def wide(value):
        return value.astype(jnp.float32)

    *slabs, pair_0, pair_1 = make_slabs(pair_bias, key_mask)
    *packs, spare = make_packs(query, keys, values, gate_logits, grad_out)
    strips = jnp.stack([near_swap(slabs[s], s) for s in range(4)])
    distant = [far_swap((pair_0, pair_1), f, (spare, strips)) for f in range(1, far)]
    packs = [near_swap(packs[s], s) for s in range(4)]
    spare, packs[1] = lax.optimization_barrier((spare, packs[1]))
    sets = [packs[:2], packs[2:]]
    groups = [strips] + [jnp.stack(one) for one in distant]
    groups = list(lax.optimization_barrier(tuple(groups)))
    starts = [4 * f for f in range(far)]
    if not relative:
        starts, groups = [0], [jnp.concatenate(groups)[chip ^ jnp.arange(chips)].reshape(8, -1, half)]
    others = [None] * len(starts)
    orders = [list(range(len(starts))), list(range(len(starts)))[::-1]]
    before, sums, returned = [[]] * len(starts), [None] * len(starts), []
    for a, order in enumerate(orders):
        if a:
            sets[a] = lax.optimization_barrier((*sets[a], out[0]))[:2]
        swapped = [in_parts(spare if a == i == 0 else sets[a][i][1], 1 if a else PACK_PARTS) for i in range(2)]
        earlier = []
        for g in order:
            if others[g] is None:
                others[g] = in_parts(groups[g], OTHER_PARTS[min(g, 1)])
            mine, closed, ended = groups[g], a == len(orders) - 1, g == order[-1]
            if closed and g != order[0]:
                mine, last = lax.optimization_barrier((mine, sums[order[order.index(g) - 1]]))
                sums[order[order.index(g) - 1]] = last
            out = main(
                sets[a], swapped, mine, others[g], earlier, before[g], scaling, size, starts[g], relative, ended, closed
            )
            if not closed:
                before[g], earlier = out[:1], out[1:]
                continue
            d_mine, d_other, *earlier = out
            d_mine = wide(d_mine)
            if ended and relative:
                for f in range(1, far):
                    d_mine = d_mine + wide(swap(sums[f], "far", f, far))
                d_mine = lax.optimization_barrier(d_mine)
            sums[g] = (d_mine + wide(other_core(d_other))).astype(jnp.bfloat16)
        returned += [near_swap(earlier[i], 2 * a + i) for i in range(2)]
    d_sum = sums[0]
    if not relative:
        d_sum = d_sum.reshape(chips, own, half)[chip ^ jnp.arange(chips)]
        total = wide(d_sum[:4])
        for f in range(1, far):
            total = total + wide(swap(d_sum[4 * f : 4 * f + 4], "far", f, far))
        d_sum = total.astype(jnp.bfloat16)
    pieces = [near_swap(d_sum[s], s) for s in range(4)]
    returned = lax.optimization_barrier((*returned, *pieces))[:4]
    swapped = other_core(jnp.stack([pack[1] for pack in returned]))
    return tuple(post(gate_logits, grad_out, returned, swapped, pieces))


def solution(mesh):
    groups, rows, cores = mesh.devices.shape
    devices = mesh.devices.reshape(groups, rows // PAIR**2, PAIR, PAIR, cores)
    mesh = jax.sharding.Mesh(devices, ("grp", "far", "near", "side", "key"))
    split = ("grp", "far", "near", "side")
    tokens = P(split, "key", None)
    pair = P(None, split, "key")
    in_specs = (tokens, tokens, tokens, tokens, pair, P(("grp", "key")), tokens)
    out_specs = (tokens, tokens, tokens, tokens, pair)
    return jax.shard_map(shards, mesh=mesh, in_specs=in_specs, out_specs=out_specs, check_vma=False)
```

```python
import functools
import math

import jax
import jax.numpy as jnp
from jax import lax
from jax.experimental import pallas as pl
from jax.experimental.pallas import tpu as pltpu
from jax.sharding import PartitionSpec as P

PAIR = 2
ROWS_AT_ONCE = 16
VMEM = pltpu.VMEM
PARAMS = pltpu.CompilerParams(vmem_limit_bytes=32 * 1024 * 1024)
PRE_PARAMS = pltpu.CompilerParams(vmem_limit_bytes=60 * 1024 * 1024)


def places():
    near = lax.axis_index("near") * PAIR + lax.axis_index("side")
    return lax.axis_index("far") * PAIR * PAIR + near, near, lax.axis_index("key")


def fetch(pairs, sems):
    copies = [pltpu.make_async_copy(ref, buffer, sems.at[i]) for i, (ref, buffer) in enumerate(pairs)]
    for copy in copies:
        copy.start()
    for copy in copies:
        copy.wait()


def slab_kernel(bias, *slabs):
    near = places()[1]
    for s in range(4):
        slabs[s][...] = bias[near ^ s]


def make_slabs(bias):
    return pl.pallas_call(
        slab_kernel,
        out_shape=[jax.ShapeDtypeStruct(bias.shape[1:], jnp.bfloat16)] * 4,
        compiler_params=PARAMS,
        name="bias_by_head",
    )(bias)


def pack_kernel(*refs):
    inputs, packs, kept, buffers, (sems, held) = refs[:5], refs[5:8], refs[8:10], refs[10:15], refs[15:]
    fetch(list(zip(inputs, buffers)), sems)
    query, keys, values, gate, cot = buffers
    rows = query.shape[0]
    size = query.shape[2] // 4
    _, near, core = places()
    for r in range(rows):
        upstream = (cot[r].astype(jnp.float32) * jax.nn.sigmoid(gate[r].astype(jnp.float32))).astype(jnp.bfloat16)
        whole = [query[r], keys[r], values[r], upstream]
        for head in range(4):
            held[head, r] = jnp.concatenate([one[:, head * size : (head + 1) * size] for one in whole], axis=1)
    for i in range(2):
        for s in range(1, 4):
            packs[s - 1][i] = held[near ^ s, core ^ i]
        kept[i][...] = held[near, core ^ i]


def make_packs(*inputs):
    one = inputs[0]
    return pl.pallas_call(
        pack_kernel,
        in_specs=[pl.BlockSpec(memory_space=pl.ANY)] * 5,
        out_shape=[jax.ShapeDtypeStruct(one.shape, jnp.bfloat16)] * 3
        + [jax.ShapeDtypeStruct(one.shape[1:], jnp.bfloat16)] * 2,
        scratch_shapes=[VMEM(one.shape, jnp.bfloat16)] * 5
        + [pltpu.SemaphoreType.DMA((5,)), VMEM((4,) + one.shape, jnp.bfloat16)],
        compiler_params=PRE_PARAMS,
        name="pack",
    )(*inputs)


NT = (((1,), (1,)), ((), ()))


def dot(a, b, dims=(((1,), (0,)), ((), ()))):
    return lax.dot_general(a, b, dims, preferred_element_type=jnp.float32)


def main_kernel(scaling, size, first, final, start, relative, *refs):
    packs, swapped, (mine, other), refs = refs[0], refs[1], refs[2:4], refs[4:]
    earlier, refs = refs[: 0 if first else 4], refs[0 if first else 4 :]
    (d_mine, d_other), refs = refs[:2], refs[2:]
    results, refs = refs[: 5 if final else 4], refs[5 if final else 4 :]
    held, q_all, d_all, k_of, v_of, dk_t, dv_t, att_all, dq_all, bias_wide, q_now, d_now, back, s_now, p_now, low_now, d_low_now, bias_sum = refs
    step = pl.program_id(0)
    chip, near, core = places()
    _, half, lanes = held.shape
    parts = lanes // size
    blocks, own, _ = mine.shape

    def lanes_of(index, j):
        return jnp.concatenate([held[2 * p + index, :, j * size : (j + 1) * size] for p in range(parts)], axis=1)

    @pl.when(step == 0)
    def _():
        for s in range(4):
            held[(near ^ s) * 2 + core] = packs[s]
            held[(near ^ s) * 2 + 1 - core] = swapped[s]
        lane = lax.broadcasted_iota(jnp.int32, (half, lanes), 1) // size
        for c in range(2):
            rows = slice(c * half, (c + 1) * half)
            q_all[rows], d_all[rows] = lanes_of(c, 0), lanes_of(c, 3)
            k, v = lanes_of(core ^ c, 1), lanes_of(core ^ c, 2)
            for r in range(parts):
                k_of[r, rows] = jnp.where(lane == r, k, 0)
                v_of[r, rows] = jnp.where(lane == r, v, 0)
        for ref, value in zip((att_all, dq_all, dk_t, dv_t), earlier):
            ref[...] = value[...]
        if first:
            for ref in (att_all, dq_all, dk_t, dv_t):
                ref[...] = jnp.zeros_like(ref)

    def strip(i):
        at = start + step * blocks + i
        at = chip ^ at if relative else at
        return pl.ds(pl.multiple_of(at * own, own), own)

    for i in range(blocks):
        rows = slice(i * own, (i + 1) * own)
        bias_wide[rows, :half] = mine[i].astype(jnp.float32)
        bias_wide[rows, half:] = other[i].astype(jnp.float32)
        q_now[rows], d_now[rows] = q_all[strip(i)], d_all[strip(i)]
    q, d = q_now[...], d_now[...]
    q_t = q.astype(jnp.float32).T.astype(jnp.bfloat16)
    d_t = d.astype(jnp.float32).T.astype(jnp.bfloat16)

    def scores(r):
        s_now[r % 2] = dot(q, k_of[r], NT)
        p_now[r % 2] = dot(d, v_of[r], NT)

    att_sum, dq_sum = None, None
    scores(0)
    for r in range(parts):
        if r + 1 < parts:
            scores(r + 1)
        for at in range(0, blocks * own, ROWS_AT_ONCE):
            rows = slice(at, at + ROWS_AT_ONCE)
            logits = s_now[r % 2, rows] * scaling + bias_wide[rows]
            expo = jnp.exp(logits - jnp.max(logits, axis=-1, keepdims=True))
            probs = expo * (1.0 / jnp.sum(expo, axis=-1, keepdims=True))
            d_probs = p_now[r % 2, rows]
            inner = jnp.sum(probs * d_probs, axis=-1, keepdims=True)
            d_logits = probs * (d_probs - inner)
            low_now[r % 2, rows] = probs.astype(jnp.bfloat16)
            d_low_now[r % 2, rows] = d_logits.astype(jnp.bfloat16)
            bias_sum[rows] = d_logits if r == 0 else bias_sum[rows] + d_logits
        low, d_low = low_now[r % 2], d_low_now[r % 2]
        att, dq = dot(low, v_of[r]), dot(d_low, k_of[r])
        cut = slice(r * size, (r + 1) * size)
        dk_t[cut] += dot(q_t[cut], d_low)
        dv_t[cut] += dot(d_t[cut], low)
        att_sum = att if r == 0 else att_sum + att
        dq_sum = dq if r == 0 else dq_sum + dq
    att_low, dq_low = att_sum.astype(jnp.bfloat16), (dq_sum * scaling).astype(jnp.bfloat16)
    for i in range(blocks):
        rows = slice(i * own, (i + 1) * own)
        att_all[strip(i)], dq_all[strip(i)] = att_low[rows], dq_low[rows]
        d_mine[i] = bias_sum[rows, :half].astype(jnp.bfloat16)
        d_other[i] = bias_sum[rows, half:].astype(jnp.bfloat16)

    @pl.when(step == pl.num_programs(0) - 1)
    def _():
        if not final:
            for ref, value in zip(results, (att_all, dq_all, dk_t, dv_t)):
                ref[...] = value[...]
            return
        dk = (dk_t[...] * scaling).T.astype(jnp.bfloat16)
        dv = dv_t[...].T.astype(jnp.bfloat16)
        for c in range(2):
            back[0, c], back[1, c] = dk[c * half : (c + 1) * half], dv[c * half : (c + 1) * half]
        for c in range(2):
            rows = slice(c * half, (c + 1) * half)
            whole = [att_all[rows], dq_all[rows], back[0, core ^ c], back[1, core ^ c]]
            for p in range(parts):
                cut = slice(p * size, (p + 1) * size)
                held[2 * p + c] = jnp.concatenate([one[:, cut] for one in whole], axis=1)
        for i in range(2):
            for s in range(1, 4):
                results[s - 1][i] = held[(near ^ s) * 2 + (core ^ i)]
            results[3 + i][...] = held[near * 2 + (core ^ i)]


def fixed(value):
    return pl.BlockSpec(value.shape, lambda i: (0,) * len(value.shape))


def main(packs, swapped, mine, other, earlier, scaling, size, blocks, final, start, relative):
    _, half, lanes = swapped.shape
    strips, own, _ = mine.shape
    key_count = queries = 2 * half
    rows = jax.ShapeDtypeStruct((queries, lanes), jnp.bfloat16)
    turned = jax.ShapeDtypeStruct((lanes, key_count), jnp.float32)
    strip = pl.BlockSpec((blocks, own, half), lambda i: (i, 0, 0))
    now = VMEM((blocks * own, lanes), jnp.bfloat16)

    results = [rows, rows, turned, turned]
    if final:
        results = [jax.ShapeDtypeStruct((2, half, lanes), jnp.bfloat16)] * 3
        results += [jax.ShapeDtypeStruct((half, lanes), jnp.bfloat16)] * 2
    elements = strips * own * key_count * (lanes // size)
    return pl.pallas_call(
        functools.partial(main_kernel, scaling, size, not earlier, final, start, relative),
        grid=(strips // blocks,),
        in_specs=[fixed(packs), fixed(swapped), strip, strip] + [fixed(one) for one in earlier],
        out_specs=[strip, strip] + [fixed(one) for one in results],
        out_shape=[jax.ShapeDtypeStruct(one.shape, one.dtype) for one in [mine, other] + results],
        scratch_shapes=[
            VMEM((8, half, lanes), jnp.bfloat16),
            VMEM(rows.shape, jnp.bfloat16),
            VMEM(rows.shape, jnp.bfloat16),
            VMEM((lanes // size, key_count, lanes), jnp.bfloat16),
            VMEM((lanes // size, key_count, lanes), jnp.bfloat16),
            VMEM(turned.shape, jnp.float32),
            VMEM(turned.shape, jnp.float32),
            VMEM(rows.shape, jnp.bfloat16),
            VMEM(rows.shape, jnp.bfloat16),
            VMEM((blocks * own, key_count), jnp.float32),
            now,
            now,
            VMEM((2, 2, half, lanes), jnp.bfloat16),
            VMEM((2, blocks * own, key_count), jnp.float32),
            VMEM((2, blocks * own, key_count), jnp.float32),
            VMEM((2, blocks * own, key_count), jnp.bfloat16),
            VMEM((2, blocks * own, key_count), jnp.bfloat16),
            VMEM((blocks * own, key_count), jnp.float32),
        ],
        compiler_params=PARAMS,
        cost_estimate=pl.CostEstimate(
            flops=1, bytes_accessed=1, transcendentals=0
        ),
        name="attention",
    )(packs, swapped, mine, other, *earlier)


def post_kernel(gate, cot, packs, swapped, d_query, d_keys, d_values, d_gate, held):
    rows, half, channels = gate.shape
    size = channels // 4
    _, near, core = places()
    for s in range(4):
        held[near ^ s, core] = packs[s]
        held[near ^ s, 1 - core] = swapped[s]
    for r in range(rows):
        full = []
        for j in range(4):
            full.append(jnp.concatenate([held[h, r, :, j * size : (j + 1) * size] for h in range(4)], axis=1))
        d_query[r], d_keys[r], d_values[r] = full[1], full[2], full[3]
        sig = jax.nn.sigmoid(gate[r].astype(jnp.float32))
        d_gate[r] = (cot[r].astype(jnp.float32) * full[0].astype(jnp.float32) * sig * (1.0 - sig)).astype(jnp.bfloat16)


def post(gate, cot, packs, swapped):
    return pl.pallas_call(
        post_kernel,
        out_shape=[jax.ShapeDtypeStruct(gate.shape, jnp.bfloat16)] * 4,
        scratch_shapes=[VMEM((4,) + gate.shape, jnp.bfloat16)],
        compiler_params=PARAMS,
        name="unpack",
    )(gate, cot, packs, swapped)


def bias_kernel(*refs):
    near = places()[1]
    for s in range(4):
        refs[4][near ^ s] = refs[s][...].astype(jnp.float32)


def bias_out(pieces):
    return pl.pallas_call(
        bias_kernel,
        out_shape=jax.ShapeDtypeStruct((4,) + pieces[0].shape, jnp.float32),
        compiler_params=PARAMS,
        name="bias_grad",
    )(*pieces)


def shards(query, keys, values, gate_logits, pair_bias, key_mask, grad_out):
    rows, half, channels = query.shape
    heads, own, _ = pair_bias.shape
    size = channels // heads
    scaling = 1.0 / math.sqrt(size)
    far, cores = lax.axis_size("far"), lax.axis_size("key")
    chips = far * PAIR * PAIR
    assert PAIR * PAIR == heads == 4 and rows == cores == 2
    relative = own % 16 == 0
    chip = places()[0]

    def swap(value, axes, s, count):
        return lax.ppermute(value, axes, [(i, i ^ s) for i in range(count)]) if s else value

    def near_swap(value, s):
        return swap(value, ("near", "side"), s, 4)

    def far_swap(value, s):
        return swap(value, "far", s, far)

    def other_core(value):
        return swap(value, "key", 1, 2)

    def wide(value):
        return value.astype(jnp.float32)

    slabs = make_slabs(pair_bias)
    strips = jnp.stack([near_swap(slabs[s], s) for s in range(4)])
    strips = jnp.where(key_mask == 1, strips, jnp.bfloat16(-1000000000.0))
    groups = [far_swap(strips, f) for f in range(far)]
    *packs, kept, spare = make_packs(query, keys, values, gate_logits, grad_out)
    packs = [near_swap(packs[s], s + 1) for s in range(3)]
    swapped = other_core(jnp.stack([spare] + [pack[1] for pack in packs]))
    packs = jnp.stack([kept] + [pack[0] for pack in packs])
    calls = [(f * 4, groups[f]) for f in range(1, far)] + [(0, groups[0])]
    if not relative:
        strips = jnp.concatenate(groups)[chip ^ jnp.arange(chips)]
        calls = [(0, strips.reshape(8, -1, half))]
    earlier, sums, d_sum = [], {}, None
    for start, mine in calls:
        other = other_core(mine)
        if d_sum is not None:
            mine, d_sum = lax.optimization_barrier((mine, d_sum))
            sums[last] = d_sum
        final = start == calls[-1][0]
        d_mine, d_other, *earlier = main(
            packs, swapped, mine, other, earlier, scaling, size, 4, final, start, relative
        )
        if final and relative:
            d_mine = wide(d_mine)
            for f in range(1, far):
                d_mine = d_mine + wide(far_swap(sums[f * 4], f))
            d_mine = lax.optimization_barrier(d_mine)
        d_sum = (wide(d_mine) + wide(other_core(d_other))).astype(jnp.bfloat16)
        sums[start], last = d_sum, start
    if not relative:
        d_sum = sums[0].reshape(chips, own, half)[chip ^ jnp.arange(chips)]
        sums = {f * 4: d_sum[f * 4 : f * 4 + 4] for f in range(far)}
        total = wide(sums[0])
        for f in range(1, far):
            total = total + wide(far_swap(sums[f * 4], f))
        d_sum = total.astype(jnp.bfloat16)
    pieces = [near_swap(d_sum[s], s) for s in range(4)]
    packs = [near_swap(earlier[s], s + 1) for s in range(3)]
    packs = lax.optimization_barrier((*packs, *pieces))[:3]
    swapped = other_core(jnp.stack([earlier[4]] + [pack[1] for pack in packs]))
    packs = jnp.stack([earlier[3]] + [pack[0] for pack in packs])
    return (*post(gate_logits, grad_out, packs, swapped), bias_out(pieces))


def solution(mesh):
    groups, rows, cores = mesh.devices.shape
    devices = mesh.devices.reshape(groups, rows // PAIR**2, PAIR, PAIR, cores)
    mesh = jax.sharding.Mesh(devices, ("grp", "far", "near", "side", "key"))
    split = ("grp", "far", "near", "side")
    tokens = P(split, "key", None)
    pair = P(None, split, "key")
    in_specs = (tokens, tokens, tokens, tokens, pair, P(("grp", "key")), tokens)
    out_specs = (tokens, tokens, tokens, tokens, pair)
    return jax.shard_map(shards, mesh=mesh, in_specs=in_specs, out_specs=out_specs, check_vma=False)
```

```python
import functools
import math

import jax
import jax.numpy as jnp
from jax import lax
from jax.experimental import pallas as pl
from jax.experimental.pallas import tpu as pltpu
from jax.sharding import PartitionSpec as P

PAIR = 2
ROWS_AT_ONCE = 16
SENT = (2, 3, 1)
VMEM = pltpu.VMEM
PARAMS = pltpu.CompilerParams(vmem_limit_bytes=32 * 1024 * 1024)
PRE_PARAMS = pltpu.CompilerParams(vmem_limit_bytes=60 * 1024 * 1024)


def places():
    near = lax.axis_index("near") * PAIR + lax.axis_index("side")
    return lax.axis_index("far") * PAIR * PAIR + near, near, lax.axis_index("key")


def fetch(pairs, sems):
    copies = [pltpu.make_async_copy(ref, buffer, sems.at[i]) for i, (ref, buffer) in enumerate(pairs)]
    for copy in copies:
        copy.start()
    for copy in copies:
        copy.wait()


def slab_kernel(bias, *slabs):
    near = places()[1]
    for s in range(4):
        slabs[s][...] = bias[near ^ s]


def make_slabs(bias):
    return pl.pallas_call(
        slab_kernel,
        out_shape=[jax.ShapeDtypeStruct(bias.shape[1:], jnp.bfloat16)] * 4,
        compiler_params=PARAMS,
        name="bias_by_head",
    )(bias)


def pack_kernel(*refs):
    inputs, packs, kept, buffers, (sems, held) = refs[:5], refs[5:8], refs[8:10], refs[10:15], refs[15:]
    fetch(list(zip(inputs, buffers)), sems)
    query, keys, values, gate, cot = buffers
    rows = query.shape[0]
    size = query.shape[2] // 4
    _, near, core = places()
    for r in range(rows):
        upstream = (cot[r].astype(jnp.float32) * jax.nn.sigmoid(gate[r].astype(jnp.float32))).astype(jnp.bfloat16)
        whole = [query[r], keys[r], values[r], upstream]
        for head in range(4):
            held[head, r] = jnp.concatenate([one[:, head * size : (head + 1) * size] for one in whole], axis=1)
    for i in range(2):
        for s in range(1, 4):
            packs[s - 1][i] = held[near ^ s, core ^ i]
        kept[i][...] = held[near, core ^ i]


def make_packs(*inputs):
    one = inputs[0]
    return pl.pallas_call(
        pack_kernel,
        in_specs=[pl.BlockSpec(memory_space=pl.ANY)] * 5,
        out_shape=[jax.ShapeDtypeStruct(one.shape, jnp.bfloat16)] * 3
        + [jax.ShapeDtypeStruct(one.shape[1:], jnp.bfloat16)] * 2,
        scratch_shapes=[VMEM(one.shape, jnp.bfloat16)] * 5
        + [pltpu.SemaphoreType.DMA((5,)), VMEM((4,) + one.shape, jnp.bfloat16)],
        compiler_params=PRE_PARAMS,
        name="pack",
    )(*inputs)


NT = (((1,), (1,)), ((), ()))


def dot(a, b, dims=(((1,), (0,)), ((), ()))):
    return lax.dot_general(a, b, dims, preferred_element_type=jnp.float32)


def main_kernel(scaling, size, first, final, start, relative, *refs):
    packs, swapped, (mine, other), refs = refs[0], refs[1], refs[2:4], refs[4:]
    earlier, refs = refs[: 0 if first else 4], refs[0 if first else 4 :]
    (d_mine, d_other), refs = refs[:2], refs[2:]
    results, refs = refs[: 5 if final else 4], refs[5 if final else 4 :]
    held, q_all, d_all, k_of, v_of, dk_t, dv_t, att_all, dq_all, bias_wide, q_now, d_now, back, s_now, p_now, low_now, d_low_now, bias_sum = refs
    step = pl.program_id(0)
    chip, near, core = places()
    _, half, lanes = held.shape
    parts = lanes // size
    blocks, own, _ = mine.shape

    def lanes_of(index, j):
        return jnp.concatenate([held[2 * p + index, :, j * size : (j + 1) * size] for p in range(parts)], axis=1)

    @pl.when(step == 0)
    def _():
        for i, s in enumerate((0, *SENT)):
            held[(near ^ s) * 2 + core] = packs[i]
            held[(near ^ s) * 2 + 1 - core] = swapped[i]
        lane = lax.broadcasted_iota(jnp.int32, (half, lanes), 1) // size
        for c in range(2):
            rows = slice(c * half, (c + 1) * half)
            q_all[rows], d_all[rows] = lanes_of(c, 0), lanes_of(c, 3)
            k, v = lanes_of(core ^ c, 1), lanes_of(core ^ c, 2)
            for r in range(parts):
                k_of[r, rows] = jnp.where(lane == r, k, 0)
                v_of[r, rows] = jnp.where(lane == r, v, 0)
        for ref, value in zip((att_all, dq_all, dk_t, dv_t), earlier):
            ref[...] = value[...]
        if first:
            for ref in (att_all, dq_all, dk_t, dv_t):
                ref[...] = jnp.zeros_like(ref)

    def strip(i):
        at = start + step * blocks + i
        at = chip ^ at if relative else at
        return pl.ds(pl.multiple_of(at * own, own), own)

    for i in range(blocks):
        rows = slice(i * own, (i + 1) * own)
        bias_wide[rows, :half] = mine[i].astype(jnp.float32)
        bias_wide[rows, half:] = other[i].astype(jnp.float32)
        q_now[rows], d_now[rows] = q_all[strip(i)], d_all[strip(i)]
    q, d = q_now[...], d_now[...]
    q_t = q.astype(jnp.float32).T.astype(jnp.bfloat16)
    d_t = d.astype(jnp.float32).T.astype(jnp.bfloat16)

    def scores(r):
        s_now[r % 2] = dot(q, k_of[r], NT)
        p_now[r % 2] = dot(d, v_of[r], NT)

    att_sum, dq_sum = None, None
    scores(0)
    for r in range(parts):
        if r + 1 < parts:
            scores(r + 1)
        for at in range(0, blocks * own, ROWS_AT_ONCE):
            rows = slice(at, at + ROWS_AT_ONCE)
            logits = s_now[r % 2, rows] * scaling + bias_wide[rows]
            expo = jnp.exp(logits - jnp.max(logits, axis=-1, keepdims=True))
            d_probs = p_now[r % 2, rows]
            inverse = 1.0 / jnp.sum(expo, axis=-1, keepdims=True)
            inner = jnp.sum(expo * d_probs, axis=-1, keepdims=True) * inverse
            probs = expo * inverse
            d_logits = probs * (d_probs - inner)
            low_now[r % 2, rows] = probs.astype(jnp.bfloat16)
            d_low_now[r % 2, rows] = d_logits.astype(jnp.bfloat16)
            bias_sum[rows] = d_logits if r == 0 else bias_sum[rows] + d_logits
        low, d_low = low_now[r % 2], d_low_now[r % 2]
        att, dq = dot(low, v_of[r]), dot(d_low, k_of[r])
        cut = slice(r * size, (r + 1) * size)
        dk_t[cut] += dot(q_t[cut], d_low)
        dv_t[cut] += dot(d_t[cut], low)
        att_sum = att if r == 0 else att_sum + att
        dq_sum = dq if r == 0 else dq_sum + dq
    att_low, dq_low = att_sum.astype(jnp.bfloat16), (dq_sum * scaling).astype(jnp.bfloat16)
    for i in range(blocks):
        rows = slice(i * own, (i + 1) * own)
        att_all[strip(i)], dq_all[strip(i)] = att_low[rows], dq_low[rows]
        d_mine[i] = bias_sum[rows, :half].astype(jnp.bfloat16)
        d_other[i] = bias_sum[rows, half:].astype(jnp.bfloat16)

    @pl.when(step == pl.num_programs(0) - 1)
    def _():
        if not final:
            for ref, value in zip(results, (att_all, dq_all, dk_t, dv_t)):
                ref[...] = value[...]
            return
        dk = (dk_t[...] * scaling).T.astype(jnp.bfloat16)
        dv = dv_t[...].T.astype(jnp.bfloat16)
        for c in range(2):
            back[0, c], back[1, c] = dk[c * half : (c + 1) * half], dv[c * half : (c + 1) * half]
        for c in range(2):
            rows = slice(c * half, (c + 1) * half)
            whole = [att_all[rows], dq_all[rows], back[0, core ^ c], back[1, core ^ c]]
            for p in range(parts):
                cut = slice(p * size, (p + 1) * size)
                held[2 * p + c] = jnp.concatenate([one[:, cut] for one in whole], axis=1)
        for i in range(2):
            for s in range(1, 4):
                results[s - 1][i] = held[(near ^ s) * 2 + (core ^ i)]
            results[3 + i][...] = held[near * 2 + (core ^ i)]


def fixed(value):
    return pl.BlockSpec(value.shape, lambda i: (0,) * len(value.shape))


def main(packs, swapped, mine, other, earlier, scaling, size, blocks, final, start, relative):
    _, half, lanes = swapped.shape
    strips, own, _ = mine.shape
    key_count = queries = 2 * half
    rows = jax.ShapeDtypeStruct((queries, lanes), jnp.bfloat16)
    turned = jax.ShapeDtypeStruct((lanes, key_count), jnp.float32)
    strip = pl.BlockSpec((blocks, own, half), lambda i: (i, 0, 0))
    now = VMEM((blocks * own, lanes), jnp.bfloat16)

    results = [rows, rows, turned, turned]
    if final:
        results = [jax.ShapeDtypeStruct((2, half, lanes), jnp.bfloat16)] * 3
        results += [jax.ShapeDtypeStruct((half, lanes), jnp.bfloat16)] * 2
    elements = strips * own * key_count * (lanes // size)
    return pl.pallas_call(
        functools.partial(main_kernel, scaling, size, not earlier, final, start, relative),
        grid=(strips // blocks,),
        in_specs=[fixed(packs), fixed(swapped), strip, strip] + [fixed(one) for one in earlier],
        out_specs=[strip, strip] + [fixed(one) for one in results],
        out_shape=[jax.ShapeDtypeStruct(one.shape, one.dtype) for one in [mine, other] + results],
        scratch_shapes=[
            VMEM((8, half, lanes), jnp.bfloat16),
            VMEM(rows.shape, jnp.bfloat16),
            VMEM(rows.shape, jnp.bfloat16),
            VMEM((lanes // size, key_count, lanes), jnp.bfloat16),
            VMEM((lanes // size, key_count, lanes), jnp.bfloat16),
            VMEM(turned.shape, jnp.float32),
            VMEM(turned.shape, jnp.float32),
            VMEM(rows.shape, jnp.bfloat16),
            VMEM(rows.shape, jnp.bfloat16),
            VMEM((blocks * own, key_count), jnp.float32),
            now,
            now,
            VMEM((2, 2, half, lanes), jnp.bfloat16),
            VMEM((2, blocks * own, key_count), jnp.float32),
            VMEM((2, blocks * own, key_count), jnp.float32),
            VMEM((2, blocks * own, key_count), jnp.bfloat16),
            VMEM((2, blocks * own, key_count), jnp.bfloat16),
            VMEM((blocks * own, key_count), jnp.float32),
        ],
        compiler_params=PARAMS,
        cost_estimate=pl.CostEstimate(
            flops=1, bytes_accessed=1, transcendentals=0
        ),
        name="attention",
    )(packs, swapped, mine, other, *earlier)


def post_kernel(gate, cot, packs, swapped, d_query, d_keys, d_values, d_gate, held):
    rows, half, channels = gate.shape
    size = channels // 4
    _, near, core = places()
    for i, s in enumerate((0, *SENT)):
        held[near ^ s, core] = packs[i]
        held[near ^ s, 1 - core] = swapped[i]
    for r in range(rows):
        full = []
        for j in range(4):
            full.append(jnp.concatenate([held[h, r, :, j * size : (j + 1) * size] for h in range(4)], axis=1))
        d_query[r], d_keys[r], d_values[r] = full[1], full[2], full[3]
        sig = jax.nn.sigmoid(gate[r].astype(jnp.float32))
        d_gate[r] = (cot[r].astype(jnp.float32) * full[0].astype(jnp.float32) * sig * (1.0 - sig)).astype(jnp.bfloat16)


def post(gate, cot, packs, swapped):
    return pl.pallas_call(
        post_kernel,
        out_shape=[jax.ShapeDtypeStruct(gate.shape, jnp.bfloat16)] * 4,
        scratch_shapes=[VMEM((4,) + gate.shape, jnp.bfloat16)],
        compiler_params=PARAMS,
        name="unpack",
    )(gate, cot, packs, swapped)


def bias_kernel(*refs):
    near = places()[1]
    for s in range(4):
        refs[4][near ^ s] = refs[s][...].astype(jnp.float32)


def bias_out(pieces):
    return pl.pallas_call(
        bias_kernel,
        out_shape=jax.ShapeDtypeStruct((4,) + pieces[0].shape, jnp.float32),
        compiler_params=PARAMS,
        name="bias_grad",
    )(*pieces)


def shards(query, keys, values, gate_logits, pair_bias, key_mask, grad_out):
    rows, half, channels = query.shape
    heads, own, _ = pair_bias.shape
    size = channels // heads
    scaling = 1.0 / math.sqrt(size)
    far, cores = lax.axis_size("far"), lax.axis_size("key")
    chips = far * PAIR * PAIR
    assert PAIR * PAIR == heads == 4 and rows == cores == 2
    relative = own % 16 == 0
    chip = places()[0]

    def swap(value, axes, s, count):
        return lax.ppermute(value, axes, [(i, i ^ s) for i in range(count)]) if s else value

    def near_swap(value, s):
        return swap(value, ("near", "side"), s, 4)

    def far_swap(value, s):
        return swap(value, "far", s, far)

    def other_core(value):
        return swap(value, "key", 1, 2)

    def wide(value):
        return value.astype(jnp.float32)

    slabs = make_slabs(pair_bias)
    strips = jnp.stack([near_swap(slabs[s], s) for s in range(4)])
    strips = jnp.where(key_mask == 1, strips, jnp.bfloat16(-1000000000.0))
    groups = [far_swap(strips, f) for f in range(far)]
    *packs, kept, spare = make_packs(query, keys, values, gate_logits, grad_out)
    packs = [near_swap(packs[s - 1], s) for s in SENT]
    swapped = other_core(jnp.stack([spare] + [pack[1] for pack in packs]))
    packs = jnp.stack([kept] + [pack[0] for pack in packs])
    calls = [(f * 4, groups[f]) for f in range(1, far)] + [(0, groups[0])]
    if not relative:
        strips = jnp.concatenate(groups)[chip ^ jnp.arange(chips)]
        calls = [(0, strips.reshape(8, -1, half))]
    earlier, sums, d_sum = [], {}, None
    others = [other_core(mine) for _, mine in calls]
    calls[0] = (calls[0][0], lax.optimization_barrier((calls[0][1], others[-1]))[0])
    for (start, mine), other in zip(calls, others):
        if d_sum is not None:
            mine, d_sum = lax.optimization_barrier((mine, d_sum))
            sums[last] = d_sum
        final = start == calls[-1][0]
        d_mine, d_other, *earlier = main(
            packs, swapped, mine, other, earlier, scaling, size, 4, final, start, relative
        )
        if final and relative:
            d_mine = wide(d_mine)
            for f in range(1, far):
                d_mine = d_mine + wide(far_swap(sums[f * 4], f))
            d_mine = lax.optimization_barrier(d_mine)
        d_sum = (wide(d_mine) + wide(other_core(d_other))).astype(jnp.bfloat16)
        sums[start], last = d_sum, start
    if not relative:
        d_sum = sums[0].reshape(chips, own, half)[chip ^ jnp.arange(chips)]
        sums = {f * 4: d_sum[f * 4 : f * 4 + 4] for f in range(far)}
        total = wide(sums[0])
        for f in range(1, far):
            total = total + wide(far_swap(sums[f * 4], f))
        d_sum = total.astype(jnp.bfloat16)
    pieces = [near_swap(d_sum[s], s) for s in range(4)]
    packs = [near_swap(earlier[s - 1], s) for s in SENT]
    packs = lax.optimization_barrier((*packs, *pieces))[:3]
    swapped = other_core(jnp.stack([earlier[4]] + [pack[1] for pack in packs]))
    packs = jnp.stack([earlier[3]] + [pack[0] for pack in packs])
    return (*post(gate_logits, grad_out, packs, swapped), bias_out(pieces))


def solution(mesh):
    groups, rows, cores = mesh.devices.shape
    devices = mesh.devices.reshape(groups, rows // PAIR**2, PAIR, PAIR, cores)
    mesh = jax.sharding.Mesh(devices, ("grp", "far", "near", "side", "key"))
    split = ("grp", "far", "near", "side")
    tokens = P(split, "key", None)
    pair = P(None, split, "key")
    in_specs = (tokens, tokens, tokens, tokens, pair, P(("grp", "key")), tokens)
    out_specs = (tokens, tokens, tokens, tokens, pair)
    return jax.shard_map(shards, mesh=mesh, in_specs=in_specs, out_specs=out_specs, check_vma=False)
```

```python
import functools
import math

import jax
import jax.numpy as jnp
from jax import lax
from jax.experimental import pallas as pl
from jax.experimental.pallas import tpu as pltpu
from jax.sharding import PartitionSpec as P

PAIR = 2
NEAR_PARTS = 2
ROWS_AT_ONCE = 16
VMEM = pltpu.VMEM
PARAMS = pltpu.CompilerParams(vmem_limit_bytes=32 * 1024 * 1024)
PRE_PARAMS = pltpu.CompilerParams(vmem_limit_bytes=60 * 1024 * 1024)


def places():
    near = lax.axis_index("near") * PAIR + lax.axis_index("side")
    return lax.axis_index("far") * PAIR * PAIR + near, near, lax.axis_index("key")


def fetch(pairs, sems):
    copies = [pltpu.make_async_copy(ref, buffer, sems.at[i]) for i, (ref, buffer) in enumerate(pairs)]
    for copy in copies:
        copy.start()
    for copy in copies:
        copy.wait()


def slab_kernel(bias, *slabs):
    near = places()[1]
    for s in range(4):
        slabs[s][...] = bias[near ^ s]


def make_slabs(bias):
    return pl.pallas_call(
        slab_kernel,
        out_shape=[jax.ShapeDtypeStruct(bias.shape[1:], jnp.bfloat16)] * 4,
        compiler_params=PARAMS,
        name="bias_by_head",
    )(bias)


def pack_kernel(*refs):
    inputs, packs, kept, buffers, (sems, held) = refs[:5], refs[5:8], refs[8:10], refs[10:15], refs[15:]
    fetch(list(zip(inputs, buffers)), sems)
    query, keys, values, gate, cot = buffers
    rows = query.shape[0]
    size = query.shape[2] // 4
    _, near, core = places()
    for r in range(rows):
        upstream = (cot[r].astype(jnp.float32) * jax.nn.sigmoid(gate[r].astype(jnp.float32))).astype(jnp.bfloat16)
        whole = [query[r], keys[r], values[r], upstream]
        for head in range(4):
            held[head, r] = jnp.concatenate([one[:, head * size : (head + 1) * size] for one in whole], axis=1)
    for i in range(2):
        for s in range(1, 4):
            packs[s - 1][i] = held[near ^ s, core ^ i]
        kept[i][...] = held[near, core ^ i]


def make_packs(*inputs):
    one = inputs[0]
    return pl.pallas_call(
        pack_kernel,
        in_specs=[pl.BlockSpec(memory_space=pl.ANY)] * 5,
        out_shape=[jax.ShapeDtypeStruct(one.shape, jnp.bfloat16)] * 3
        + [jax.ShapeDtypeStruct(one.shape[1:], jnp.bfloat16)] * 2,
        scratch_shapes=[VMEM(one.shape, jnp.bfloat16)] * 5
        + [pltpu.SemaphoreType.DMA((5,)), VMEM((4,) + one.shape, jnp.bfloat16)],
        compiler_params=PRE_PARAMS,
        name="pack",
    )(*inputs)


NT = (((1,), (1,)), ((), ()))


def dot(a, b, dims=(((1,), (0,)), ((), ()))):
    return lax.dot_general(a, b, dims, preferred_element_type=jnp.float32)


def main_kernel(scaling, size, start, relative, begun, ended, opened, closed, split, *refs):
    packs, swapped, (mine, other), refs = refs[:2], refs[2:4], refs[4:6], refs[6:]
    earlier, refs = refs[: 4 if begun else 0], refs[4 if begun else 0 :]
    before, refs = refs[: 1 if opened else 0], refs[1 if opened else 0 :]
    d_bias, refs = refs[: 2 if closed else 1], refs[2 if closed else 1 :]
    results, refs = refs[: 2 + split if ended else 4], refs[2 + split if ended else 4 :]
    q_all, d_all, k_of, v_of, dk_t, dv_t, att_all, dq_all, bias_wide, q_now, d_now, s_now, p_now, low_now, d_low_now, bias_sum = refs
    step = pl.program_id(0)
    chip, _, core = places()
    parts, (half, _) = len(packs), packs[0].shape
    blocks, own, _ = mine.shape
    lanes = parts * size

    def side(i):
        return pl.ds(pl.multiple_of((core ^ i) * half, half), half)

    @pl.when(step == 0)
    def _():
        lane = lax.broadcasted_iota(jnp.int32, (half, lanes), 1) // size
        for i in range(2):
            here = [(swapped if i else packs)[p][...] for p in range(parts)]
            q, k, v, d = [
                jnp.concatenate([one[:, j * size : (j + 1) * size] for one in here], axis=1) for j in range(4)
            ]
            q_all[side(i)], d_all[side(i)] = q, d
            rows = slice(i * half, (i + 1) * half)
            for r in range(parts):
                k_of[r, rows] = jnp.where(lane == r, k, 0)
                v_of[r, rows] = jnp.where(lane == r, v, 0)
        for i, ref in enumerate((att_all, dq_all, dk_t, dv_t)):
            ref[...] = earlier[i][...] if begun else jnp.zeros_like(ref)

    def strip(i):
        at = start + step * blocks + i
        at = chip ^ at if relative else at
        return pl.ds(pl.multiple_of(at * own, own), own)

    for i in range(blocks):
        rows = slice(i * own, (i + 1) * own)
        bias_wide[rows, :half] = mine[i].astype(jnp.float32)
        bias_wide[rows, half:] = other[i].astype(jnp.float32)
        q_now[rows], d_now[rows] = q_all[strip(i)], d_all[strip(i)]
    q, d = q_now[...], d_now[...]
    q_t = q.astype(jnp.float32).T.astype(jnp.bfloat16)
    d_t = d.astype(jnp.float32).T.astype(jnp.bfloat16)

    def scores(r):
        s_now[r % 2] = dot(q, k_of[r], NT)
        p_now[r % 2] = dot(d, v_of[r], NT)

    att_sum, dq_sum = None, None
    scores(0)
    for r in range(parts):
        if r + 1 < parts:
            scores(r + 1)
        for at in range(0, blocks * own, ROWS_AT_ONCE):
            rows = slice(at, at + ROWS_AT_ONCE)
            logits = s_now[r % 2, rows] * scaling + bias_wide[rows]
            expo = jnp.exp(logits - jnp.max(logits, axis=-1, keepdims=True))
            probs = expo * (1.0 / jnp.sum(expo, axis=-1, keepdims=True))
            d_probs = p_now[r % 2, rows]
            inner = jnp.sum(probs * d_probs, axis=-1, keepdims=True)
            d_logits = probs * (d_probs - inner)
            low_now[r % 2, rows] = probs.astype(jnp.bfloat16)
            d_low_now[r % 2, rows] = d_logits.astype(jnp.bfloat16)
            if r:
                d_logits = bias_sum[rows] + d_logits
            elif opened:
                d_logits = before[0][rows] + d_logits
            bias_sum[rows] = d_logits
        low, d_low = low_now[r % 2], d_low_now[r % 2]
        att, dq = dot(low, v_of[r]), dot(d_low, k_of[r])
        cut = slice(r * size, (r + 1) * size)
        dk_t[cut] += dot(q_t[cut], d_low)
        dv_t[cut] += dot(d_t[cut], low)
        att_sum = att if r == 0 else att_sum + att
        dq_sum = dq if r == 0 else dq_sum + dq
    att_low, dq_low = att_sum.astype(jnp.bfloat16), (dq_sum * scaling).astype(jnp.bfloat16)
    for i in range(blocks):
        rows = slice(i * own, (i + 1) * own)
        att_all[strip(i)], dq_all[strip(i)] = att_low[rows], dq_low[rows]
        if closed:
            d_bias[0][i] = bias_sum[rows, :half].astype(jnp.bfloat16)
            d_bias[1][i] = bias_sum[rows, half:].astype(jnp.bfloat16)
    if not closed:
        d_bias[0][...] = bias_sum[...]

    @pl.when(step == pl.num_programs(0) - 1)
    def _():
        if not ended:
            for ref, value in zip(results, (att_all, dq_all, dk_t, dv_t)):
                ref[...] = value[...]
            return
        dk = (dk_t[...] * scaling).T.astype(jnp.bfloat16)
        dv = dv_t[...].T.astype(jnp.bfloat16)
        for i in range(2):
            rows = slice(i * half, (i + 1) * half)
            whole = [att_all[side(i)], dq_all[side(i)], dk[rows], dv[rows]]
            for p in range(parts):
                pack = jnp.concatenate([one[:, p * size : (p + 1) * size] for one in whole], axis=1)
                if split and p == 0:
                    results[i][...] = pack
                else:
                    results[p + split][i] = pack


def fixed(value):
    return pl.BlockSpec(value.shape, lambda i: (0,) * len(value.shape))


def main(packs, swapped, mine, other, earlier, before, scaling, size, start, relative, ended, closed, split):
    parts, (half, width) = len(packs), swapped[0].shape
    strips, own, _ = mine.shape
    blocks, lanes = 4, parts * size
    key_count = queries = 2 * half
    rows = jax.ShapeDtypeStruct((queries, lanes), jnp.bfloat16)
    turned = jax.ShapeDtypeStruct((lanes, key_count), jnp.float32)
    wide = jax.ShapeDtypeStruct((strips * own, key_count), jnp.float32)
    strip = pl.BlockSpec((blocks, own, half), lambda i: (i, 0, 0))
    wide_strip = pl.BlockSpec((blocks * own, key_count), lambda i: (i, 0))
    now = VMEM((blocks * own, lanes), jnp.bfloat16)
    results = [rows, rows, turned, turned]
    if ended:
        ours = [jax.ShapeDtypeStruct((half, width), jnp.bfloat16)] * 2
        results = [jax.ShapeDtypeStruct((2, half, width), jnp.bfloat16)] * (parts - split)
        results = ours * split + results
    d_bias = [mine, other] if closed else [wide]
    return pl.pallas_call(
        functools.partial(main_kernel, scaling, size, start, relative, bool(earlier), ended, bool(before), closed, split),
        grid=(strips // blocks,),
        in_specs=[fixed(one) for one in [*packs, *swapped]]
        + [strip, strip]
        + [fixed(one) for one in earlier]
        + [wide_strip] * len(before),
        out_specs=([strip] * 2 if closed else [wide_strip]) + [fixed(one) for one in results],
        out_shape=[jax.ShapeDtypeStruct(one.shape, one.dtype) for one in d_bias + results],
        scratch_shapes=[
            VMEM(rows.shape, jnp.bfloat16),
            VMEM(rows.shape, jnp.bfloat16),
            VMEM((parts, key_count, lanes), jnp.bfloat16),
            VMEM((parts, key_count, lanes), jnp.bfloat16),
            VMEM(turned.shape, jnp.float32),
            VMEM(turned.shape, jnp.float32),
            VMEM(rows.shape, jnp.bfloat16),
            VMEM(rows.shape, jnp.bfloat16),
            VMEM((blocks * own, key_count), jnp.float32),
            now,
            now,
            VMEM((2, blocks * own, key_count), jnp.float32),
            VMEM((2, blocks * own, key_count), jnp.float32),
            VMEM((2, blocks * own, key_count), jnp.bfloat16),
            VMEM((2, blocks * own, key_count), jnp.bfloat16),
            VMEM((blocks * own, key_count), jnp.float32),
        ],
        compiler_params=PARAMS,
        cost_estimate=pl.CostEstimate(flops=1, bytes_accessed=1, transcendentals=0),
        name="attention",
    )(*packs, *swapped, mine, other, *earlier, *before)


def post_kernel(gate, cot, packs, swapped, d_query, d_keys, d_values, d_gate, held):
    rows, half, channels = gate.shape
    size = channels // 4
    _, near, core = places()
    for s in range(4):
        held[near ^ s, core] = packs[s]
        held[near ^ s, 1 - core] = swapped[s]
    for r in range(rows):
        full = []
        for j in range(4):
            full.append(jnp.concatenate([held[h, r, :, j * size : (j + 1) * size] for h in range(4)], axis=1))
        d_query[r], d_keys[r], d_values[r] = full[1], full[2], full[3]
        sig = jax.nn.sigmoid(gate[r].astype(jnp.float32))
        d_gate[r] = (cot[r].astype(jnp.float32) * full[0].astype(jnp.float32) * sig * (1.0 - sig)).astype(jnp.bfloat16)


def post(gate, cot, packs, swapped):
    return pl.pallas_call(
        post_kernel,
        out_shape=[jax.ShapeDtypeStruct(gate.shape, jnp.bfloat16)] * 4,
        scratch_shapes=[VMEM((4,) + gate.shape, jnp.bfloat16)],
        compiler_params=PARAMS,
        name="unpack",
    )(gate, cot, packs, swapped)


def bias_kernel(*refs):
    near = places()[1]
    for s in range(4):
        refs[4][near ^ s] = refs[s][...].astype(jnp.float32)


def bias_out(pieces):
    return pl.pallas_call(
        bias_kernel,
        out_shape=jax.ShapeDtypeStruct((4,) + pieces[0].shape, jnp.float32),
        compiler_params=PARAMS,
        name="bias_grad",
    )(*pieces)


def shards(query, keys, values, gate_logits, pair_bias, key_mask, grad_out):
    rows, half, channels = query.shape
    heads, own, _ = pair_bias.shape
    size = channels // heads
    scaling = 1.0 / math.sqrt(size)
    far, cores = lax.axis_size("far"), lax.axis_size("key")
    chips = far * PAIR * PAIR
    assert PAIR * PAIR == heads == 4 and rows == cores == 2
    relative = own % 16 == 0
    chip = places()[0]

    def swap(value, axes, s, count):
        return lax.ppermute(value, axes, [(i, i ^ s) for i in range(count)]) if s else value

    def near_swap(value, s):
        return swap(value, ("near", "side"), s, 4)

    def far_swap(value, s):
        return swap(value, "far", s, far)

    def other_core(value):
        return swap(value, "key", 1, 2)

    def wide(value):
        return value.astype(jnp.float32)

    slabs = make_slabs(pair_bias)
    strips = jnp.stack([near_swap(slabs[s], s) for s in range(4)])
    strips = jnp.where(key_mask == 1, strips, jnp.bfloat16(-1000000000.0))
    groups = [far_swap(strips, f) for f in range(far)]
    *packs, kept, spare = make_packs(query, keys, values, gate_logits, grad_out)
    packs = [near_swap(packs[s], s + 1) for s in range(3)]
    starts = [f * 4 for f in range(far)]
    if not relative:
        starts, groups = [0], [jnp.concatenate(groups)[chip ^ jnp.arange(chips)].reshape(8, -1, half)]
    others = [jnp.concatenate([other_core(part) for part in jnp.split(groups[0], NEAR_PARTS)])] + [None] * (len(starts) - 1)
    orders = [list(range(len(starts))), list(range(len(starts)))[::-1]]
    before, sums, returned = [[]] * len(starts), [None] * len(starts), []
    for a, order in enumerate(orders):
        ours = [packs[0]] if a == 0 else packs[1:]
        if a:
            ours = list(lax.optimization_barrier((*ours, before[0][0]))[:2])
        swapped = [other_core(pack[1]) for pack in ours]
        ours = [pack[0] for pack in ours]
        if a == 0:
            spare = lax.optimization_barrier((spare, ours[0]))[0]
            ours, swapped = [kept] + ours, [other_core(spare)] + swapped
        earlier = []
        for g in order:
            if others[g] is None:
                groups[g] = lax.optimization_barrier((groups[g], before[0][0]))[0]
                others[g] = other_core(groups[g])
            mine, closed, ended = groups[g], a == len(orders) - 1, g == order[-1]
            if closed and g != order[0]:
                mine, last = lax.optimization_barrier((mine, sums[order[order.index(g) - 1]]))
                sums[order[order.index(g) - 1]] = last
            out = main(
                ours, swapped, mine, others[g], earlier, before[g], scaling, size, starts[g], relative, ended, closed, 1 - a
            )
            if not closed:
                before[g], earlier = out[:1], out[1:]
                continue
            d_mine, d_other, *earlier = out
            d_mine = wide(d_mine)
            if ended and relative:
                for f in range(1, far):
                    d_mine = d_mine + wide(far_swap(sums[f], f))
                d_mine = lax.optimization_barrier(d_mine)
            sums[g] = (d_mine + wide(other_core(d_other))).astype(jnp.bfloat16)
        if a == 0:
            stay, pass_on, *earlier = earlier
        returned += [near_swap(value, len(returned) + i + 1) for i, value in enumerate(earlier)]
    d_sum = sums[0]
    if not relative:
        d_sum = d_sum.reshape(chips, own, half)[chip ^ jnp.arange(chips)]
        total = wide(d_sum[:4])
        for f in range(1, far):
            total = total + wide(far_swap(d_sum[4 * f : 4 * f + 4], f))
        d_sum = total.astype(jnp.bfloat16)
    pieces = [near_swap(d_sum[s], s) for s in range(4)]
    returned = lax.optimization_barrier((*returned, *pieces))[:3]
    swapped = other_core(jnp.stack([pass_on] + [pack[1] for pack in returned]))
    packs = jnp.stack([stay] + [pack[0] for pack in returned])
    return (*post(gate_logits, grad_out, packs, swapped), bias_out(pieces))


def solution(mesh):
    groups, rows, cores = mesh.devices.shape
    devices = mesh.devices.reshape(groups, rows // PAIR**2, PAIR, PAIR, cores)
    mesh = jax.sharding.Mesh(devices, ("grp", "far", "near", "side", "key"))
    split = ("grp", "far", "near", "side")
    tokens = P(split, "key", None)
    pair = P(None, split, "key")
    in_specs = (tokens, tokens, tokens, tokens, pair, P(("grp", "key")), tokens)
    out_specs = (tokens, tokens, tokens, tokens, pair)
    return jax.shard_map(shards, mesh=mesh, in_specs=in_specs, out_specs=out_specs, check_vma=False)
```

```python
import functools
import math

import jax
import jax.numpy as jnp
from jax import lax
from jax.experimental import pallas as pl
from jax.experimental.pallas import tpu as pltpu
from jax.sharding import PartitionSpec as P

PAIR = 2
NEAR_PARTS = 2
ROWS_AT_ONCE = 16
VMEM = pltpu.VMEM
PARAMS = pltpu.CompilerParams(vmem_limit_bytes=32 * 1024 * 1024)
PRE_PARAMS = pltpu.CompilerParams(vmem_limit_bytes=60 * 1024 * 1024)


def places():
    near = lax.axis_index("near") * PAIR + lax.axis_index("side")
    return lax.axis_index("far") * PAIR * PAIR + near, near, lax.axis_index("key")


def fetch(pairs, sems):
    copies = [pltpu.make_async_copy(ref, buffer, sems.at[i]) for i, (ref, buffer) in enumerate(pairs)]
    for copy in copies:
        copy.start()
    for copy in copies:
        copy.wait()


def slab_kernel(bias, *slabs):
    near = places()[1]
    for s in range(4):
        slabs[s][...] = bias[near ^ s]


def make_slabs(bias):
    return pl.pallas_call(
        slab_kernel,
        out_shape=[jax.ShapeDtypeStruct(bias.shape[1:], jnp.bfloat16)] * 4,
        compiler_params=PARAMS,
        name="bias_by_head",
    )(bias)


def pack_kernel(*refs):
    inputs, packs, kept, buffers, (sems, held) = refs[:5], refs[5:8], refs[8:10], refs[10:15], refs[15:]
    fetch(list(zip(inputs, buffers)), sems)
    query, keys, values, gate, cot = buffers
    rows = query.shape[0]
    size = query.shape[2] // 4
    _, near, core = places()
    for r in range(rows):
        upstream = (cot[r].astype(jnp.float32) * jax.nn.sigmoid(gate[r].astype(jnp.float32))).astype(jnp.bfloat16)
        whole = [query[r], keys[r], values[r], upstream]
        for head in range(4):
            held[head, r] = jnp.concatenate([one[:, head * size : (head + 1) * size] for one in whole], axis=1)
    for i in range(2):
        for s in range(1, 4):
            packs[s - 1][i] = held[near ^ s, core ^ i]
        kept[i][...] = held[near, core ^ i]


def make_packs(*inputs):
    one = inputs[0]
    return pl.pallas_call(
        pack_kernel,
        in_specs=[pl.BlockSpec(memory_space=pl.ANY)] * 5,
        out_shape=[jax.ShapeDtypeStruct(one.shape, jnp.bfloat16)] * 3
        + [jax.ShapeDtypeStruct(one.shape[1:], jnp.bfloat16)] * 2,
        scratch_shapes=[VMEM(one.shape, jnp.bfloat16)] * 5
        + [pltpu.SemaphoreType.DMA((5,)), VMEM((4,) + one.shape, jnp.bfloat16)],
        compiler_params=PRE_PARAMS,
        name="pack",
    )(*inputs)


NT = (((1,), (1,)), ((), ()))


def dot(a, b, dims=(((1,), (0,)), ((), ()))):
    return lax.dot_general(a, b, dims, preferred_element_type=jnp.float32)


def main_kernel(scaling, size, start, relative, begun, ended, opened, closed, split, *refs):
    packs, swapped, (mine, other), refs = refs[:2], refs[2:4], refs[4:6], refs[6:]
    earlier, refs = refs[: 4 if begun else 0], refs[4 if begun else 0 :]
    before, refs = refs[: 1 if opened else 0], refs[1 if opened else 0 :]
    d_bias, refs = refs[: 2 if closed else 1], refs[2 if closed else 1 :]
    results, refs = refs[: 2 + split if ended else 4], refs[2 + split if ended else 4 :]
    q_all, d_all, k_of, v_of, dk_t, dv_t, att_all, dq_all, bias_wide, q_now, d_now, s_now, p_now, low_now, d_low_now, bias_sum = refs
    step = pl.program_id(0)
    chip, _, core = places()
    parts, (half, _) = len(packs), packs[0].shape
    blocks, own, _ = mine.shape
    lanes = parts * size

    def side(i):
        return pl.ds(pl.multiple_of((core ^ i) * half, half), half)

    @pl.when(step == 0)
    def _():
        lane = lax.broadcasted_iota(jnp.int32, (half, lanes), 1) // size
        for i in range(2):
            here = [(swapped if i else packs)[p][...] for p in range(parts)]
            q, k, v, d = [
                jnp.concatenate([one[:, j * size : (j + 1) * size] for one in here], axis=1) for j in range(4)
            ]
            q_all[side(i)], d_all[side(i)] = q, d
            rows = slice(i * half, (i + 1) * half)
            for r in range(parts):
                k_of[r, rows] = jnp.where(lane == r, k, 0)
                v_of[r, rows] = jnp.where(lane == r, v, 0)
        for i, ref in enumerate((att_all, dq_all, dk_t, dv_t)):
            ref[...] = earlier[i][...] if begun else jnp.zeros_like(ref)

    def strip(i):
        at = start + step * blocks + i
        at = chip ^ at if relative else at
        return pl.ds(pl.multiple_of(at * own, own), own)

    for i in range(blocks):
        rows = slice(i * own, (i + 1) * own)
        bias_wide[rows, :half] = mine[i].astype(jnp.float32)
        bias_wide[rows, half:] = other[i].astype(jnp.float32)
        q_now[rows], d_now[rows] = q_all[strip(i)], d_all[strip(i)]
    q, d = q_now[...], d_now[...]
    q_t = q.astype(jnp.float32).T.astype(jnp.bfloat16)
    d_t = d.astype(jnp.float32).T.astype(jnp.bfloat16)

    def scores(r):
        s_now[r % 2] = dot(q, k_of[r], NT)
        p_now[r % 2] = dot(d, v_of[r], NT)

    att_sum, dq_sum = None, None
    scores(0)
    for r in range(parts):
        if r + 1 < parts:
            scores(r + 1)
        for at in range(0, blocks * own, ROWS_AT_ONCE):
            rows = slice(at, at + ROWS_AT_ONCE)
            logits = s_now[r % 2, rows] * scaling + bias_wide[rows]
            expo = jnp.exp(logits - jnp.max(logits, axis=-1, keepdims=True))
            probs = expo * (1.0 / jnp.sum(expo, axis=-1, keepdims=True))
            d_probs = p_now[r % 2, rows]
            inner = jnp.sum(probs * d_probs, axis=-1, keepdims=True)
            d_logits = probs * (d_probs - inner)
            low_now[r % 2, rows] = probs.astype(jnp.bfloat16)
            d_low_now[r % 2, rows] = d_logits.astype(jnp.bfloat16)
            if r:
                d_logits = bias_sum[rows] + d_logits
            elif opened:
                d_logits = before[0][rows] + d_logits
            bias_sum[rows] = d_logits
        low, d_low = low_now[r % 2], d_low_now[r % 2]
        att, dq = dot(low, v_of[r]), dot(d_low, k_of[r])
        cut = slice(r * size, (r + 1) * size)
        dk_t[cut] += dot(q_t[cut], d_low)
        dv_t[cut] += dot(d_t[cut], low)
        att_sum = att if r == 0 else att_sum + att
        dq_sum = dq if r == 0 else dq_sum + dq
    att_low, dq_low = att_sum.astype(jnp.bfloat16), (dq_sum * scaling).astype(jnp.bfloat16)
    for i in range(blocks):
        rows = slice(i * own, (i + 1) * own)
        att_all[strip(i)], dq_all[strip(i)] = att_low[rows], dq_low[rows]
        if closed:
            d_bias[0][i] = bias_sum[rows, :half].astype(jnp.bfloat16)
            d_bias[1][i] = bias_sum[rows, half:].astype(jnp.bfloat16)
    if not closed:
        d_bias[0][...] = bias_sum[...]

    @pl.when(step == pl.num_programs(0) - 1)
    def _():
        if not ended:
            for ref, value in zip(results, (att_all, dq_all, dk_t, dv_t)):
                ref[...] = value[...]
            return
        dk = (dk_t[...] * scaling).T.astype(jnp.bfloat16)
        dv = dv_t[...].T.astype(jnp.bfloat16)
        for i in range(2):
            rows = slice(i * half, (i + 1) * half)
            whole = [att_all[side(i)], dq_all[side(i)], dk[rows], dv[rows]]
            for p in range(parts):
                pack = jnp.concatenate([one[:, p * size : (p + 1) * size] for one in whole], axis=1)
                if split and p == 0:
                    results[i][...] = pack
                else:
                    results[p + split][i] = pack


def fixed(value):
    return pl.BlockSpec(value.shape, lambda i: (0,) * len(value.shape))


def main(packs, swapped, mine, other, earlier, before, scaling, size, start, relative, ended, closed, split):
    parts, (half, width) = len(packs), swapped[0].shape
    strips, own, _ = mine.shape
    blocks, lanes = 4, parts * size
    key_count = queries = 2 * half
    rows = jax.ShapeDtypeStruct((queries, lanes), jnp.bfloat16)
    turned = jax.ShapeDtypeStruct((lanes, key_count), jnp.float32)
    wide = jax.ShapeDtypeStruct((strips * own, key_count), jnp.float32)
    strip = pl.BlockSpec((blocks, own, half), lambda i: (i, 0, 0))
    wide_strip = pl.BlockSpec((blocks * own, key_count), lambda i: (i, 0))
    now = VMEM((blocks * own, lanes), jnp.bfloat16)
    results = [rows, rows, turned, turned]
    if ended:
        ours = [jax.ShapeDtypeStruct((half, width), jnp.bfloat16)] * 2
        results = [jax.ShapeDtypeStruct((2, half, width), jnp.bfloat16)] * (parts - split)
        results = ours * split + results
    d_bias = [mine, other] if closed else [wide]
    return pl.pallas_call(
        functools.partial(main_kernel, scaling, size, start, relative, bool(earlier), ended, bool(before), closed, split),
        grid=(strips // blocks,),
        in_specs=[fixed(one) for one in [*packs, *swapped]]
        + [strip, strip]
        + [fixed(one) for one in earlier]
        + [wide_strip] * len(before),
        out_specs=([strip] * 2 if closed else [wide_strip]) + [fixed(one) for one in results],
        out_shape=[jax.ShapeDtypeStruct(one.shape, one.dtype) for one in d_bias + results],
        scratch_shapes=[
            VMEM(rows.shape, jnp.bfloat16),
            VMEM(rows.shape, jnp.bfloat16),
            VMEM((parts, key_count, lanes), jnp.bfloat16),
            VMEM((parts, key_count, lanes), jnp.bfloat16),
            VMEM(turned.shape, jnp.float32),
            VMEM(turned.shape, jnp.float32),
            VMEM(rows.shape, jnp.bfloat16),
            VMEM(rows.shape, jnp.bfloat16),
            VMEM((blocks * own, key_count), jnp.float32),
            now,
            now,
            VMEM((2, blocks * own, key_count), jnp.float32),
            VMEM((2, blocks * own, key_count), jnp.float32),
            VMEM((2, blocks * own, key_count), jnp.bfloat16),
            VMEM((2, blocks * own, key_count), jnp.bfloat16),
            VMEM((blocks * own, key_count), jnp.float32),
        ],
        compiler_params=PARAMS,
        cost_estimate=pl.CostEstimate(flops=1, bytes_accessed=1, transcendentals=0),
        name="attention",
    )(*packs, *swapped, mine, other, *earlier, *before)


def post_kernel(gate, cot, packs, swapped, d_query, d_keys, d_values, d_gate, held):
    rows, half, channels = gate.shape
    size = channels // 4
    _, near, core = places()
    for s in range(4):
        held[near ^ s, core] = packs[s]
        held[near ^ s, 1 - core] = swapped[s]
    for r in range(rows):
        full = []
        for j in range(4):
            full.append(jnp.concatenate([held[h, r, :, j * size : (j + 1) * size] for h in range(4)], axis=1))
        d_query[r], d_keys[r], d_values[r] = full[1], full[2], full[3]
        sig = jax.nn.sigmoid(gate[r].astype(jnp.float32))
        d_gate[r] = (cot[r].astype(jnp.float32) * full[0].astype(jnp.float32) * sig * (1.0 - sig)).astype(jnp.bfloat16)


def post(gate, cot, packs, swapped):
    return pl.pallas_call(
        post_kernel,
        out_shape=[jax.ShapeDtypeStruct(gate.shape, jnp.bfloat16)] * 4,
        scratch_shapes=[VMEM((4,) + gate.shape, jnp.bfloat16)],
        compiler_params=PARAMS,
        name="unpack",
    )(gate, cot, packs, swapped)


def bias_kernel(*refs):
    near = places()[1]
    for s in range(4):
        refs[4][near ^ s] = refs[s][...].astype(jnp.float32)


def bias_out(pieces):
    return pl.pallas_call(
        bias_kernel,
        out_shape=jax.ShapeDtypeStruct((4,) + pieces[0].shape, jnp.float32),
        compiler_params=PARAMS,
        name="bias_grad",
    )(*pieces)


def shards(query, keys, values, gate_logits, pair_bias, key_mask, grad_out):
    rows, half, channels = query.shape
    heads, own, _ = pair_bias.shape
    size = channels // heads
    scaling = 1.0 / math.sqrt(size)
    far, cores = lax.axis_size("far"), lax.axis_size("key")
    chips = far * PAIR * PAIR
    assert PAIR * PAIR == heads == 4 and rows == cores == 2
    relative = own % 16 == 0
    chip = places()[0]

    def swap(value, axes, s, count):
        return lax.ppermute(value, axes, [(i, i ^ s) for i in range(count)]) if s else value

    def near_swap(value, s):
        return swap(value, ("near", "side"), s, 4)

    def far_swap(value, s):
        return swap(value, "far", s, far)

    def other_core(value):
        return swap(value, "key", 1, 2)

    def wide(value):
        return value.astype(jnp.float32)

    slabs = make_slabs(pair_bias)
    strips = jnp.stack([near_swap(slabs[s], s) for s in range(4)])
    strips = jnp.where(key_mask == 1, strips, jnp.bfloat16(-1000000000.0))
    groups = [far_swap(strips, f) for f in range(far)]
    *packs, kept, spare = make_packs(query, keys, values, gate_logits, grad_out)
    packs = [near_swap(packs[s], s + 1) for s in range(3)]
    starts = [f * 4 for f in range(far)]
    if not relative:
        starts, groups = [0], [jnp.concatenate(groups)[chip ^ jnp.arange(chips)].reshape(8, -1, half)]
    others = [jnp.concatenate([other_core(part) for part in jnp.split(groups[0], NEAR_PARTS)])] + [None] * (len(starts) - 1)
    sets = [None, None]
    before, sums, returned, state = [[]] * len(starts), [None] * len(starts), [], [[], []]
    for g, start in enumerate(starts):
        ended = g == len(starts) - 1
        for a in range(2):
            if g == 0:
                ours = [packs[0]] if a == 0 else packs[1:]
                if a:
                    ours = list(lax.optimization_barrier((*ours, before[0][0]))[:2])
                swapped = [other_core(pack[1]) for pack in ours]
                ours = [pack[0] for pack in ours]
                if a == 0:
                    spare = lax.optimization_barrier((spare, ours[0]))[0]
                    ours, swapped = [kept] + ours, [other_core(spare)] + swapped
                sets[a] = ours, swapped
            elif a == 0:
                groups[g] = lax.optimization_barrier((groups[g], d_mine))[0]
                others[g] = other_core(groups[g])
            out = main(
                *sets[a], groups[g], others[g], state[a], before[g], scaling, size, start, relative, ended, bool(a), 1 - a
            )
            if a == 0:
                before[g], state[a] = out[:1], out[1:]
            else:
                d_mine, d_other, *state[a] = out
                sums[g] = (wide(d_mine) + wide(other_core(d_other))).astype(jnp.bfloat16)
    stay, pass_on, *state[0] = state[0]
    returned = [near_swap(value, i + 1) for i, value in enumerate([*state[0], *state[1]])]
    if relative:
        total = wide(sums[0])
        for f in range(1, far):
            total = total + wide(far_swap(sums[f], f))
    else:
        d_sum = sums[0].reshape(chips, own, half)[chip ^ jnp.arange(chips)]
        total = wide(d_sum[:4])
        for f in range(1, far):
            total = total + wide(far_swap(d_sum[4 * f : 4 * f + 4], f))
    d_sum = total.astype(jnp.bfloat16)
    pieces = [near_swap(d_sum[s], s) for s in range(4)]
    returned = lax.optimization_barrier((*returned, *pieces))[:3]
    swapped = other_core(jnp.stack([pass_on] + [pack[1] for pack in returned]))
    packs = jnp.stack([stay] + [pack[0] for pack in returned])
    return (*post(gate_logits, grad_out, packs, swapped), bias_out(pieces))


def solution(mesh):
    groups, rows, cores = mesh.devices.shape
    devices = mesh.devices.reshape(groups, rows // PAIR**2, PAIR, PAIR, cores)
    mesh = jax.sharding.Mesh(devices, ("grp", "far", "near", "side", "key"))
    split = ("grp", "far", "near", "side")
    tokens = P(split, "key", None)
    pair = P(None, split, "key")
    in_specs = (tokens, tokens, tokens, tokens, pair, P(("grp", "key")), tokens)
    out_specs = (tokens, tokens, tokens, tokens, pair)
    return jax.shard_map(shards, mesh=mesh, in_specs=in_specs, out_specs=out_specs, check_vma=False)
```

```python
import functools
import math

import jax
import jax.numpy as jnp
from jax import lax
from jax.experimental import pallas as pl
from jax.experimental.pallas import tpu as pltpu
from jax.sharding import PartitionSpec as P

PAIR = 2
NEAR_PARTS = 2
ROWS_AT_ONCE = 16
VMEM = pltpu.VMEM
PARAMS = pltpu.CompilerParams(vmem_limit_bytes=32 * 1024 * 1024)
PRE_PARAMS = pltpu.CompilerParams(vmem_limit_bytes=60 * 1024 * 1024)


def places():
    near = lax.axis_index("near") * PAIR + lax.axis_index("side")
    return lax.axis_index("far") * PAIR * PAIR + near, near, lax.axis_index("key")


def fetch(pairs, sems):
    copies = [pltpu.make_async_copy(ref, buffer, sems.at[i]) for i, (ref, buffer) in enumerate(pairs)]
    for copy in copies:
        copy.start()
    for copy in copies:
        copy.wait()


def slab_kernel(bias, *slabs):
    near = places()[1]
    for s in range(4):
        slabs[s][...] = bias[near ^ s]


def make_slabs(bias):
    return pl.pallas_call(
        slab_kernel,
        out_shape=[jax.ShapeDtypeStruct(bias.shape[1:], jnp.bfloat16)] * 4,
        compiler_params=PARAMS,
        name="bias_by_head",
    )(bias)


def pack_kernel(*refs):
    inputs, packs, kept, buffers, (sems, held) = refs[:5], refs[5:8], refs[8:10], refs[10:15], refs[15:]
    fetch(list(zip(inputs, buffers)), sems)
    query, keys, values, gate, cot = buffers
    rows = query.shape[0]
    size = query.shape[2] // 4
    _, near, core = places()
    for r in range(rows):
        upstream = (cot[r].astype(jnp.float32) * jax.nn.sigmoid(gate[r].astype(jnp.float32))).astype(jnp.bfloat16)
        whole = [query[r], keys[r], values[r], upstream]
        for head in range(4):
            held[head, r] = jnp.concatenate([one[:, head * size : (head + 1) * size] for one in whole], axis=1)
    for i in range(2):
        for s in range(1, 4):
            packs[s - 1][i] = held[near ^ s, core ^ i]
        kept[i][...] = held[near, core ^ i]


def make_packs(*inputs):
    one = inputs[0]
    return pl.pallas_call(
        pack_kernel,
        in_specs=[pl.BlockSpec(memory_space=pl.ANY)] * 5,
        out_shape=[jax.ShapeDtypeStruct(one.shape, jnp.bfloat16)] * 3
        + [jax.ShapeDtypeStruct(one.shape[1:], jnp.bfloat16)] * 2,
        scratch_shapes=[VMEM(one.shape, jnp.bfloat16)] * 5
        + [pltpu.SemaphoreType.DMA((5,)), VMEM((4,) + one.shape, jnp.bfloat16)],
        compiler_params=PRE_PARAMS,
        name="pack",
    )(*inputs)


NT = (((1,), (1,)), ((), ()))


def dot(a, b, dims=(((1,), (0,)), ((), ()))):
    return lax.dot_general(a, b, dims, preferred_element_type=jnp.float32)


def main_kernel(scaling, size, blocks, start, relative, begun, ended, opened, closed, split, *refs):
    packs, swapped, (mine, other), refs = refs[:2], refs[2:4], refs[4:6], refs[6:]
    earlier, refs = refs[: 4 if begun else 0], refs[4 if begun else 0 :]
    before, refs = refs[: 1 if opened else 0], refs[1 if opened else 0 :]
    d_bias, refs = refs[: 2 if closed else 1], refs[2 if closed else 1 :]
    results, refs = refs[: 2 + split if ended else 4], refs[2 + split if ended else 4 :]
    q_all, d_all, k_of, v_of, dk_t, dv_t, att_all, dq_all, bias_wide, q_now, d_now, s_now, p_now, low_now, d_low_now, bias_sum = refs
    steps = q_all.shape[0] // (blocks * mine.shape[1]) if not relative else 1
    step = pl.program_id(0) if steps > 1 else 0
    chip, _, core = places()
    parts, (half, _) = len(packs), packs[0].shape
    own = mine.shape[1]
    lanes = parts * size

    def side(i):
        return pl.ds(pl.multiple_of((core ^ i) * half, half), half)

    def first():
        lane = lax.broadcasted_iota(jnp.int32, (half, lanes), 1) // size
        for i in range(2):
            here = [(swapped if i else packs)[p][...] for p in range(parts)]
            q, k, v, d = [
                jnp.concatenate([one[:, j * size : (j + 1) * size] for one in here], axis=1) for j in range(4)
            ]
            q_all[side(i)], d_all[side(i)] = q, d
            rows = slice(i * half, (i + 1) * half)
            for r in range(parts):
                k_of[r, rows] = jnp.where(lane == r, k, 0)
                v_of[r, rows] = jnp.where(lane == r, v, 0)
        for i, ref in enumerate((att_all, dq_all, dk_t, dv_t)):
            ref[...] = earlier[i][...] if begun else jnp.zeros_like(ref)

    first() if steps == 1 else pl.when(step == 0)(first)

    def strip(i):
        at = start + step * blocks + i
        at = chip ^ at if relative else at
        return pl.ds(pl.multiple_of(at * own, own), own)

    for i in range(blocks):
        rows = slice(i * own, (i + 1) * own)
        bias_wide[rows, :half] = mine[i].astype(jnp.float32)
        bias_wide[rows, half:] = other[i].astype(jnp.float32)
        q_now[rows], d_now[rows] = q_all[strip(i)], d_all[strip(i)]
    q, d = q_now[...], d_now[...]
    q_t = q.astype(jnp.float32).T.astype(jnp.bfloat16)
    d_t = d.astype(jnp.float32).T.astype(jnp.bfloat16)

    def scores(r):
        s_now[r % 2] = dot(q, k_of[r], NT)
        p_now[r % 2] = dot(d, v_of[r], NT)

    att_sum, dq_sum = None, None
    scores(0)
    for r in range(parts):
        if r + 1 < parts:
            scores(r + 1)
        for at in range(0, blocks * own, ROWS_AT_ONCE):
            rows = slice(at, at + ROWS_AT_ONCE)
            logits = s_now[r % 2, rows] * scaling + bias_wide[rows]
            expo = jnp.exp(logits - jnp.max(logits, axis=-1, keepdims=True))
            probs = expo * (1.0 / jnp.sum(expo, axis=-1, keepdims=True))
            d_probs = p_now[r % 2, rows]
            inner = jnp.sum(probs * d_probs, axis=-1, keepdims=True)
            d_logits = probs * (d_probs - inner)
            low_now[r % 2, rows] = probs.astype(jnp.bfloat16)
            d_low_now[r % 2, rows] = d_logits.astype(jnp.bfloat16)
            if r:
                d_logits = bias_sum[rows] + d_logits
            elif opened:
                d_logits = before[0][rows] + d_logits
            bias_sum[rows] = d_logits
        low, d_low = low_now[r % 2], d_low_now[r % 2]
        att, dq = dot(low, v_of[r]), dot(d_low, k_of[r])
        cut = slice(r * size, (r + 1) * size)
        dk_t[cut] += dot(q_t[cut], d_low)
        dv_t[cut] += dot(d_t[cut], low)
        att_sum = att if r == 0 else att_sum + att
        dq_sum = dq if r == 0 else dq_sum + dq
    att_low, dq_low = att_sum.astype(jnp.bfloat16), (dq_sum * scaling).astype(jnp.bfloat16)
    for i in range(blocks):
        rows = slice(i * own, (i + 1) * own)
        att_all[strip(i)], dq_all[strip(i)] = att_low[rows], dq_low[rows]
        if closed:
            d_bias[0][i] = bias_sum[rows, :half].astype(jnp.bfloat16)
            d_bias[1][i] = bias_sum[rows, half:].astype(jnp.bfloat16)
    if not closed:
        d_bias[0][...] = bias_sum[...]

    def last():
        if not ended:
            for ref, value in zip(results, (att_all, dq_all, dk_t, dv_t)):
                ref[...] = value[...]
            return
        dk = (dk_t[...] * scaling).T.astype(jnp.bfloat16)
        dv = dv_t[...].T.astype(jnp.bfloat16)
        for i in range(2):
            rows = slice(i * half, (i + 1) * half)
            whole = [att_all[side(i)], dq_all[side(i)], dk[rows], dv[rows]]
            for p in range(parts):
                pack = jnp.concatenate([one[:, p * size : (p + 1) * size] for one in whole], axis=1)
                if split and p == 0:
                    results[i][...] = pack
                else:
                    results[p + split][i] = pack

    last() if steps == 1 else pl.when(step == steps - 1)(last)


def fixed(value):
    return pl.BlockSpec(value.shape, lambda i: (0,) * len(value.shape))


def main(packs, swapped, mine, other, earlier, before, scaling, size, start, relative, ended, closed, split):
    parts, (half, width) = len(packs), swapped[0].shape
    strips, own, _ = mine.shape
    blocks, lanes = 4, parts * size
    key_count = queries = 2 * half
    rows = jax.ShapeDtypeStruct((queries, lanes), jnp.bfloat16)
    turned = jax.ShapeDtypeStruct((lanes, key_count), jnp.float32)
    wide = jax.ShapeDtypeStruct((strips * own, key_count), jnp.float32)
    strip = pl.BlockSpec((blocks, own, half), lambda i: (i, 0, 0))
    wide_strip = pl.BlockSpec((blocks * own, key_count), lambda i: (i, 0))
    now = VMEM((blocks * own, lanes), jnp.bfloat16)
    results = [rows, rows, turned, turned]
    if ended:
        ours = [jax.ShapeDtypeStruct((half, width), jnp.bfloat16)] * 2
        results = [jax.ShapeDtypeStruct((2, half, width), jnp.bfloat16)] * (parts - split)
        results = ours * split + results
    d_bias = [mine, other] if closed else [wide]
    grid = {}
    if not relative:
        grid = dict(
            grid=(strips // blocks,),
            in_specs=[fixed(one) for one in [*packs, *swapped]]
            + [strip, strip]
            + [fixed(one) for one in earlier]
            + [wide_strip] * len(before),
            out_specs=([strip] * 2 if closed else [wide_strip]) + [fixed(one) for one in results],
        )
    return pl.pallas_call(
        functools.partial(
            main_kernel, scaling, size, blocks, start, relative, bool(earlier), ended, bool(before), closed, split
        ),
        **grid,
        out_shape=[jax.ShapeDtypeStruct(one.shape, one.dtype) for one in d_bias + results],
        scratch_shapes=[
            VMEM(rows.shape, jnp.bfloat16),
            VMEM(rows.shape, jnp.bfloat16),
            VMEM((parts, key_count, lanes), jnp.bfloat16),
            VMEM((parts, key_count, lanes), jnp.bfloat16),
            VMEM(turned.shape, jnp.float32),
            VMEM(turned.shape, jnp.float32),
            VMEM(rows.shape, jnp.bfloat16),
            VMEM(rows.shape, jnp.bfloat16),
            VMEM((blocks * own, key_count), jnp.float32),
            now,
            now,
            VMEM((2, blocks * own, key_count), jnp.float32),
            VMEM((2, blocks * own, key_count), jnp.float32),
            VMEM((2, blocks * own, key_count), jnp.bfloat16),
            VMEM((2, blocks * own, key_count), jnp.bfloat16),
            VMEM((blocks * own, key_count), jnp.float32),
        ],
        compiler_params=PARAMS,
        cost_estimate=pl.CostEstimate(flops=1, bytes_accessed=1, transcendentals=0),
        name="attention",
    )(*packs, *swapped, mine, other, *earlier, *before)


def post_kernel(gate, cot, packs, swapped, d_query, d_keys, d_values, d_gate, held):
    rows, half, channels = gate.shape
    size = channels // 4
    _, near, core = places()
    for s in range(4):
        held[near ^ s, core] = packs[s]
        held[near ^ s, 1 - core] = swapped[s]
    for r in range(rows):
        full = []
        for j in range(4):
            full.append(jnp.concatenate([held[h, r, :, j * size : (j + 1) * size] for h in range(4)], axis=1))
        d_query[r], d_keys[r], d_values[r] = full[1], full[2], full[3]
        sig = jax.nn.sigmoid(gate[r].astype(jnp.float32))
        d_gate[r] = (cot[r].astype(jnp.float32) * full[0].astype(jnp.float32) * sig * (1.0 - sig)).astype(jnp.bfloat16)


def post(gate, cot, packs, swapped):
    return pl.pallas_call(
        post_kernel,
        out_shape=[jax.ShapeDtypeStruct(gate.shape, jnp.bfloat16)] * 4,
        scratch_shapes=[VMEM((4,) + gate.shape, jnp.bfloat16)],
        compiler_params=PARAMS,
        name="unpack",
    )(gate, cot, packs, swapped)


def bias_kernel(*refs):
    near = places()[1]
    for s in range(4):
        refs[4][near ^ s] = refs[s][...].astype(jnp.float32)


def bias_out(pieces):
    return pl.pallas_call(
        bias_kernel,
        out_shape=jax.ShapeDtypeStruct((4,) + pieces[0].shape, jnp.float32),
        compiler_params=PARAMS,
        name="bias_grad",
    )(*pieces)


def shards(query, keys, values, gate_logits, pair_bias, key_mask, grad_out):
    rows, half, channels = query.shape
    heads, own, _ = pair_bias.shape
    size = channels // heads
    scaling = 1.0 / math.sqrt(size)
    far, cores = lax.axis_size("far"), lax.axis_size("key")
    chips = far * PAIR * PAIR
    assert PAIR * PAIR == heads == 4 and rows == cores == 2
    relative = own % 16 == 0
    chip = places()[0]

    def swap(value, axes, s, count):
        return lax.ppermute(value, axes, [(i, i ^ s) for i in range(count)]) if s else value

    def near_swap(value, s):
        return swap(value, ("near", "side"), s, 4)

    def far_swap(value, s):
        return swap(value, "far", s, far)

    def other_core(value):
        return swap(value, "key", 1, 2)

    def wide(value):
        return value.astype(jnp.float32)

    slabs = make_slabs(pair_bias)
    strips = jnp.stack([near_swap(slabs[s], s) for s in range(4)])
    strips = jnp.where(key_mask == 1, strips, jnp.bfloat16(-1000000000.0))
    groups = [far_swap(strips, f) for f in range(far)]
    *packs, kept, spare = make_packs(query, keys, values, gate_logits, grad_out)
    packs = [near_swap(packs[s], s + 1) for s in range(3)]
    starts = [f * 4 for f in range(far)]
    if not relative:
        starts, groups = [0], [jnp.concatenate(groups)[chip ^ jnp.arange(chips)].reshape(8, -1, half)]
    others = [jnp.concatenate([other_core(part) for part in jnp.split(groups[0], NEAR_PARTS)])] + [None] * (len(starts) - 1)
    orders = [list(range(len(starts))), list(range(len(starts)))[::-1]]
    before, sums, returned = [[]] * len(starts), [None] * len(starts), []
    for a, order in enumerate(orders):
        ours = [packs[0]] if a == 0 else packs[1:]
        if a:
            ours = list(lax.optimization_barrier((*ours, before[0][0]))[:2])
        swapped = [other_core(pack[1]) for pack in ours]
        ours = [pack[0] for pack in ours]
        if a == 0:
            spare = lax.optimization_barrier((spare, ours[0]))[0]
            ours, swapped = [kept] + ours, [other_core(spare)] + swapped
        earlier = []
        for g in order:
            if others[g] is None:
                groups[g] = lax.optimization_barrier((groups[g], before[0][0]))[0]
                others[g] = other_core(groups[g])
            mine, closed, ended = groups[g], a == len(orders) - 1, g == order[-1]
            if closed and g != order[0]:
                mine, last = lax.optimization_barrier((mine, sums[order[order.index(g) - 1]]))
                sums[order[order.index(g) - 1]] = last
            out = main(
                ours, swapped, mine, others[g], earlier, before[g], scaling, size, starts[g], relative, ended, closed, 1 - a
            )
            if not closed:
                before[g], earlier = out[:1], out[1:]
                continue
            d_mine, d_other, *earlier = out
            d_mine = wide(d_mine)
            if ended and relative:
                for f in range(1, far):
                    d_mine = d_mine + wide(far_swap(sums[f], f))
                d_mine = lax.optimization_barrier(d_mine)
            sums[g] = (d_mine + wide(other_core(d_other))).astype(jnp.bfloat16)
        if a == 0:
            stay, pass_on, *earlier = earlier
        returned += [near_swap(value, len(returned) + i + 1) for i, value in enumerate(earlier)]
    d_sum = sums[0]
    if not relative:
        d_sum = d_sum.reshape(chips, own, half)[chip ^ jnp.arange(chips)]
        total = wide(d_sum[:4])
        for f in range(1, far):
            total = total + wide(far_swap(d_sum[4 * f : 4 * f + 4], f))
        d_sum = total.astype(jnp.bfloat16)
    pieces = [near_swap(d_sum[s], s) for s in range(4)]
    returned = lax.optimization_barrier((*returned, *pieces))[:3]
    swapped = other_core(jnp.stack([pass_on] + [pack[1] for pack in returned]))
    packs = jnp.stack([stay] + [pack[0] for pack in returned])
    return (*post(gate_logits, grad_out, packs, swapped), bias_out(pieces))


def solution(mesh):
    groups, rows, cores = mesh.devices.shape
    devices = mesh.devices.reshape(groups, rows // PAIR**2, PAIR, PAIR, cores)
    mesh = jax.sharding.Mesh(devices, ("grp", "far", "near", "side", "key"))
    split = ("grp", "far", "near", "side")
    tokens = P(split, "key", None)
    pair = P(None, split, "key")
    in_specs = (tokens, tokens, tokens, tokens, pair, P(("grp", "key")), tokens)
    out_specs = (tokens, tokens, tokens, tokens, pair)
    return jax.shard_map(shards, mesh=mesh, in_specs=in_specs, out_specs=out_specs, check_vma=False)
```

```python
import functools
import math

import jax
import jax.numpy as jnp
from jax import lax
from jax.experimental import pallas as pl
from jax.experimental.pallas import tpu as pltpu
from jax.sharding import PartitionSpec as P

PAIR = 2
NEAR_PARTS = 2
ROWS_AT_ONCE = 16
VMEM = pltpu.VMEM
PARAMS = pltpu.CompilerParams(vmem_limit_bytes=32 * 1024 * 1024)
PRE_PARAMS = pltpu.CompilerParams(vmem_limit_bytes=60 * 1024 * 1024)


def places():
    near = lax.axis_index("near") * PAIR + lax.axis_index("side")
    return lax.axis_index("far") * PAIR * PAIR + near, near, lax.axis_index("key")


def fetch(pairs, sems):
    copies = [pltpu.make_async_copy(ref, buffer, sems.at[i]) for i, (ref, buffer) in enumerate(pairs)]
    for copy in copies:
        copy.start()
    for copy in copies:
        copy.wait()


def slab_kernel(bias, *slabs):
    near = places()[1]
    for s in range(4):
        slabs[s][...] = bias[near ^ s]


def make_slabs(bias):
    return pl.pallas_call(
        slab_kernel,
        out_shape=[jax.ShapeDtypeStruct(bias.shape[1:], jnp.bfloat16)] * 4,
        compiler_params=PARAMS,
        name="bias_by_head",
    )(bias)


def pack_kernel(*refs):
    inputs, packs, kept, buffers, (sems, held) = refs[:5], refs[5:8], refs[8:10], refs[10:15], refs[15:]
    fetch(list(zip(inputs, buffers)), sems)
    query, keys, values, gate, cot = buffers
    rows = query.shape[0]
    size = query.shape[2] // 4
    _, near, core = places()
    for r in range(rows):
        upstream = (cot[r].astype(jnp.float32) * jax.nn.sigmoid(gate[r].astype(jnp.float32))).astype(jnp.bfloat16)
        whole = [query[r], keys[r], values[r], upstream]
        for head in range(4):
            held[head, r] = jnp.concatenate([one[:, head * size : (head + 1) * size] for one in whole], axis=1)
    for i in range(2):
        for s in range(1, 4):
            packs[s - 1][i] = held[near ^ s, core ^ i]
        kept[i][...] = held[near, core ^ i]


def make_packs(*inputs):
    one = inputs[0]
    return pl.pallas_call(
        pack_kernel,
        in_specs=[pl.BlockSpec(memory_space=pl.ANY)] * 5,
        out_shape=[jax.ShapeDtypeStruct(one.shape, jnp.bfloat16)] * 3
        + [jax.ShapeDtypeStruct(one.shape[1:], jnp.bfloat16)] * 2,
        scratch_shapes=[VMEM(one.shape, jnp.bfloat16)] * 5
        + [pltpu.SemaphoreType.DMA((5,)), VMEM((4,) + one.shape, jnp.bfloat16)],
        compiler_params=PRE_PARAMS,
        name="pack",
    )(*inputs)


NT = (((1,), (1,)), ((), ()))


def dot(a, b, dims=(((1,), (0,)), ((), ()))):
    return lax.dot_general(a, b, dims, preferred_element_type=jnp.float32)


def main_kernel(scaling, size, blocks, start, relative, begun, ended, opened, closed, split, *refs):
    packs, swapped, (mine, other), refs = refs[:2], refs[2:4], refs[4:6], refs[6:]
    earlier, refs = refs[: 4 if begun else 0], refs[4 if begun else 0 :]
    before, refs = refs[: 1 if opened else 0], refs[1 if opened else 0 :]
    d_bias, refs = refs[: 2 if closed else 1], refs[2 if closed else 1 :]
    results, refs = refs[: 2 + split if ended else 4], refs[2 + split if ended else 4 :]
    q_all, d_all, k_of, v_of, dk_t, dv_t, att_all, dq_all, bias_wide, q_now, d_now, s_now, p_now, low_now, d_low_now, bias_sum, k_t, v_t, att_now, dq_now = refs
    steps = q_all.shape[0] // (blocks * mine.shape[1]) if not relative else 1
    step = pl.program_id(0) if steps > 1 else 0
    chip, _, core = places()
    parts, (half, _) = len(packs), packs[0].shape
    own = mine.shape[1]
    lanes = parts * size

    def side(i):
        return pl.ds(pl.multiple_of((core ^ i) * half, half), half)

    def first():
        lane = lax.broadcasted_iota(jnp.int32, (half, lanes), 1) // size
        for i in range(2):
            here = [(swapped if i else packs)[p][...] for p in range(parts)]
            q, k, v, d = [
                jnp.concatenate([one[:, j * size : (j + 1) * size] for one in here], axis=1) for j in range(4)
            ]
            q_all[side(i)], d_all[side(i)] = q, d
            rows = slice(i * half, (i + 1) * half)
            k_t[:, rows] = k.astype(jnp.float32).T.astype(jnp.bfloat16)
            v_t[:, rows] = v.astype(jnp.float32).T.astype(jnp.bfloat16)
            for r in range(parts):
                k_of[r, rows] = jnp.where(lane == r, k, 0)
                v_of[r, rows] = jnp.where(lane == r, v, 0)
        for i, ref in enumerate((att_all, dq_all, dk_t, dv_t)):
            ref[...] = earlier[i][...] if begun else jnp.zeros_like(ref)

    first() if steps == 1 else pl.when(step == 0)(first)

    def strip(i):
        at = start + step * blocks + i
        at = chip ^ at if relative else at
        return pl.ds(pl.multiple_of(at * own, own), own)

    for i in range(blocks):
        rows = slice(i * own, (i + 1) * own)
        bias_wide[rows, :half] = mine[i].astype(jnp.float32)
        bias_wide[rows, half:] = other[i].astype(jnp.float32)
        q_now[rows], d_now[rows] = q_all[strip(i)], d_all[strip(i)]
    q, d = q_now[...], d_now[...]
    q_t = q.astype(jnp.float32).T.astype(jnp.bfloat16)
    d_t = d.astype(jnp.float32).T.astype(jnp.bfloat16)

    def scores(r):
        s_now[r % 2] = dot(q, k_of[r], NT)
        p_now[r % 2] = dot(d, v_of[r], NT)

    scores(0)
    for r in range(parts):
        if r + 1 < parts:
            scores(r + 1)
        for at in range(0, blocks * own, ROWS_AT_ONCE):
            rows = slice(at, at + ROWS_AT_ONCE)
            logits = s_now[r % 2, rows] * scaling + bias_wide[rows]
            expo = jnp.exp(logits - jnp.max(logits, axis=-1, keepdims=True))
            probs = expo * (1.0 / jnp.sum(expo, axis=-1, keepdims=True))
            d_probs = p_now[r % 2, rows]
            inner = jnp.sum(probs * d_probs, axis=-1, keepdims=True)
            d_logits = probs * (d_probs - inner)
            low_now[r % 2, rows] = probs.astype(jnp.bfloat16)
            d_low_now[r % 2, rows] = d_logits.astype(jnp.bfloat16)
            if r:
                d_logits = bias_sum[rows] + d_logits
            elif opened:
                d_logits = before[0][rows] + d_logits
            bias_sum[rows] = d_logits
        low, d_low = low_now[r % 2], d_low_now[r % 2]
        cut = slice(r * size, (r + 1) * size)
        att_now[cut] = dot(v_t[cut], low, NT)
        dq_now[cut] = dot(k_t[cut], d_low, NT)
        dk_t[cut] += dot(q_t[cut], d_low)
        dv_t[cut] += dot(d_t[cut], low)
    att_low, dq_low = att_now[...].T.astype(jnp.bfloat16), (dq_now[...] * scaling).T.astype(jnp.bfloat16)
    for i in range(blocks):
        rows = slice(i * own, (i + 1) * own)
        att_all[strip(i)], dq_all[strip(i)] = att_low[rows], dq_low[rows]
        if closed:
            d_bias[0][i] = bias_sum[rows, :half].astype(jnp.bfloat16)
            d_bias[1][i] = bias_sum[rows, half:].astype(jnp.bfloat16)
    if not closed:
        d_bias[0][...] = bias_sum[...]

    def last():
        if not ended:
            for ref, value in zip(results, (att_all, dq_all, dk_t, dv_t)):
                ref[...] = value[...]
            return
        dk = (dk_t[...] * scaling).T.astype(jnp.bfloat16)
        dv = dv_t[...].T.astype(jnp.bfloat16)
        for i in range(2):
            rows = slice(i * half, (i + 1) * half)
            whole = [att_all[side(i)], dq_all[side(i)], dk[rows], dv[rows]]
            for p in range(parts):
                pack = jnp.concatenate([one[:, p * size : (p + 1) * size] for one in whole], axis=1)
                if split and p == 0:
                    results[i][...] = pack
                else:
                    results[p + split][i] = pack

    last() if steps == 1 else pl.when(step == steps - 1)(last)


def fixed(value):
    return pl.BlockSpec(value.shape, lambda i: (0,) * len(value.shape))


def main(packs, swapped, mine, other, earlier, before, scaling, size, start, relative, ended, closed, split):
    parts, (half, width) = len(packs), swapped[0].shape
    strips, own, _ = mine.shape
    blocks, lanes = 4, parts * size
    key_count = queries = 2 * half
    rows = jax.ShapeDtypeStruct((queries, lanes), jnp.bfloat16)
    turned = jax.ShapeDtypeStruct((lanes, key_count), jnp.float32)
    wide = jax.ShapeDtypeStruct((strips * own, key_count), jnp.float32)
    strip = pl.BlockSpec((blocks, own, half), lambda i: (i, 0, 0))
    wide_strip = pl.BlockSpec((blocks * own, key_count), lambda i: (i, 0))
    now = VMEM((blocks * own, lanes), jnp.bfloat16)
    results = [rows, rows, turned, turned]
    if ended:
        ours = [jax.ShapeDtypeStruct((half, width), jnp.bfloat16)] * 2
        results = [jax.ShapeDtypeStruct((2, half, width), jnp.bfloat16)] * (parts - split)
        results = ours * split + results
    d_bias = [mine, other] if closed else [wide]
    grid = {}
    if not relative:
        grid = dict(
            grid=(strips // blocks,),
            in_specs=[fixed(one) for one in [*packs, *swapped]]
            + [strip, strip]
            + [fixed(one) for one in earlier]
            + [wide_strip] * len(before),
            out_specs=([strip] * 2 if closed else [wide_strip]) + [fixed(one) for one in results],
        )
    return pl.pallas_call(
        functools.partial(
            main_kernel, scaling, size, blocks, start, relative, bool(earlier), ended, bool(before), closed, split
        ),
        **grid,
        out_shape=[jax.ShapeDtypeStruct(one.shape, one.dtype) for one in d_bias + results],
        scratch_shapes=[
            VMEM(rows.shape, jnp.bfloat16),
            VMEM(rows.shape, jnp.bfloat16),
            VMEM((parts, key_count, lanes), jnp.bfloat16),
            VMEM((parts, key_count, lanes), jnp.bfloat16),
            VMEM(turned.shape, jnp.float32),
            VMEM(turned.shape, jnp.float32),
            VMEM(rows.shape, jnp.bfloat16),
            VMEM(rows.shape, jnp.bfloat16),
            VMEM((blocks * own, key_count), jnp.float32),
            now,
            now,
            VMEM((2, blocks * own, key_count), jnp.float32),
            VMEM((2, blocks * own, key_count), jnp.float32),
            VMEM((2, blocks * own, key_count), jnp.bfloat16),
            VMEM((2, blocks * own, key_count), jnp.bfloat16),
            VMEM((blocks * own, key_count), jnp.float32),
            VMEM((lanes, key_count), jnp.bfloat16),
            VMEM((lanes, key_count), jnp.bfloat16),
            VMEM((lanes, blocks * own), jnp.float32),
            VMEM((lanes, blocks * own), jnp.float32),
        ],
        compiler_params=PARAMS,
        cost_estimate=pl.CostEstimate(flops=1, bytes_accessed=1, transcendentals=0),
        name="attention",
    )(*packs, *swapped, mine, other, *earlier, *before)


def post_kernel(gate, cot, packs, swapped, d_query, d_keys, d_values, d_gate, held):
    rows, half, channels = gate.shape
    size = channels // 4
    _, near, core = places()
    for s in range(4):
        held[near ^ s, core] = packs[s]
        held[near ^ s, 1 - core] = swapped[s]
    for r in range(rows):
        full = []
        for j in range(4):
            full.append(jnp.concatenate([held[h, r, :, j * size : (j + 1) * size] for h in range(4)], axis=1))
        d_query[r], d_keys[r], d_values[r] = full[1], full[2], full[3]
        sig = jax.nn.sigmoid(gate[r].astype(jnp.float32))
        d_gate[r] = (cot[r].astype(jnp.float32) * full[0].astype(jnp.float32) * sig * (1.0 - sig)).astype(jnp.bfloat16)


def post(gate, cot, packs, swapped):
    return pl.pallas_call(
        post_kernel,
        out_shape=[jax.ShapeDtypeStruct(gate.shape, jnp.bfloat16)] * 4,
        scratch_shapes=[VMEM((4,) + gate.shape, jnp.bfloat16)],
        compiler_params=PARAMS,
        name="unpack",
    )(gate, cot, packs, swapped)


def bias_kernel(*refs):
    near = places()[1]
    for s in range(4):
        refs[4][near ^ s] = refs[s][...].astype(jnp.float32)


def bias_out(pieces):
    return pl.pallas_call(
        bias_kernel,
        out_shape=jax.ShapeDtypeStruct((4,) + pieces[0].shape, jnp.float32),
        compiler_params=PARAMS,
        name="bias_grad",
    )(*pieces)


def shards(query, keys, values, gate_logits, pair_bias, key_mask, grad_out):
    rows, half, channels = query.shape
    heads, own, _ = pair_bias.shape
    size = channels // heads
    scaling = 1.0 / math.sqrt(size)
    far, cores = lax.axis_size("far"), lax.axis_size("key")
    chips = far * PAIR * PAIR
    assert PAIR * PAIR == heads == 4 and rows == cores == 2
    relative = own % 16 == 0
    chip = places()[0]

    def swap(value, axes, s, count):
        return lax.ppermute(value, axes, [(i, i ^ s) for i in range(count)]) if s else value

    def near_swap(value, s):
        return swap(value, ("near", "side"), s, 4)

    def far_swap(value, s):
        return swap(value, "far", s, far)

    def other_core(value):
        return swap(value, "key", 1, 2)

    def wide(value):
        return value.astype(jnp.float32)

    slabs = make_slabs(pair_bias)
    strips = jnp.stack([near_swap(slabs[s], s) for s in range(4)])
    strips = jnp.where(key_mask == 1, strips, jnp.bfloat16(-1000000000.0))
    groups = [far_swap(strips, f) for f in range(far)]
    *packs, kept, spare = make_packs(query, keys, values, gate_logits, grad_out)
    packs = [near_swap(packs[s], s + 1) for s in range(3)]
    starts = [f * 4 for f in range(far)]
    if not relative:
        starts, groups = [0], [jnp.concatenate(groups)[chip ^ jnp.arange(chips)].reshape(8, -1, half)]
    others = [jnp.concatenate([other_core(part) for part in jnp.split(groups[0], NEAR_PARTS)])] + [None] * (len(starts) - 1)
    orders = [list(range(len(starts))), list(range(len(starts)))[::-1]]
    before, sums, returned = [[]] * len(starts), [None] * len(starts), []
    for a, order in enumerate(orders):
        ours = [packs[0]] if a == 0 else packs[1:]
        if a:
            ours = list(lax.optimization_barrier((*ours, before[0][0]))[:2])
        swapped = [other_core(pack[1]) for pack in ours]
        ours = [pack[0] for pack in ours]
        if a == 0:
            spare = lax.optimization_barrier((spare, ours[0]))[0]
            ours, swapped = [kept] + ours, [other_core(spare)] + swapped
        earlier = []
        for g in order:
            if others[g] is None:
                groups[g] = lax.optimization_barrier((groups[g], before[0][0]))[0]
                others[g] = other_core(groups[g])
            mine, closed, ended = groups[g], a == len(orders) - 1, g == order[-1]
            if closed and g != order[0]:
                mine, last = lax.optimization_barrier((mine, sums[order[order.index(g) - 1]]))
                sums[order[order.index(g) - 1]] = last
            out = main(
                ours, swapped, mine, others[g], earlier, before[g], scaling, size, starts[g], relative, ended, closed, 1 - a
            )
            if not closed:
                before[g], earlier = out[:1], out[1:]
                continue
            d_mine, d_other, *earlier = out
            d_mine = wide(d_mine)
            if ended and relative:
                for f in range(1, far):
                    d_mine = d_mine + wide(far_swap(sums[f], f))
                d_mine = lax.optimization_barrier(d_mine)
            sums[g] = (d_mine + wide(other_core(d_other))).astype(jnp.bfloat16)
        if a == 0:
            stay, pass_on, *earlier = earlier
        returned += [near_swap(value, len(returned) + i + 1) for i, value in enumerate(earlier)]
    d_sum = sums[0]
    if not relative:
        d_sum = d_sum.reshape(chips, own, half)[chip ^ jnp.arange(chips)]
        total = wide(d_sum[:4])
        for f in range(1, far):
            total = total + wide(far_swap(d_sum[4 * f : 4 * f + 4], f))
        d_sum = total.astype(jnp.bfloat16)
    pieces = [near_swap(d_sum[s], s) for s in range(4)]
    returned = lax.optimization_barrier((*returned, *pieces))[:3]
    swapped = other_core(jnp.stack([pass_on] + [pack[1] for pack in returned]))
    packs = jnp.stack([stay] + [pack[0] for pack in returned])
    return (*post(gate_logits, grad_out, packs, swapped), bias_out(pieces))


def solution(mesh):
    groups, rows, cores = mesh.devices.shape
    devices = mesh.devices.reshape(groups, rows // PAIR**2, PAIR, PAIR, cores)
    mesh = jax.sharding.Mesh(devices, ("grp", "far", "near", "side", "key"))
    split = ("grp", "far", "near", "side")
    tokens = P(split, "key", None)
    pair = P(None, split, "key")
    in_specs = (tokens, tokens, tokens, tokens, pair, P(("grp", "key")), tokens)
    out_specs = (tokens, tokens, tokens, tokens, pair)
    return jax.shard_map(shards, mesh=mesh, in_specs=in_specs, out_specs=out_specs, check_vma=False)
```

```python
import functools
import math

import jax
import jax.numpy as jnp
from jax import lax
from jax.experimental import pallas as pl
from jax.experimental.pallas import tpu as pltpu
from jax.sharding import PartitionSpec as P

PAIR = 2
NEAR_PARTS = 2
ROWS_AT_ONCE = 32
VMEM = pltpu.VMEM
PARAMS = pltpu.CompilerParams(vmem_limit_bytes=32 * 1024 * 1024)
PRE_PARAMS = pltpu.CompilerParams(vmem_limit_bytes=60 * 1024 * 1024)


def places():
    near = lax.axis_index("near") * PAIR + lax.axis_index("side")
    return lax.axis_index("far") * PAIR * PAIR + near, near, lax.axis_index("key")


def fetch(pairs, sems):
    copies = [pltpu.make_async_copy(ref, buffer, sems.at[i]) for i, (ref, buffer) in enumerate(pairs)]
    for copy in copies:
        copy.start()
    for copy in copies:
        copy.wait()


def slab_kernel(bias, *slabs):
    near = places()[1]
    for s in range(4):
        slabs[s][...] = bias[near ^ s]


def make_slabs(bias):
    return pl.pallas_call(
        slab_kernel,
        out_shape=[jax.ShapeDtypeStruct(bias.shape[1:], jnp.bfloat16)] * 4,
        compiler_params=PARAMS,
        name="bias_by_head",
    )(bias)


def pack_kernel(*refs):
    inputs, packs, kept, buffers, (sems, held) = refs[:5], refs[5:8], refs[8:10], refs[10:15], refs[15:]
    fetch(list(zip(inputs, buffers)), sems)
    query, keys, values, gate, cot = buffers
    rows = query.shape[0]
    size = query.shape[2] // 4
    _, near, core = places()
    for r in range(rows):
        upstream = (cot[r].astype(jnp.float32) * jax.nn.sigmoid(gate[r].astype(jnp.float32))).astype(jnp.bfloat16)
        whole = [query[r], keys[r], values[r], upstream]
        for head in range(4):
            held[head, r] = jnp.concatenate([one[:, head * size : (head + 1) * size] for one in whole], axis=1)
    for i in range(2):
        for s in range(1, 4):
            packs[s - 1][i] = held[near ^ s, core ^ i]
        kept[i][...] = held[near, core ^ i]


def make_packs(*inputs):
    one = inputs[0]
    return pl.pallas_call(
        pack_kernel,
        in_specs=[pl.BlockSpec(memory_space=pl.ANY)] * 5,
        out_shape=[jax.ShapeDtypeStruct(one.shape, jnp.bfloat16)] * 3
        + [jax.ShapeDtypeStruct(one.shape[1:], jnp.bfloat16)] * 2,
        scratch_shapes=[VMEM(one.shape, jnp.bfloat16)] * 5
        + [pltpu.SemaphoreType.DMA((5,)), VMEM((4,) + one.shape, jnp.bfloat16)],
        compiler_params=PRE_PARAMS,
        name="pack",
    )(*inputs)


NT = (((1,), (1,)), ((), ()))


def dot(a, b, dims=(((1,), (0,)), ((), ()))):
    return lax.dot_general(a, b, dims, preferred_element_type=jnp.float32)


def main_kernel(scaling, size, blocks, start, relative, begun, ended, opened, closed, split, *refs):
    packs, swapped, (mine, other), refs = refs[:2], refs[2:4], refs[4:6], refs[6:]
    earlier, refs = refs[: 4 if begun else 0], refs[4 if begun else 0 :]
    before, refs = refs[: 1 if opened else 0], refs[1 if opened else 0 :]
    d_bias, refs = refs[: 2 if closed else 1], refs[2 if closed else 1 :]
    results, refs = refs[: 2 + split if ended else 4], refs[2 + split if ended else 4 :]
    q_all, d_all, k_of, v_of, dk_t, dv_t, att_all, dq_all, bias_wide, q_now, d_now, s_now, p_now, low_now, d_low_now, bias_sum = refs
    steps = q_all.shape[0] // (blocks * mine.shape[1]) if not relative else 1
    step = pl.program_id(0) if steps > 1 else 0
    chip, _, core = places()
    parts, (half, _) = len(packs), packs[0].shape
    own = mine.shape[1]
    lanes = parts * size

    def side(i):
        return pl.ds(pl.multiple_of((core ^ i) * half, half), half)

    def first():
        lane = lax.broadcasted_iota(jnp.int32, (half, lanes), 1) // size
        for i in range(2):
            here = [(swapped if i else packs)[p][...] for p in range(parts)]
            q, k, v, d = [
                jnp.concatenate([one[:, j * size : (j + 1) * size] for one in here], axis=1) for j in range(4)
            ]
            q_all[side(i)], d_all[side(i)] = q, d
            rows = slice(i * half, (i + 1) * half)
            for r in range(parts):
                k_of[r, rows] = jnp.where(lane == r, k, 0)
                v_of[r, rows] = jnp.where(lane == r, v, 0)
        for i, ref in enumerate((att_all, dq_all, dk_t, dv_t)):
            ref[...] = earlier[i][...] if begun else jnp.zeros_like(ref)

    first() if steps == 1 else pl.when(step == 0)(first)

    def strip(i):
        at = start + step * blocks + i
        at = chip ^ at if relative else at
        return pl.ds(pl.multiple_of(at * own, own), own)

    for i in range(blocks):
        rows = slice(i * own, (i + 1) * own)
        bias_wide[rows, :half] = mine[i].astype(jnp.float32)
        bias_wide[rows, half:] = other[i].astype(jnp.float32)
        q_now[rows], d_now[rows] = q_all[strip(i)], d_all[strip(i)]
    q, d = q_now[...], d_now[...]
    q_t = q.astype(jnp.float32).T.astype(jnp.bfloat16)
    d_t = d.astype(jnp.float32).T.astype(jnp.bfloat16)

    def scores(r):
        s_now[r % 2] = dot(q, k_of[r], NT)
        p_now[r % 2] = dot(d, v_of[r], NT)

    att_sum, dq_sum = None, None
    scores(0)
    for r in range(parts):
        if r + 1 < parts:
            scores(r + 1)
        for at in range(0, blocks * own, ROWS_AT_ONCE):
            rows = slice(at, at + ROWS_AT_ONCE)
            logits = s_now[r % 2, rows] * scaling + bias_wide[rows]
            expo = jnp.exp(logits - jnp.max(logits, axis=-1, keepdims=True))
            d_probs = p_now[r % 2, rows]
            inverse = 1.0 / jnp.sum(expo, axis=-1, keepdims=True)
            inner = jnp.sum(expo * d_probs, axis=-1, keepdims=True) * inverse
            probs = expo * inverse
            d_logits = probs * (d_probs - inner)
            low_now[r % 2, rows] = probs.astype(jnp.bfloat16)
            d_low_now[r % 2, rows] = d_logits.astype(jnp.bfloat16)
            if r:
                d_logits = bias_sum[rows] + d_logits
            elif opened:
                d_logits = before[0][rows] + d_logits
            bias_sum[rows] = d_logits
        low, d_low = low_now[r % 2], d_low_now[r % 2]
        att, dq = dot(low, v_of[r]), dot(d_low, k_of[r])
        cut = slice(r * size, (r + 1) * size)
        dk_t[cut] += dot(q_t[cut], d_low)
        dv_t[cut] += dot(d_t[cut], low)
        att_sum = att if r == 0 else att_sum + att
        dq_sum = dq if r == 0 else dq_sum + dq
    att_low, dq_low = att_sum.astype(jnp.bfloat16), (dq_sum * scaling).astype(jnp.bfloat16)
    for i in range(blocks):
        rows = slice(i * own, (i + 1) * own)
        att_all[strip(i)], dq_all[strip(i)] = att_low[rows], dq_low[rows]
        if closed:
            d_bias[0][i] = bias_sum[rows, :half].astype(jnp.bfloat16)
            d_bias[1][i] = bias_sum[rows, half:].astype(jnp.bfloat16)
    if not closed:
        d_bias[0][...] = bias_sum[...]

    def last():
        if not ended:
            for ref, value in zip(results, (att_all, dq_all, dk_t, dv_t)):
                ref[...] = value[...]
            return
        dk = (dk_t[...] * scaling).T.astype(jnp.bfloat16)
        dv = dv_t[...].T.astype(jnp.bfloat16)
        for i in range(2):
            rows = slice(i * half, (i + 1) * half)
            whole = [att_all[side(i)], dq_all[side(i)], dk[rows], dv[rows]]
            for p in range(parts):
                pack = jnp.concatenate([one[:, p * size : (p + 1) * size] for one in whole], axis=1)
                if split and p == 0:
                    results[i][...] = pack
                else:
                    results[p + split][i] = pack

    last() if steps == 1 else pl.when(step == steps - 1)(last)


def fixed(value):
    return pl.BlockSpec(value.shape, lambda i: (0,) * len(value.shape))


def main(packs, swapped, mine, other, earlier, before, scaling, size, start, relative, ended, closed, split):
    parts, (half, width) = len(packs), swapped[0].shape
    strips, own, _ = mine.shape
    blocks, lanes = 4, parts * size
    key_count = queries = 2 * half
    rows = jax.ShapeDtypeStruct((queries, lanes), jnp.bfloat16)
    turned = jax.ShapeDtypeStruct((lanes, key_count), jnp.float32)
    wide = jax.ShapeDtypeStruct((strips * own, key_count), jnp.float32)
    strip = pl.BlockSpec((blocks, own, half), lambda i: (i, 0, 0))
    wide_strip = pl.BlockSpec((blocks * own, key_count), lambda i: (i, 0))
    now = VMEM((blocks * own, lanes), jnp.bfloat16)
    results = [rows, rows, turned, turned]
    if ended:
        ours = [jax.ShapeDtypeStruct((half, width), jnp.bfloat16)] * 2
        results = [jax.ShapeDtypeStruct((2, half, width), jnp.bfloat16)] * (parts - split)
        results = ours * split + results
    d_bias = [mine, other] if closed else [wide]
    grid = {}
    if not relative:
        grid = dict(
            grid=(strips // blocks,),
            in_specs=[fixed(one) for one in [*packs, *swapped]]
            + [strip, strip]
            + [fixed(one) for one in earlier]
            + [wide_strip] * len(before),
            out_specs=([strip] * 2 if closed else [wide_strip]) + [fixed(one) for one in results],
        )
    return pl.pallas_call(
        functools.partial(
            main_kernel, scaling, size, blocks, start, relative, bool(earlier), ended, bool(before), closed, split
        ),
        **grid,
        out_shape=[jax.ShapeDtypeStruct(one.shape, one.dtype) for one in d_bias + results],
        scratch_shapes=[
            VMEM(rows.shape, jnp.bfloat16),
            VMEM(rows.shape, jnp.bfloat16),
            VMEM((parts, key_count, lanes), jnp.bfloat16),
            VMEM((parts, key_count, lanes), jnp.bfloat16),
            VMEM(turned.shape, jnp.float32),
            VMEM(turned.shape, jnp.float32),
            VMEM(rows.shape, jnp.bfloat16),
            VMEM(rows.shape, jnp.bfloat16),
            VMEM((blocks * own, key_count), jnp.float32),
            now,
            now,
            VMEM((2, blocks * own, key_count), jnp.float32),
            VMEM((2, blocks * own, key_count), jnp.float32),
            VMEM((2, blocks * own, key_count), jnp.bfloat16),
            VMEM((2, blocks * own, key_count), jnp.bfloat16),
            VMEM((blocks * own, key_count), jnp.float32),
        ],
        compiler_params=PARAMS,
        cost_estimate=pl.CostEstimate(flops=1, bytes_accessed=1, transcendentals=0),
        name="attention",
    )(*packs, *swapped, mine, other, *earlier, *before)


def post_kernel(gate, cot, packs, swapped, d_query, d_keys, d_values, d_gate, held):
    rows, half, channels = gate.shape
    size = channels // 4
    _, near, core = places()
    for s in range(4):
        held[near ^ s, core] = packs[s]
        held[near ^ s, 1 - core] = swapped[s]
    for r in range(rows):
        full = []
        for j in range(4):
            full.append(jnp.concatenate([held[h, r, :, j * size : (j + 1) * size] for h in range(4)], axis=1))
        d_query[r], d_keys[r], d_values[r] = full[1], full[2], full[3]
        sig = jax.nn.sigmoid(gate[r].astype(jnp.float32))
        d_gate[r] = (cot[r].astype(jnp.float32) * full[0].astype(jnp.float32) * sig * (1.0 - sig)).astype(jnp.bfloat16)


def post(gate, cot, packs, swapped):
    return pl.pallas_call(
        post_kernel,
        out_shape=[jax.ShapeDtypeStruct(gate.shape, jnp.bfloat16)] * 4,
        scratch_shapes=[VMEM((4,) + gate.shape, jnp.bfloat16)],
        compiler_params=PARAMS,
        name="unpack",
    )(gate, cot, packs, swapped)


def bias_kernel(*refs):
    near = places()[1]
    for s in range(4):
        refs[4][near ^ s] = refs[s][...].astype(jnp.float32)


def bias_out(pieces):
    return pl.pallas_call(
        bias_kernel,
        out_shape=jax.ShapeDtypeStruct((4,) + pieces[0].shape, jnp.float32),
        compiler_params=PARAMS,
        name="bias_grad",
    )(*pieces)


def shards(query, keys, values, gate_logits, pair_bias, key_mask, grad_out):
    rows, half, channels = query.shape
    heads, own, _ = pair_bias.shape
    size = channels // heads
    scaling = 1.0 / math.sqrt(size)
    far, cores = lax.axis_size("far"), lax.axis_size("key")
    chips = far * PAIR * PAIR
    assert PAIR * PAIR == heads == 4 and rows == cores == 2
    relative = own % 16 == 0
    chip = places()[0]

    def swap(value, axes, s, count):
        return lax.ppermute(value, axes, [(i, i ^ s) for i in range(count)]) if s else value

    def near_swap(value, s):
        return swap(value, ("near", "side"), s, 4)

    def far_swap(value, s):
        return swap(value, "far", s, far)

    def other_core(value):
        return swap(value, "key", 1, 2)

    def wide(value):
        return value.astype(jnp.float32)

    slabs = make_slabs(pair_bias)
    strips = jnp.stack([near_swap(slabs[s], s) for s in range(4)])
    strips = jnp.where(key_mask == 1, strips, jnp.bfloat16(-1000000000.0))
    groups = [far_swap(strips, f) for f in range(far)]
    *packs, kept, spare = make_packs(query, keys, values, gate_logits, grad_out)
    packs = [near_swap(packs[s], s + 1) for s in range(3)]
    starts = [f * 4 for f in range(far)]
    if not relative:
        starts, groups = [0], [jnp.concatenate(groups)[chip ^ jnp.arange(chips)].reshape(8, -1, half)]
    others = [jnp.concatenate([other_core(part) for part in jnp.split(groups[0], NEAR_PARTS)])] + [None] * (len(starts) - 1)
    orders = [list(range(len(starts))), list(range(len(starts)))[::-1]]
    before, sums, returned = [[]] * len(starts), [None] * len(starts), []
    for a, order in enumerate(orders):
        ours = [packs[0]] if a == 0 else packs[1:]
        if a:
            ours = list(lax.optimization_barrier((*ours, before[0][0]))[:2])
        swapped = [other_core(pack[1]) for pack in ours]
        ours = [pack[0] for pack in ours]
        if a == 0:
            spare = lax.optimization_barrier((spare, ours[0]))[0]
            ours, swapped = [kept] + ours, [other_core(spare)] + swapped
        earlier = []
        for g in order:
            if others[g] is None:
                groups[g] = lax.optimization_barrier((groups[g], before[0][0]))[0]
                others[g] = other_core(groups[g])
            mine, closed, ended = groups[g], a == len(orders) - 1, g == order[-1]
            if closed and g != order[0]:
                mine, last = lax.optimization_barrier((mine, sums[order[order.index(g) - 1]]))
                sums[order[order.index(g) - 1]] = last
            out = main(
                ours, swapped, mine, others[g], earlier, before[g], scaling, size, starts[g], relative, ended, closed, 1 - a
            )
            if not closed:
                before[g], earlier = out[:1], out[1:]
                continue
            d_mine, d_other, *earlier = out
            d_mine = wide(d_mine)
            if ended and relative:
                for f in range(1, far):
                    d_mine = d_mine + wide(far_swap(sums[f], f))
                d_mine = lax.optimization_barrier(d_mine)
            sums[g] = (d_mine + wide(other_core(d_other))).astype(jnp.bfloat16)
        if a == 0:
            stay, pass_on, *earlier = earlier
        returned += [near_swap(value, len(returned) + i + 1) for i, value in enumerate(earlier)]
    d_sum = sums[0]
    if not relative:
        d_sum = d_sum.reshape(chips, own, half)[chip ^ jnp.arange(chips)]
        total = wide(d_sum[:4])
        for f in range(1, far):
            total = total + wide(far_swap(d_sum[4 * f : 4 * f + 4], f))
        d_sum = total.astype(jnp.bfloat16)
    pieces = [near_swap(d_sum[s], s) for s in range(4)]
    returned = lax.optimization_barrier((*returned, *pieces))[:3]
    swapped = other_core(jnp.stack([pass_on] + [pack[1] for pack in returned]))
    packs = jnp.stack([stay] + [pack[0] for pack in returned])
    return (*post(gate_logits, grad_out, packs, swapped), bias_out(pieces))


def solution(mesh):
    groups, rows, cores = mesh.devices.shape
    devices = mesh.devices.reshape(groups, rows // PAIR**2, PAIR, PAIR, cores)
    mesh = jax.sharding.Mesh(devices, ("grp", "far", "near", "side", "key"))
    split = ("grp", "far", "near", "side")
    tokens = P(split, "key", None)
    pair = P(None, split, "key")
    in_specs = (tokens, tokens, tokens, tokens, pair, P(("grp", "key")), tokens)
    out_specs = (tokens, tokens, tokens, tokens, pair)
    return jax.shard_map(shards, mesh=mesh, in_specs=in_specs, out_specs=out_specs, check_vma=False)
```

```python
import functools
import math

import jax
import jax.numpy as jnp
from jax import lax
from jax.experimental import pallas as pl
from jax.experimental.pallas import tpu as pltpu
from jax.sharding import PartitionSpec as P

PAIR = 2
NEAR_PARTS = 2
SENT = (2, 3, 1)
ROWS_AT_ONCE = 16
VMEM = pltpu.VMEM
PARAMS = pltpu.CompilerParams(vmem_limit_bytes=32 * 1024 * 1024)
PRE_PARAMS = pltpu.CompilerParams(vmem_limit_bytes=60 * 1024 * 1024)


def places():
    near = lax.axis_index("near") * PAIR + lax.axis_index("side")
    return lax.axis_index("far") * PAIR * PAIR + near, near, lax.axis_index("key")


def fetch(pairs, sems):
    copies = [pltpu.make_async_copy(ref, buffer, sems.at[i]) for i, (ref, buffer) in enumerate(pairs)]
    for copy in copies:
        copy.start()
    for copy in copies:
        copy.wait()


def slab_kernel(bias, *slabs):
    near = places()[1]
    for s in range(4):
        slabs[s][...] = bias[near ^ s]


def make_slabs(bias):
    return pl.pallas_call(
        slab_kernel,
        out_shape=[jax.ShapeDtypeStruct(bias.shape[1:], jnp.bfloat16)] * 4,
        compiler_params=PARAMS,
        name="bias_by_head",
    )(bias)


def pack_kernel(*refs):
    inputs, packs, kept, buffers, (sems, held) = refs[:5], refs[5:8], refs[8:10], refs[10:15], refs[15:]
    fetch(list(zip(inputs, buffers)), sems)
    query, keys, values, gate, cot = buffers
    rows = query.shape[0]
    size = query.shape[2] // 4
    _, near, core = places()
    for r in range(rows):
        upstream = (cot[r].astype(jnp.float32) * jax.nn.sigmoid(gate[r].astype(jnp.float32))).astype(jnp.bfloat16)
        whole = [query[r], keys[r], values[r], upstream]
        for head in range(4):
            held[head, r] = jnp.concatenate([one[:, head * size : (head + 1) * size] for one in whole], axis=1)
    for i in range(2):
        for s in range(1, 4):
            packs[s - 1][i] = held[near ^ s, core ^ i]
        kept[i][...] = held[near, core ^ i]


def make_packs(*inputs):
    one = inputs[0]
    return pl.pallas_call(
        pack_kernel,
        in_specs=[pl.BlockSpec(memory_space=pl.ANY)] * 5,
        out_shape=[jax.ShapeDtypeStruct(one.shape, jnp.bfloat16)] * 3
        + [jax.ShapeDtypeStruct(one.shape[1:], jnp.bfloat16)] * 2,
        scratch_shapes=[VMEM(one.shape, jnp.bfloat16)] * 5
        + [pltpu.SemaphoreType.DMA((5,)), VMEM((4,) + one.shape, jnp.bfloat16)],
        compiler_params=PRE_PARAMS,
        name="pack",
    )(*inputs)


NT = (((1,), (1,)), ((), ()))


def dot(a, b, dims=(((1,), (0,)), ((), ()))):
    return lax.dot_general(a, b, dims, preferred_element_type=jnp.float32)


def main_kernel(scaling, size, blocks, start, relative, begun, ended, opened, closed, split, *refs):
    packs, swapped, (mine, other), refs = refs[:2], refs[2:4], refs[4:6], refs[6:]
    earlier, refs = refs[: 4 if begun else 0], refs[4 if begun else 0 :]
    before, refs = refs[: 1 if opened else 0], refs[1 if opened else 0 :]
    d_bias, refs = refs[: 2 if closed else 1], refs[2 if closed else 1 :]
    results, refs = refs[: 2 + split if ended else 4], refs[2 + split if ended else 4 :]
    q_all, d_all, k_of, v_of, dk_t, dv_t, att_all, dq_all, bias_wide, q_now, d_now, s_now, p_now, low_now, d_low_now, bias_sum = refs
    steps = q_all.shape[0] // (blocks * mine.shape[1]) if not relative else 1
    step = pl.program_id(0) if steps > 1 else 0
    chip, _, core = places()
    parts, (half, _) = len(packs), packs[0].shape
    own = mine.shape[1]
    lanes = parts * size

    def side(i):
        return pl.ds(pl.multiple_of((core ^ i) * half, half), half)

    def first():
        lane = lax.broadcasted_iota(jnp.int32, (half, lanes), 1) // size
        for i in range(2):
            here = [(swapped if i else packs)[p][...] for p in range(parts)]
            q, k, v, d = [
                jnp.concatenate([one[:, j * size : (j + 1) * size] for one in here], axis=1) for j in range(4)
            ]
            q_all[side(i)], d_all[side(i)] = q, d
            rows = slice(i * half, (i + 1) * half)
            for r in range(parts):
                k_of[r, rows] = jnp.where(lane == r, k, 0)
                v_of[r, rows] = jnp.where(lane == r, v, 0)
        for i, ref in enumerate((att_all, dq_all, dk_t, dv_t)):
            ref[...] = earlier[i][...] if begun else jnp.zeros_like(ref)

    first() if steps == 1 else pl.when(step == 0)(first)

    def strip(i):
        at = start + step * blocks + i
        at = chip ^ at if relative else at
        return pl.ds(pl.multiple_of(at * own, own), own)

    for i in range(blocks):
        rows = slice(i * own, (i + 1) * own)
        bias_wide[rows, :half] = mine[i].astype(jnp.float32)
        bias_wide[rows, half:] = other[i].astype(jnp.float32)
        q_now[rows], d_now[rows] = q_all[strip(i)], d_all[strip(i)]
    q, d = q_now[...], d_now[...]
    q_t = q.astype(jnp.float32).T.astype(jnp.bfloat16)
    d_t = d.astype(jnp.float32).T.astype(jnp.bfloat16)

    def scores(r):
        s_now[r % 2] = dot(q, k_of[r], NT)
        p_now[r % 2] = dot(d, v_of[r], NT)

    att_sum, dq_sum = None, None
    scores(0)
    for r in range(parts):
        if r + 1 < parts:
            scores(r + 1)
        for at in range(0, blocks * own, ROWS_AT_ONCE):
            rows = slice(at, at + ROWS_AT_ONCE)
            logits = s_now[r % 2, rows] * scaling + bias_wide[rows]
            expo = jnp.exp(logits - jnp.max(logits, axis=-1, keepdims=True))
            probs = expo * (1.0 / jnp.sum(expo, axis=-1, keepdims=True))
            d_probs = p_now[r % 2, rows]
            inner = jnp.sum(probs * d_probs, axis=-1, keepdims=True)
            d_logits = probs * (d_probs - inner)
            low_now[r % 2, rows] = probs.astype(jnp.bfloat16)
            d_low_now[r % 2, rows] = d_logits.astype(jnp.bfloat16)
            if r:
                d_logits = bias_sum[rows] + d_logits
            elif opened:
                d_logits = before[0][rows] + d_logits
            bias_sum[rows] = d_logits
        low, d_low = low_now[r % 2], d_low_now[r % 2]
        att, dq = dot(low, v_of[r]), dot(d_low, k_of[r])
        cut = slice(r * size, (r + 1) * size)
        dk_t[cut] += dot(q_t[cut], d_low)
        dv_t[cut] += dot(d_t[cut], low)
        att_sum = att if r == 0 else att_sum + att
        dq_sum = dq if r == 0 else dq_sum + dq
    att_low, dq_low = att_sum.astype(jnp.bfloat16), (dq_sum * scaling).astype(jnp.bfloat16)
    for i in range(blocks):
        rows = slice(i * own, (i + 1) * own)
        att_all[strip(i)], dq_all[strip(i)] = att_low[rows], dq_low[rows]
        if closed:
            d_bias[0][i] = bias_sum[rows, :half].astype(jnp.bfloat16)
            d_bias[1][i] = bias_sum[rows, half:].astype(jnp.bfloat16)
    if not closed:
        d_bias[0][...] = bias_sum[...]

    def last():
        if not ended:
            for ref, value in zip(results, (att_all, dq_all, dk_t, dv_t)):
                ref[...] = value[...]
            return
        dk = (dk_t[...] * scaling).T.astype(jnp.bfloat16)
        dv = dv_t[...].T.astype(jnp.bfloat16)
        for i in range(2):
            rows = slice(i * half, (i + 1) * half)
            whole = [att_all[side(i)], dq_all[side(i)], dk[rows], dv[rows]]
            for p in range(parts):
                pack = jnp.concatenate([one[:, p * size : (p + 1) * size] for one in whole], axis=1)
                if split and p == 0:
                    results[i][...] = pack
                else:
                    results[p + split][i] = pack

    last() if steps == 1 else pl.when(step == steps - 1)(last)


def fixed(value):
    return pl.BlockSpec(value.shape, lambda i: (0,) * len(value.shape))


def main(packs, swapped, mine, other, earlier, before, scaling, size, start, relative, ended, closed, split):
    parts, (half, width) = len(packs), swapped[0].shape
    strips, own, _ = mine.shape
    blocks, lanes = 4, parts * size
    key_count = queries = 2 * half
    rows = jax.ShapeDtypeStruct((queries, lanes), jnp.bfloat16)
    turned = jax.ShapeDtypeStruct((lanes, key_count), jnp.float32)
    wide = jax.ShapeDtypeStruct((strips * own, key_count), jnp.float32)
    strip = pl.BlockSpec((blocks, own, half), lambda i: (i, 0, 0))
    wide_strip = pl.BlockSpec((blocks * own, key_count), lambda i: (i, 0))
    now = VMEM((blocks * own, lanes), jnp.bfloat16)
    results = [rows, rows, turned, turned]
    if ended:
        ours = [jax.ShapeDtypeStruct((half, width), jnp.bfloat16)] * 2
        results = [jax.ShapeDtypeStruct((2, half, width), jnp.bfloat16)] * (parts - split)
        results = ours * split + results
    d_bias = [mine, other] if closed else [wide]
    grid = {}
    if not relative:
        grid = dict(
            grid=(strips // blocks,),
            in_specs=[fixed(one) for one in [*packs, *swapped]]
            + [strip, strip]
            + [fixed(one) for one in earlier]
            + [wide_strip] * len(before),
            out_specs=([strip] * 2 if closed else [wide_strip]) + [fixed(one) for one in results],
        )
    return pl.pallas_call(
        functools.partial(
            main_kernel, scaling, size, blocks, start, relative, bool(earlier), ended, bool(before), closed, split
        ),
        **grid,
        out_shape=[jax.ShapeDtypeStruct(one.shape, one.dtype) for one in d_bias + results],
        scratch_shapes=[
            VMEM(rows.shape, jnp.bfloat16),
            VMEM(rows.shape, jnp.bfloat16),
            VMEM((parts, key_count, lanes), jnp.bfloat16),
            VMEM((parts, key_count, lanes), jnp.bfloat16),
            VMEM(turned.shape, jnp.float32),
            VMEM(turned.shape, jnp.float32),
            VMEM(rows.shape, jnp.bfloat16),
            VMEM(rows.shape, jnp.bfloat16),
            VMEM((blocks * own, key_count), jnp.float32),
            now,
            now,
            VMEM((2, blocks * own, key_count), jnp.float32),
            VMEM((2, blocks * own, key_count), jnp.float32),
            VMEM((2, blocks * own, key_count), jnp.bfloat16),
            VMEM((2, blocks * own, key_count), jnp.bfloat16),
            VMEM((blocks * own, key_count), jnp.float32),
        ],
        compiler_params=PARAMS,
        cost_estimate=pl.CostEstimate(flops=1, bytes_accessed=1, transcendentals=0),
        name="attention",
    )(*packs, *swapped, mine, other, *earlier, *before)


def post_kernel(gate, cot, packs, swapped, d_query, d_keys, d_values, d_gate, held):
    rows, half, channels = gate.shape
    size = channels // 4
    _, near, core = places()
    for i, s in enumerate((0, *SENT)):
        held[near ^ s, core] = packs[i]
        held[near ^ s, 1 - core] = swapped[i]
    for r in range(rows):
        full = []
        for j in range(4):
            full.append(jnp.concatenate([held[h, r, :, j * size : (j + 1) * size] for h in range(4)], axis=1))
        d_query[r], d_keys[r], d_values[r] = full[1], full[2], full[3]
        sig = jax.nn.sigmoid(gate[r].astype(jnp.float32))
        d_gate[r] = (cot[r].astype(jnp.float32) * full[0].astype(jnp.float32) * sig * (1.0 - sig)).astype(jnp.bfloat16)


def post(gate, cot, packs, swapped):
    return pl.pallas_call(
        post_kernel,
        out_shape=[jax.ShapeDtypeStruct(gate.shape, jnp.bfloat16)] * 4,
        scratch_shapes=[VMEM((4,) + gate.shape, jnp.bfloat16)],
        compiler_params=PARAMS,
        name="unpack",
    )(gate, cot, packs, swapped)


def bias_kernel(*refs):
    near = places()[1]
    for s in range(4):
        refs[4][near ^ s] = refs[s][...].astype(jnp.float32)


def bias_out(pieces):
    return pl.pallas_call(
        bias_kernel,
        out_shape=jax.ShapeDtypeStruct((4,) + pieces[0].shape, jnp.float32),
        compiler_params=PARAMS,
        name="bias_grad",
    )(*pieces)


def shards(query, keys, values, gate_logits, pair_bias, key_mask, grad_out):
    rows, half, channels = query.shape
    heads, own, _ = pair_bias.shape
    size = channels // heads
    scaling = 1.0 / math.sqrt(size)
    far, cores = lax.axis_size("far"), lax.axis_size("key")
    chips = far * PAIR * PAIR
    assert PAIR * PAIR == heads == 4 and rows == cores == 2
    relative = own % 16 == 0
    chip = places()[0]

    def swap(value, axes, s, count):
        return lax.ppermute(value, axes, [(i, i ^ s) for i in range(count)]) if s else value

    def near_swap(value, s):
        return swap(value, ("near", "side"), s, 4)

    def far_swap(value, s):
        return swap(value, "far", s, far)

    def other_core(value):
        return swap(value, "key", 1, 2)

    def wide(value):
        return value.astype(jnp.float32)

    slabs = make_slabs(pair_bias)
    strips = jnp.stack([near_swap(slabs[s], s) for s in range(4)])
    strips = jnp.where(key_mask == 1, strips, jnp.bfloat16(-1000000000.0))
    groups = [far_swap(strips, f) for f in range(far)]
    *packs, kept, spare = make_packs(query, keys, values, gate_logits, grad_out)
    packs = [near_swap(packs[s], s + 1) for s in range(3)]
    starts = [f * 4 for f in range(far)]
    if not relative:
        starts, groups = [0], [jnp.concatenate(groups)[chip ^ jnp.arange(chips)].reshape(8, -1, half)]
    others = [jnp.concatenate([other_core(part) for part in jnp.split(groups[0], NEAR_PARTS)])] + [None] * (len(starts) - 1)
    orders = [list(range(len(starts))), list(range(len(starts)))[::-1]]
    before, sums, returned = [[]] * len(starts), [None] * len(starts), []
    for a, order in enumerate(orders):
        ours = [packs[0]] if a == 0 else packs[1:]
        if a:
            ours = list(lax.optimization_barrier((*ours, before[0][0]))[:2])
        swapped = [other_core(pack[1]) for pack in ours]
        ours = [pack[0] for pack in ours]
        if a == 0:
            spare = lax.optimization_barrier((spare, ours[0]))[0]
            ours, swapped = [kept] + ours, [other_core(spare)] + swapped
        earlier = []
        for g in order:
            if others[g] is None:
                groups[g] = lax.optimization_barrier((groups[g], before[0][0]))[0]
                others[g] = other_core(groups[g])
            mine, closed, ended = groups[g], a == len(orders) - 1, g == order[-1]
            if closed and g != order[0]:
                mine, last = lax.optimization_barrier((mine, sums[order[order.index(g) - 1]]))
                sums[order[order.index(g) - 1]] = last
            out = main(
                ours, swapped, mine, others[g], earlier, before[g], scaling, size, starts[g], relative, ended, closed, 1 - a
            )
            if not closed:
                before[g], earlier = out[:1], out[1:]
                continue
            d_mine, d_other, *earlier = out
            d_mine = wide(d_mine)
            if ended and relative:
                for f in range(1, far):
                    d_mine = d_mine + wide(far_swap(sums[f], f))
                d_mine = lax.optimization_barrier(d_mine)
            sums[g] = (d_mine + wide(other_core(d_other))).astype(jnp.bfloat16)
        if a == 0:
            stay, pass_on, *earlier = earlier
        returned += earlier
    d_sum = sums[0]
    if not relative:
        d_sum = d_sum.reshape(chips, own, half)[chip ^ jnp.arange(chips)]
        total = wide(d_sum[:4])
        for f in range(1, far):
            total = total + wide(far_swap(d_sum[4 * f : 4 * f + 4], f))
        d_sum = total.astype(jnp.bfloat16)
    pieces = [near_swap(d_sum[s], s) for s in range(4)]
    returned = lax.optimization_barrier(tuple(returned))
    returned = [near_swap(returned[s - 1], s) for s in SENT]
    returned = lax.optimization_barrier((*returned, *pieces))[:3]
    swapped = other_core(jnp.stack([pass_on] + [pack[1] for pack in returned]))
    packs = jnp.stack([stay] + [pack[0] for pack in returned])
    return (*post(gate_logits, grad_out, packs, swapped), bias_out(pieces))


def solution(mesh):
    groups, rows, cores = mesh.devices.shape
    devices = mesh.devices.reshape(groups, rows // PAIR**2, PAIR, PAIR, cores)
    mesh = jax.sharding.Mesh(devices, ("grp", "far", "near", "side", "key"))
    split = ("grp", "far", "near", "side")
    tokens = P(split, "key", None)
    pair = P(None, split, "key")
    in_specs = (tokens, tokens, tokens, tokens, pair, P(("grp", "key")), tokens)
    out_specs = (tokens, tokens, tokens, tokens, pair)
    return jax.shard_map(shards, mesh=mesh, in_specs=in_specs, out_specs=out_specs, check_vma=False)
```

```python
import functools
import math

import jax
import jax.numpy as jnp
from jax import lax
from jax.experimental import pallas as pl
from jax.experimental.pallas import tpu as pltpu
from jax.sharding import PartitionSpec as P

PAIR = 2
NEAR_PARTS = 2
SENT = (2, 3, 1)
ROWS_AT_ONCE = 16
VMEM = pltpu.VMEM
PARAMS = pltpu.CompilerParams(vmem_limit_bytes=32 * 1024 * 1024)
PRE_PARAMS = pltpu.CompilerParams(vmem_limit_bytes=60 * 1024 * 1024)


def places():
    near = lax.axis_index("near") * PAIR + lax.axis_index("side")
    return lax.axis_index("far") * PAIR * PAIR + near, near, lax.axis_index("key")


def fetch(pairs, sems):
    copies = [pltpu.make_async_copy(ref, buffer, sems.at[i]) for i, (ref, buffer) in enumerate(pairs)]
    for copy in copies:
        copy.start()
    for copy in copies:
        copy.wait()


def slab_kernel(bias, *slabs):
    near = places()[1]
    for s in range(4):
        slabs[s][...] = bias[near ^ s]


def make_slabs(bias):
    return pl.pallas_call(
        slab_kernel,
        out_shape=[jax.ShapeDtypeStruct(bias.shape[1:], jnp.bfloat16)] * 4,
        compiler_params=PARAMS,
        name="bias_by_head",
    )(bias)


def pack_kernel(*refs):
    inputs, packs, kept, buffers, (sems, held) = refs[:5], refs[5:8], refs[8:10], refs[10:15], refs[15:]
    fetch(list(zip(inputs, buffers)), sems)
    query, keys, values, gate, cot = buffers
    rows = query.shape[0]
    size = query.shape[2] // 4
    _, near, core = places()
    for r in range(rows):
        upstream = (cot[r].astype(jnp.float32) * jax.nn.sigmoid(gate[r].astype(jnp.float32))).astype(jnp.bfloat16)
        whole = [query[r], keys[r], values[r], upstream]
        for head in range(4):
            held[head, r] = jnp.concatenate([one[:, head * size : (head + 1) * size] for one in whole], axis=1)
    for i in range(2):
        for s in range(1, 4):
            packs[s - 1][i] = held[near ^ s, core ^ i]
        kept[i][...] = held[near, core ^ i]


def make_packs(*inputs):
    one = inputs[0]
    return pl.pallas_call(
        pack_kernel,
        in_specs=[pl.BlockSpec(memory_space=pl.ANY)] * 5,
        out_shape=[jax.ShapeDtypeStruct(one.shape, jnp.bfloat16)] * 3
        + [jax.ShapeDtypeStruct(one.shape[1:], jnp.bfloat16)] * 2,
        scratch_shapes=[VMEM(one.shape, jnp.bfloat16)] * 5
        + [pltpu.SemaphoreType.DMA((5,)), VMEM((4,) + one.shape, jnp.bfloat16)],
        compiler_params=PRE_PARAMS,
        name="pack",
    )(*inputs)


NT = (((1,), (1,)), ((), ()))


def dot(a, b, dims=(((1,), (0,)), ((), ()))):
    return lax.dot_general(a, b, dims, preferred_element_type=jnp.float32)


def main_kernel(scaling, size, blocks, start, relative, begun, ended, opened, closed, split, *refs):
    packs, swapped, (mine, other), refs = refs[:2], refs[2:4], refs[4:6], refs[6:]
    earlier, refs = refs[: 4 if begun else 0], refs[4 if begun else 0 :]
    before, refs = refs[: 1 if opened else 0], refs[1 if opened else 0 :]
    d_bias, refs = refs[: 2 if closed else 1], refs[2 if closed else 1 :]
    results, refs = refs[: 2 + split if ended else 4], refs[2 + split if ended else 4 :]
    q_all, d_all, k_of, v_of, dk_t, dv_t, att_all, dq_all, bias_wide, q_now, d_now, s_now, p_now, low_now, d_low_now, bias_sum = refs
    steps = q_all.shape[0] // (blocks * mine.shape[1]) if not relative else 1
    step = pl.program_id(0) if steps > 1 else 0
    chip, _, core = places()
    parts, (half, _) = len(packs), packs[0].shape
    own = mine.shape[1]
    lanes = parts * size

    def side(i):
        return pl.ds(pl.multiple_of((core ^ i) * half, half), half)

    def first():
        lane = lax.broadcasted_iota(jnp.int32, (half, lanes), 1) // size
        for i in range(2):
            here = [(swapped if i else packs)[p][...] for p in range(parts)]
            q, k, v, d = [
                jnp.concatenate([one[:, j * size : (j + 1) * size] for one in here], axis=1) for j in range(4)
            ]
            q_all[side(i)], d_all[side(i)] = q, d
            rows = slice(i * half, (i + 1) * half)
            for r in range(parts):
                k_of[r, rows] = jnp.where(lane == r, k, 0)
                v_of[r, rows] = jnp.where(lane == r, v, 0)
        for i, ref in enumerate((att_all, dq_all, dk_t, dv_t)):
            ref[...] = earlier[i][...] if begun else jnp.zeros_like(ref)

    first() if steps == 1 else pl.when(step == 0)(first)

    def strip(i):
        at = start + step * blocks + i
        at = chip ^ at if relative else at
        return pl.ds(pl.multiple_of(at * own, own), own)

    for i in range(blocks):
        rows = slice(i * own, (i + 1) * own)
        bias_wide[rows, :half] = mine[i].astype(jnp.float32)
        bias_wide[rows, half:] = other[i].astype(jnp.float32)
        q_now[rows], d_now[rows] = q_all[strip(i)], d_all[strip(i)]
    q, d = q_now[...], d_now[...]
    q_t = q.astype(jnp.float32).T.astype(jnp.bfloat16)
    d_t = d.astype(jnp.float32).T.astype(jnp.bfloat16)

    def scores(r):
        s_now[r % 2] = dot(q, k_of[r], NT)
        p_now[r % 2] = dot(d, v_of[r], NT)

    att_sum, dq_sum = None, None
    scores(0)
    for r in range(parts):
        if r + 1 < parts:
            scores(r + 1)
        for at in range(0, blocks * own, ROWS_AT_ONCE):
            rows = slice(at, at + ROWS_AT_ONCE)
            logits = s_now[r % 2, rows] * scaling + bias_wide[rows]
            expo = jnp.exp(logits - jnp.max(logits, axis=-1, keepdims=True))
            probs = expo * (1.0 / jnp.sum(expo, axis=-1, keepdims=True))
            d_probs = p_now[r % 2, rows]
            inner = jnp.sum(probs * d_probs, axis=-1, keepdims=True)
            d_logits = probs * (d_probs - inner)
            low_now[r % 2, rows] = probs.astype(jnp.bfloat16)
            d_low_now[r % 2, rows] = d_logits.astype(jnp.bfloat16)
            if r:
                d_logits = bias_sum[rows] + d_logits
            elif opened:
                d_logits = before[0][rows] + d_logits
            bias_sum[rows] = d_logits
        low, d_low = low_now[r % 2], d_low_now[r % 2]
        att, dq = dot(low, v_of[r]), dot(d_low, k_of[r])
        cut = slice(r * size, (r + 1) * size)
        dk_t[cut] += dot(q_t[cut], d_low)
        dv_t[cut] += dot(d_t[cut], low)
        att_sum = att if r == 0 else att_sum + att
        dq_sum = dq if r == 0 else dq_sum + dq
    att_low, dq_low = att_sum.astype(jnp.bfloat16), (dq_sum * scaling).astype(jnp.bfloat16)
    for i in range(blocks):
        rows = slice(i * own, (i + 1) * own)
        att_all[strip(i)], dq_all[strip(i)] = att_low[rows], dq_low[rows]
        if closed:
            d_bias[0][i] = bias_sum[rows, :half].astype(jnp.bfloat16)
            d_bias[1][i] = bias_sum[rows, half:].astype(jnp.bfloat16)
    if not closed:
        d_bias[0][...] = bias_sum[...]

    def last():
        if not ended:
            for ref, value in zip(results, (att_all, dq_all, dk_t, dv_t)):
                ref[...] = value[...]
            return
        dk = (dk_t[...] * scaling).T.astype(jnp.bfloat16)
        dv = dv_t[...].T.astype(jnp.bfloat16)
        for i in range(2):
            rows = slice(i * half, (i + 1) * half)
            whole = [att_all[side(i)], dq_all[side(i)], dk[rows], dv[rows]]
            for p in range(parts):
                pack = jnp.concatenate([one[:, p * size : (p + 1) * size] for one in whole], axis=1)
                if split and p == 0:
                    results[i][...] = pack
                else:
                    results[p + split][i] = pack

    last() if steps == 1 else pl.when(step == steps - 1)(last)


def fixed(value):
    return pl.BlockSpec(value.shape, lambda i: (0,) * len(value.shape))


def main(packs, swapped, mine, other, earlier, before, scaling, size, start, relative, ended, closed, split):
    parts, (half, width) = len(packs), swapped[0].shape
    strips, own, _ = mine.shape
    blocks, lanes = 4, parts * size
    key_count = queries = 2 * half
    rows = jax.ShapeDtypeStruct((queries, lanes), jnp.bfloat16)
    turned = jax.ShapeDtypeStruct((lanes, key_count), jnp.float32)
    wide = jax.ShapeDtypeStruct((strips * own, key_count), jnp.float32)
    strip = pl.BlockSpec((blocks, own, half), lambda i: (i, 0, 0))
    wide_strip = pl.BlockSpec((blocks * own, key_count), lambda i: (i, 0))
    now = VMEM((blocks * own, lanes), jnp.bfloat16)
    results = [rows, rows, turned, turned]
    if ended:
        ours = [jax.ShapeDtypeStruct((half, width), jnp.bfloat16)] * 2
        results = [jax.ShapeDtypeStruct((2, half, width), jnp.bfloat16)] * (parts - split)
        results = ours * split + results
    d_bias = [mine, other] if closed else [wide]
    grid = {}
    if not relative:
        grid = dict(
            grid=(strips // blocks,),
            in_specs=[fixed(one) for one in [*packs, *swapped]]
            + [strip, strip]
            + [fixed(one) for one in earlier]
            + [wide_strip] * len(before),
            out_specs=([strip] * 2 if closed else [wide_strip]) + [fixed(one) for one in results],
        )
    return pl.pallas_call(
        functools.partial(
            main_kernel, scaling, size, blocks, start, relative, bool(earlier), ended, bool(before), closed, split
        ),
        **grid,
        out_shape=[jax.ShapeDtypeStruct(one.shape, one.dtype) for one in d_bias + results],
        scratch_shapes=[
            VMEM(rows.shape, jnp.bfloat16),
            VMEM(rows.shape, jnp.bfloat16),
            VMEM((parts, key_count, lanes), jnp.bfloat16),
            VMEM((parts, key_count, lanes), jnp.bfloat16),
            VMEM(turned.shape, jnp.float32),
            VMEM(turned.shape, jnp.float32),
            VMEM(rows.shape, jnp.bfloat16),
            VMEM(rows.shape, jnp.bfloat16),
            VMEM((blocks * own, key_count), jnp.float32),
            now,
            now,
            VMEM((2, blocks * own, key_count), jnp.float32),
            VMEM((2, blocks * own, key_count), jnp.float32),
            VMEM((2, blocks * own, key_count), jnp.bfloat16),
            VMEM((2, blocks * own, key_count), jnp.bfloat16),
            VMEM((blocks * own, key_count), jnp.float32),
        ],
        compiler_params=PARAMS,
        cost_estimate=pl.CostEstimate(flops=1, bytes_accessed=1, transcendentals=0),
        name="attention",
    )(*packs, *swapped, mine, other, *earlier, *before)


def post_kernel(gate, cot, packs, swapped, d_query, d_keys, d_values, d_gate, held):
    rows, half, channels = gate.shape
    size = channels // 4
    _, near, core = places()
    for i, s in enumerate((0, *SENT)):
        held[near ^ s, core] = packs[i]
        held[near ^ s, 1 - core] = swapped[i]
    for r in range(rows):
        full = []
        for j in range(4):
            full.append(jnp.concatenate([held[h, r, :, j * size : (j + 1) * size] for h in range(4)], axis=1))
        d_query[r], d_keys[r], d_values[r] = full[1], full[2], full[3]
        sig = jax.nn.sigmoid(gate[r].astype(jnp.float32))
        d_gate[r] = (cot[r].astype(jnp.float32) * full[0].astype(jnp.float32) * sig * (1.0 - sig)).astype(jnp.bfloat16)


def post(gate, cot, packs, swapped):
    return pl.pallas_call(
        post_kernel,
        out_shape=[jax.ShapeDtypeStruct(gate.shape, jnp.bfloat16)] * 4,
        scratch_shapes=[VMEM((4,) + gate.shape, jnp.bfloat16)],
        compiler_params=PARAMS,
        name="unpack",
    )(gate, cot, packs, swapped)


def bias_kernel(*refs):
    near = places()[1]
    for s in range(4):
        refs[4][near ^ s] = refs[s][...].astype(jnp.float32)


def bias_out(pieces):
    return pl.pallas_call(
        bias_kernel,
        out_shape=jax.ShapeDtypeStruct((4,) + pieces[0].shape, jnp.float32),
        compiler_params=PARAMS,
        name="bias_grad",
    )(*pieces)


def shards(query, keys, values, gate_logits, pair_bias, key_mask, grad_out):
    rows, half, channels = query.shape
    heads, own, _ = pair_bias.shape
    size = channels // heads
    scaling = 1.0 / math.sqrt(size)
    far, cores = lax.axis_size("far"), lax.axis_size("key")
    chips = far * PAIR * PAIR
    assert PAIR * PAIR == heads == 4 and rows == cores == 2
    relative = own % 16 == 0
    chip = places()[0]

    def swap(value, axes, s, count):
        return lax.ppermute(value, axes, [(i, i ^ s) for i in range(count)]) if s else value

    def near_swap(value, s):
        return swap(value, ("near", "side"), s, 4)

    def far_swap(value, s):
        return swap(value, "far", s, far)

    def other_core(value):
        return swap(value, "key", 1, 2)

    def wide(value):
        return value.astype(jnp.float32)

    slabs = make_slabs(pair_bias)
    strips = jnp.stack([near_swap(slabs[s], s) for s in range(4)])
    strips = jnp.where(key_mask == 1, strips, jnp.bfloat16(-1000000000.0))
    groups = [far_swap(strips, f) for f in range(far)]
    *packs, kept, spare = make_packs(query, keys, values, gate_logits, grad_out)
    packs = [near_swap(packs[s], s + 1) for s in range(3)]
    starts = [f * 4 for f in range(far)]
    if not relative:
        starts, groups = [0], [jnp.concatenate(groups)[chip ^ jnp.arange(chips)].reshape(8, -1, half)]
    others = [jnp.concatenate([other_core(part) for part in jnp.split(groups[0], NEAR_PARTS)])] + [None] * (len(starts) - 1)
    orders = [list(range(len(starts))), list(range(len(starts)))[::-1]]
    before, sums, returned = [[]] * len(starts), [None] * len(starts), []
    for a, order in enumerate(orders):
        ours = [packs[0]] if a == 0 else packs[1:]
        if a:
            ours = list(lax.optimization_barrier((*ours, before[0][0]))[:2])
        swapped = [other_core(pack[1]) for pack in ours]
        ours = [pack[0] for pack in ours]
        if a == 0:
            spare = lax.optimization_barrier((spare, ours[0]))[0]
            ours, swapped = [kept] + ours, [other_core(spare)] + swapped
        earlier = []
        for g in order:
            if others[g] is None:
                groups[g] = lax.optimization_barrier((groups[g], before[0][0]))[0]
                others[g] = other_core(groups[g])
            mine, closed, ended = groups[g], a == len(orders) - 1, g == order[-1]
            if closed and g != order[0]:
                mine, last, back = lax.optimization_barrier((mine, sums[order[order.index(g) - 1]], back))
                sums[order[order.index(g) - 1]] = last
            out = main(
                ours, swapped, mine, others[g], earlier, before[g], scaling, size, starts[g], relative, ended, closed, 1 - a
            )
            if not closed:
                before[g], earlier = out[:1], out[1:]
                continue
            d_mine, d_other, *earlier = out
            d_mine = wide(d_mine)
            if ended and relative:
                for f in range(1, far):
                    d_mine = d_mine + wide(far_swap(sums[f], f))
                d_mine = lax.optimization_barrier(d_mine)
            sums[g] = (d_mine + wide(other_core(d_other))).astype(jnp.bfloat16)
        if a == 0:
            stay, pass_on, *earlier = earlier
            back = other_core(pass_on)
        returned += earlier
    d_sum = sums[0]
    if not relative:
        d_sum = d_sum.reshape(chips, own, half)[chip ^ jnp.arange(chips)]
        total = wide(d_sum[:4])
        for f in range(1, far):
            total = total + wide(far_swap(d_sum[4 * f : 4 * f + 4], f))
        d_sum = total.astype(jnp.bfloat16)
    pieces = [near_swap(d_sum[s], s) for s in range(4)]
    returned = lax.optimization_barrier(tuple(returned))
    returned = [near_swap(returned[s - 1], s) for s in SENT]
    returned = lax.optimization_barrier((*returned, *pieces))[:3]
    late = other_core(jnp.stack([pack[1] for pack in returned]))
    swapped = jnp.concatenate([back[None], late])
    packs = jnp.stack([stay] + [pack[0] for pack in returned])
    return (*post(gate_logits, grad_out, packs, swapped), bias_out(pieces))


def solution(mesh):
    groups, rows, cores = mesh.devices.shape
    devices = mesh.devices.reshape(groups, rows // PAIR**2, PAIR, PAIR, cores)
    mesh = jax.sharding.Mesh(devices, ("grp", "far", "near", "side", "key"))
    split = ("grp", "far", "near", "side")
    tokens = P(split, "key", None)
    pair = P(None, split, "key")
    in_specs = (tokens, tokens, tokens, tokens, pair, P(("grp", "key")), tokens)
    out_specs = (tokens, tokens, tokens, tokens, pair)
    return jax.shard_map(shards, mesh=mesh, in_specs=in_specs, out_specs=out_specs, check_vma=False)
```

```python
import functools
import math

import jax
import jax.numpy as jnp
from jax import lax
from jax.experimental import pallas as pl
from jax.experimental.pallas import tpu as pltpu
from jax.sharding import PartitionSpec as P

PAIR = 2
NEAR_PARTS = 2
SENT = (2, 3, 1)
ROWS_AT_ONCE = 16
VMEM = pltpu.VMEM
PARAMS = pltpu.CompilerParams(vmem_limit_bytes=32 * 1024 * 1024)
PRE_PARAMS = pltpu.CompilerParams(vmem_limit_bytes=60 * 1024 * 1024)


def places():
    near = lax.axis_index("near") * PAIR + lax.axis_index("side")
    return lax.axis_index("far") * PAIR * PAIR + near, near, lax.axis_index("key")


def fetch(pairs, sems):
    copies = [pltpu.make_async_copy(ref, buffer, sems.at[i]) for i, (ref, buffer) in enumerate(pairs)]
    for copy in copies:
        copy.start()
    for copy in copies:
        copy.wait()


def slab_kernel(bias, *slabs):
    near = places()[1]
    for s in range(4):
        slabs[s][...] = bias[near ^ s]


def make_slabs(bias):
    return pl.pallas_call(
        slab_kernel,
        out_shape=[jax.ShapeDtypeStruct(bias.shape[1:], jnp.bfloat16)] * 4,
        compiler_params=PARAMS,
        name="bias_by_head",
    )(bias)


def pack_kernel(*refs):
    inputs, packs, kept, buffers, (sems, held) = refs[:5], refs[5:8], refs[8:10], refs[10:15], refs[15:]
    fetch(list(zip(inputs, buffers)), sems)
    query, keys, values, gate, cot = buffers
    rows = query.shape[0]
    size = query.shape[2] // 4
    _, near, core = places()
    for r in range(rows):
        upstream = (cot[r].astype(jnp.float32) * jax.nn.sigmoid(gate[r].astype(jnp.float32))).astype(jnp.bfloat16)
        whole = [query[r], keys[r], values[r], upstream]
        for head in range(4):
            held[head, r] = jnp.concatenate([one[:, head * size : (head + 1) * size] for one in whole], axis=1)
    for i in range(2):
        for s in range(1, 4):
            packs[s - 1][i] = held[near ^ s, core ^ i]
        kept[i][...] = held[near, core ^ i]


def make_packs(*inputs):
    one = inputs[0]
    return pl.pallas_call(
        pack_kernel,
        in_specs=[pl.BlockSpec(memory_space=pl.ANY)] * 5,
        out_shape=[jax.ShapeDtypeStruct(one.shape, jnp.bfloat16)] * 3
        + [jax.ShapeDtypeStruct(one.shape[1:], jnp.bfloat16)] * 2,
        scratch_shapes=[VMEM(one.shape, jnp.bfloat16)] * 5
        + [pltpu.SemaphoreType.DMA((5,)), VMEM((4,) + one.shape, jnp.bfloat16)],
        compiler_params=PRE_PARAMS,
        name="pack",
    )(*inputs)


NT = (((1,), (1,)), ((), ()))


def dot(a, b, dims=(((1,), (0,)), ((), ()))):
    return lax.dot_general(a, b, dims, preferred_element_type=jnp.float32)


def main_kernel(scaling, size, blocks, start, relative, begun, ended, opened, closed, split, *refs):
    packs, swapped, (mine, other), refs = refs[:2], refs[2:4], refs[4:6], refs[6:]
    earlier, refs = refs[: 4 if begun else 0], refs[4 if begun else 0 :]
    before, refs = refs[: 1 if opened else 0], refs[1 if opened else 0 :]
    d_bias, refs = refs[: 2 if closed else 1], refs[2 if closed else 1 :]
    results, refs = refs[: 2 + split if ended else 4], refs[2 + split if ended else 4 :]
    q_all, d_all, k_of, v_of, dk_t, dv_t, att_all, dq_all, bias_wide, q_now, d_now, s_now, p_now, low_now, d_low_now, bias_sum = refs
    steps = q_all.shape[0] // (blocks * mine.shape[1]) if not relative else 1
    step = pl.program_id(0) if steps > 1 else 0
    chip, _, core = places()
    parts, (half, _) = len(packs), packs[0].shape
    own = mine.shape[1]
    lanes = parts * size

    def side(i):
        return pl.ds(pl.multiple_of((core ^ i) * half, half), half)

    def first():
        lane = lax.broadcasted_iota(jnp.int32, (half, lanes), 1) // size
        for i in range(2):
            here = [(swapped if i else packs)[p][...] for p in range(parts)]
            q, k, v, d = [
                jnp.concatenate([one[:, j * size : (j + 1) * size] for one in here], axis=1) for j in range(4)
            ]
            q_all[side(i)], d_all[side(i)] = q, d
            rows = slice(i * half, (i + 1) * half)
            for r in range(parts):
                k_of[r, rows] = jnp.where(lane == r, k, 0)
                v_of[r, rows] = jnp.where(lane == r, v, 0)
        for i, ref in enumerate((att_all, dq_all, dk_t, dv_t)):
            ref[...] = earlier[i][...] if begun else jnp.zeros_like(ref)

    first() if steps == 1 else pl.when(step == 0)(first)

    def strip(i):
        at = start + step * blocks + i
        at = chip ^ at if relative else at
        return pl.ds(pl.multiple_of(at * own, own), own)

    for i in range(blocks):
        rows = slice(i * own, (i + 1) * own)
        bias_wide[rows, :half] = mine[i].astype(jnp.float32)
        bias_wide[rows, half:] = other[i].astype(jnp.float32)
        q_now[rows], d_now[rows] = q_all[strip(i)], d_all[strip(i)]
    q, d = q_now[...], d_now[...]
    q_t = q.astype(jnp.float32).T.astype(jnp.bfloat16)
    d_t = d.astype(jnp.float32).T.astype(jnp.bfloat16)

    def scores(r):
        s_now[r % 2] = dot(q, k_of[r], NT)
        p_now[r % 2] = dot(d, v_of[r], NT)

    att_sum, dq_sum = None, None
    scores(0)
    for r in range(parts):
        if r + 1 < parts:
            scores(r + 1)
        for at in range(0, blocks * own, ROWS_AT_ONCE):
            rows = slice(at, at + ROWS_AT_ONCE)
            logits = s_now[r % 2, rows] * scaling + bias_wide[rows]
            expo = jnp.exp(logits - jnp.max(logits, axis=-1, keepdims=True))
            probs = expo * (1.0 / jnp.sum(expo, axis=-1, keepdims=True))
            d_probs = p_now[r % 2, rows]
            inner = jnp.sum(probs * d_probs, axis=-1, keepdims=True)
            d_logits = probs * (d_probs - inner)
            low_now[r % 2, rows] = probs.astype(jnp.bfloat16)
            d_low_now[r % 2, rows] = d_logits.astype(jnp.bfloat16)
            if r:
                d_logits = bias_sum[rows] + d_logits
            elif opened:
                d_logits = before[0][rows] + d_logits
            bias_sum[rows] = d_logits
        low, d_low = low_now[r % 2], d_low_now[r % 2]
        att, dq = dot(low, v_of[r]), dot(d_low, k_of[r])
        cut = slice(r * size, (r + 1) * size)
        dk_t[cut] += dot(q_t[cut], d_low)
        dv_t[cut] += dot(d_t[cut], low)
        att_sum = att if r == 0 else att_sum + att
        dq_sum = dq if r == 0 else dq_sum + dq
    att_low, dq_low = att_sum.astype(jnp.bfloat16), (dq_sum * scaling).astype(jnp.bfloat16)
    for i in range(blocks):
        rows = slice(i * own, (i + 1) * own)
        att_all[strip(i)], dq_all[strip(i)] = att_low[rows], dq_low[rows]
        if closed:
            d_bias[0][i] = bias_sum[rows, :half].astype(jnp.bfloat16)
            d_bias[1][i] = bias_sum[rows, half:].astype(jnp.bfloat16)
    if not closed:
        d_bias[0][...] = bias_sum[...]

    def last():
        if not ended:
            for ref, value in zip(results, (att_all, dq_all, dk_t, dv_t)):
                ref[...] = value[...]
            return
        dk = (dk_t[...] * scaling).T.astype(jnp.bfloat16)
        dv = dv_t[...].T.astype(jnp.bfloat16)
        for i in range(2):
            rows = slice(i * half, (i + 1) * half)
            whole = [att_all[side(i)], dq_all[side(i)], dk[rows], dv[rows]]
            for p in range(parts):
                pack = jnp.concatenate([one[:, p * size : (p + 1) * size] for one in whole], axis=1)
                if split and p == 0:
                    results[i][...] = pack
                else:
                    results[p + split][i] = pack

    last() if steps == 1 else pl.when(step == steps - 1)(last)


def fixed(value):
    return pl.BlockSpec(value.shape, lambda i: (0,) * len(value.shape))


def main(packs, swapped, mine, other, earlier, before, scaling, size, start, relative, ended, closed, split):
    parts, (half, width) = len(packs), swapped[0].shape
    strips, own, _ = mine.shape
    blocks, lanes = 4, parts * size
    key_count = queries = 2 * half
    rows = jax.ShapeDtypeStruct((queries, lanes), jnp.bfloat16)
    turned = jax.ShapeDtypeStruct((lanes, key_count), jnp.float32)
    wide = jax.ShapeDtypeStruct((strips * own, key_count), jnp.float32)
    strip = pl.BlockSpec((blocks, own, half), lambda i: (i, 0, 0))
    wide_strip = pl.BlockSpec((blocks * own, key_count), lambda i: (i, 0))
    now = VMEM((blocks * own, lanes), jnp.bfloat16)
    results = [rows, rows, turned, turned]
    if ended:
        ours = [jax.ShapeDtypeStruct((half, width), jnp.bfloat16)] * 2
        results = [jax.ShapeDtypeStruct((2, half, width), jnp.bfloat16)] * (parts - split)
        results = ours * split + results
    d_bias = [mine, other] if closed else [wide]
    grid = {}
    if not relative:
        grid = dict(
            grid=(strips // blocks,),
            in_specs=[fixed(one) for one in [*packs, *swapped]]
            + [strip, strip]
            + [fixed(one) for one in earlier]
            + [wide_strip] * len(before),
            out_specs=([strip] * 2 if closed else [wide_strip]) + [fixed(one) for one in results],
        )
    return pl.pallas_call(
        functools.partial(
            main_kernel, scaling, size, blocks, start, relative, bool(earlier), ended, bool(before), closed, split
        ),
        **grid,
        out_shape=[jax.ShapeDtypeStruct(one.shape, one.dtype) for one in d_bias + results],
        scratch_shapes=[
            VMEM(rows.shape, jnp.bfloat16),
            VMEM(rows.shape, jnp.bfloat16),
            VMEM((parts, key_count, lanes), jnp.bfloat16),
            VMEM((parts, key_count, lanes), jnp.bfloat16),
            VMEM(turned.shape, jnp.float32),
            VMEM(turned.shape, jnp.float32),
            VMEM(rows.shape, jnp.bfloat16),
            VMEM(rows.shape, jnp.bfloat16),
            VMEM((blocks * own, key_count), jnp.float32),
            now,
            now,
            VMEM((2, blocks * own, key_count), jnp.float32),
            VMEM((2, blocks * own, key_count), jnp.float32),
            VMEM((2, blocks * own, key_count), jnp.bfloat16),
            VMEM((2, blocks * own, key_count), jnp.bfloat16),
            VMEM((blocks * own, key_count), jnp.float32),
        ],
        compiler_params=PARAMS,
        cost_estimate=pl.CostEstimate(flops=1, bytes_accessed=1, transcendentals=0),
        name="attention",
    )(*packs, *swapped, mine, other, *earlier, *before)


def post_kernel(gate, cot, packs, swapped, d_query, d_keys, d_values, d_gate, held):
    rows, half, channels = gate.shape
    size = channels // 4
    _, near, core = places()
    for i, s in enumerate((0, *SENT)):
        held[near ^ s, core] = packs[i]
        held[near ^ s, 1 - core] = swapped[i]
    for r in range(rows):
        full = []
        for j in range(4):
            full.append(jnp.concatenate([held[h, r, :, j * size : (j + 1) * size] for h in range(4)], axis=1))
        d_query[r], d_keys[r], d_values[r] = full[1], full[2], full[3]
        sig = jax.nn.sigmoid(gate[r].astype(jnp.float32))
        d_gate[r] = (cot[r].astype(jnp.float32) * full[0].astype(jnp.float32) * sig * (1.0 - sig)).astype(jnp.bfloat16)


def post(gate, cot, packs, swapped):
    return pl.pallas_call(
        post_kernel,
        out_shape=[jax.ShapeDtypeStruct(gate.shape, jnp.bfloat16)] * 4,
        scratch_shapes=[VMEM((4,) + gate.shape, jnp.bfloat16)],
        compiler_params=PARAMS,
        name="unpack",
    )(gate, cot, packs, swapped)


def bias_kernel(*refs):
    near = places()[1]
    for s in range(4):
        refs[4][near ^ s] = refs[s][...].astype(jnp.float32)


def bias_out(pieces):
    return pl.pallas_call(
        bias_kernel,
        out_shape=jax.ShapeDtypeStruct((4,) + pieces[0].shape, jnp.float32),
        compiler_params=PARAMS,
        name="bias_grad",
    )(*pieces)


def shards(query, keys, values, gate_logits, pair_bias, key_mask, grad_out):
    rows, half, channels = query.shape
    heads, own, _ = pair_bias.shape
    size = channels // heads
    scaling = 1.0 / math.sqrt(size)
    far, cores = lax.axis_size("far"), lax.axis_size("key")
    chips = far * PAIR * PAIR
    assert PAIR * PAIR == heads == 4 and rows == cores == 2
    relative = own % 16 == 0
    chip = places()[0]

    def swap(value, axes, s, count):
        return lax.ppermute(value, axes, [(i, i ^ s) for i in range(count)]) if s else value

    def near_swap(value, s):
        return swap(value, ("near", "side"), s, 4)

    def far_swap(value, s):
        return swap(value, "far", s, far)

    def other_core(value):
        return swap(value, "key", 1, 2)

    def wide(value):
        return value.astype(jnp.float32)

    slabs = make_slabs(pair_bias)
    strips = jnp.stack([near_swap(slabs[s], s) for s in range(4)])
    strips = jnp.where(key_mask == 1, strips, jnp.bfloat16(-1000000000.0))
    groups = [far_swap(strips, f) for f in range(far)]
    *packs, kept, spare = make_packs(query, keys, values, gate_logits, grad_out)
    packs = [near_swap(packs[s], s + 1) for s in range(3)]
    starts = [f * 4 for f in range(far)]
    if not relative:
        starts, groups = [0], [jnp.concatenate(groups)[chip ^ jnp.arange(chips)].reshape(8, -1, half)]
    others = [jnp.concatenate([other_core(part) for part in jnp.split(groups[0], NEAR_PARTS)])] + [None] * (len(starts) - 1)
    orders = [list(range(len(starts))), list(range(len(starts)))[::-1]]
    before, sums, returned = [[]] * len(starts), [None] * len(starts), []
    for a, order in enumerate(orders):
        ours = [packs[0]] if a == 0 else packs[1:]
        if a:
            ours = list(lax.optimization_barrier((*ours, before[0][0]))[:2])
        swapped = [other_core(pack[1]) for pack in ours]
        ours = [pack[0] for pack in ours]
        if a == 0:
            spare = lax.optimization_barrier((spare, ours[0]))[0]
            ours, swapped = [kept] + ours, [other_core(spare)] + swapped
        earlier = []
        for g in order:
            if others[g] is None:
                groups[g] = lax.optimization_barrier((groups[g], before[0][0]))[0]
                others[g] = other_core(groups[g])
            mine, closed, ended = groups[g], a == len(orders) - 1, g == order[-1]
            if closed and g != order[0]:
                mine, last, back = lax.optimization_barrier((mine, sums[order[order.index(g) - 1]], back))
                sums[order[order.index(g) - 1]] = last
            out = main(
                ours, swapped, mine, others[g], earlier, before[g], scaling, size, starts[g], relative, ended, closed, 1 - a
            )
            if not closed:
                before[g], earlier = out[:1], out[1:]
                continue
            d_mine, d_other, *earlier = out
            d_mine = wide(d_mine)
            if ended and relative:
                for f in range(1, far):
                    d_mine = d_mine + wide(far_swap(sums[f], f))
                d_mine = lax.optimization_barrier(d_mine)
            sums[g] = (d_mine + wide(other_core(d_other))).astype(jnp.bfloat16)
        if a == 0:
            stay, pass_on, *earlier = earlier
            back = other_core(pass_on)
        returned += earlier
    d_sum = sums[0]
    if not relative:
        d_sum = d_sum.reshape(chips, own, half)[chip ^ jnp.arange(chips)]
        total = wide(d_sum[:4])
        for f in range(1, far):
            total = total + wide(far_swap(d_sum[4 * f : 4 * f + 4], f))
        d_sum = total.astype(jnp.bfloat16)
    pieces = [near_swap(d_sum[s], s) for s in range(4)]
    returned = lax.optimization_barrier(tuple(returned))
    returned = [near_swap(returned[s - 1], s) for s in SENT]
    returned = lax.optimization_barrier((*returned, *pieces))[:3]
    late = [other_core(pack[1]) for pack in returned]
    swapped = jnp.stack([back] + late)
    packs = jnp.stack([stay] + [pack[0] for pack in returned])
    return (*post(gate_logits, grad_out, packs, swapped), bias_out(pieces))


def solution(mesh):
    groups, rows, cores = mesh.devices.shape
    devices = mesh.devices.reshape(groups, rows // PAIR**2, PAIR, PAIR, cores)
    mesh = jax.sharding.Mesh(devices, ("grp", "far", "near", "side", "key"))
    split = ("grp", "far", "near", "side")
    tokens = P(split, "key", None)
    pair = P(None, split, "key")
    in_specs = (tokens, tokens, tokens, tokens, pair, P(("grp", "key")), tokens)
    out_specs = (tokens, tokens, tokens, tokens, pair)
    return jax.shard_map(shards, mesh=mesh, in_specs=in_specs, out_specs=out_specs, check_vma=False)
```
